32 devices in a mesh: lat: 8 (over y, x, core), lon: 4 (over z).
Axes of the slice: x: 2, y: 2, z: 4, core: 2. Of those that a mesh axis runs over, the one named last changes fastest.
Arguments:
- fields_in: bfloat16 [4, 128, 256, 641], P(None, 'lat', 'lon'), may hold values from -6 to 6
- cotangent: bfloat16 [4, 128, 256, 641], P(None, 'lat', 'lon'), may hold values from -6 to 6
- member_dates: int32 [4], replicated, may hold values from 0 to 15
- date_table: float32 [16, 641], replicated, may hold values from -3 to 3
- norm_gains: float32 [2, 641], replicated, may hold values from 0.25 to 1.75
- spectral_filter: float32 [128, 641], replicated, may hold values from 0.5 to 2
- weight_in: float32 [641, 1282], replicated, may hold values from -0.25 to 0.25
- weight_out: float32 [1282, 641], replicated, may hold values from -0.15625 to 0.15625
- gain_moments: float32 [2, 641], replicated, may hold values from 13107.2 to 262144
- in_row_stats: float32 [641], replicated, may hold values from 9175.04 to 144179.2
- in_column_stats: float32 [1282], replicated, may hold values from 9175.04 to 144179.2
- out_row_stats: float32 [1282], replicated, may hold values from 19660.8 to 314572.8
- out_column_stats: float32 [641], replicated, may hold values from 19660.8 to 314572.8
- filter_row_stats: float32 [128], replicated, may hold values from 131.072 to 6553.6
- filter_column_stats: float32 [641], replicated, may hold values from 131.072 to 6553.6
Outputs:
- block_output: bfloat16 [4, 128, 256, 641], P(None, 'lat', 'lon')
- input_grad: float32 [4, 128, 256, 641], P(None, 'lat', 'lon')
- grad_weight_in: float32 [641, 1282], replicated
- grad_weight_out: float32 [1282, 641], replicated
- grad_filter: float32 [128, 641], replicated
- grad_gains: float32 [2, 641], replicated
- new_weight_in: float32 [641, 1282], replicated
- new_weight_out: float32 [1282, 641], replicated
- new_filter: float32 [128, 641], replicated
- new_gains: float32 [2, 641], replicated
- new_in_row_stats: float32 [641], replicated
- new_in_column_stats: float32 [1282], replicated
- new_out_row_stats: float32 [1282], replicated
- new_out_column_stats: float32 [641], replicated
- new_filter_row_stats: float32 [128], replicated
- new_filter_column_stats: float32 [641], replicated
- new_gain_moments: float32 [2, 641], replicated
The draws below stay inside these ranges and needn't reach their ends.
Inputs may be any that keep to these rules, and one draw needn't show every extreme that they name: `member_dates`: the date index of each member.
All inputs are finite; a program needn't handle non-finite values.
Results may differ from the reference program's by a relative error of at most 0.014.
Values may be sent and summed in bfloat16 or wider, within the bound.
No kernel may reach another device: no remote copies, remote signals or barrier semaphores. Data moves between devices by JAX's collectives and lax.ppermute only.
A program may use at most 384 MiB of HBM per device.

```python
import math
import jax
import jax.numpy as jnp
from jax import lax

C = 641
H = 1282
NLAT = 128
NLON = 256
L = 128
M = 96
MEMBERS = 4
NDATES = 16
STEP = 3


def place_ends(array, own_key, least, high):
    spot = [jax.random.randint(jax.random.fold_in(own_key, axis), (), 0, length) for axis, length in enumerate(array.shape)]
    longest = array.shape.index(max(array.shape))
    beside = spot[:longest] + [(spot[longest] + 1) % array.shape[longest]] + spot[longest + 1:]
    return array.at[tuple(spot)].set(least).at[tuple(beside)].set(high)


def block_levels(own_key, extent, shards, least, largest):
    loudness, own = 1.0, jax.random.fold_in(own_key, 6)
    for dim, blocks in shards:
        draws = jnp.exp(jax.random.uniform(jax.random.fold_in(own, dim), (blocks,), jnp.float32, least / len(shards), largest / len(shards)))
        loudness = loudness * jnp.repeat(draws, extent[dim] // blocks).reshape([-1 if axis == dim else 1 for axis in range(len(extent))])
    return loudness


def normal_values(own_key, extent, scale, limit, shards=(), held_as=jnp.bfloat16):
    gain = block_levels(own_key, extent, shards, -0.22, 0.18) if shards else 1.0
    values = jax.random.normal(own_key, extent, jnp.float32) * scale * gain
    return jnp.minimum(jnp.maximum(values, -limit), limit).astype(held_as)


def setup_inputs(seed: int = 0) -> dict:
    streams_of = jax.random.split(jax.random.key(seed), 16)
    return {
        "fields_in": normal_values(streams_of[0], (MEMBERS, NLAT, NLON, C), 1.0, 6.0, ((1, 8), (2, 4))),
        "cotangent": normal_values(streams_of[1], (MEMBERS, NLAT, NLON, C), 1.0, 6.0, ((1, 8), (2, 4))),
        "member_dates": place_ends(jax.random.randint(streams_of[2], (MEMBERS,), 0, NDATES), jax.random.fold_in(streams_of[2], 1), 0, NDATES - 1).astype(jnp.int32),
        "date_table": normal_values(streams_of[3], (NDATES, C), 0.5, 3.0, (), jnp.float32),
        "norm_gains": jnp.clip(1.0 + 0.15 * jax.random.normal(streams_of[4], (2, C), jnp.float32), 0.25, 1.75),
        "spectral_filter": jnp.clip(jax.random.uniform(streams_of[5], (L, C), jnp.float32, 0.5, 2.0), 0.5, 2.0),
        "weight_in": normal_values(streams_of[6], (C, H), C ** -0.5, 0.25, (), jnp.float32),
        "weight_out": normal_values(streams_of[7], (H, C), H ** -0.5, 0.15625, (), jnp.float32),
        "gain_moments": jnp.clip(jnp.exp(jax.random.uniform(streams_of[8], (2, C), jnp.float32, math.log(13107.2), math.log(262144.0))), 13107.2, 262144.0),
        "in_row_stats": jnp.clip(jnp.exp(jax.random.uniform(streams_of[9], (C,), jnp.float32, math.log(9175.04), math.log(144179.2))), 9175.04, 144179.2),
        "in_column_stats": jnp.clip(jnp.exp(jax.random.uniform(streams_of[10], (H,), jnp.float32, math.log(9175.04), math.log(144179.2))), 9175.04, 144179.2),
        "out_row_stats": jnp.clip(jnp.exp(jax.random.uniform(streams_of[11], (H,), jnp.float32, math.log(19660.8), math.log(314572.8))), 19660.8, 314572.8),
        "out_column_stats": jnp.clip(jnp.exp(jax.random.uniform(streams_of[12], (C,), jnp.float32, math.log(19660.8), math.log(314572.8))), 19660.8, 314572.8),
        "filter_row_stats": jnp.clip(jnp.exp(jax.random.uniform(streams_of[13], (L,), jnp.float32, math.log(131.072), math.log(6553.6))), 131.072, 6553.6),
        "filter_column_stats": jnp.clip(jnp.exp(jax.random.uniform(streams_of[14], (C,), jnp.float32, math.log(131.072), math.log(6553.6))), 131.072, 6553.6),
    }


HIGHEST = lax.Precision.HIGHEST
NORM_EPS = 1e-06
FIRST_EPS = 1e-30
SECOND_EPS = 0.001
CLIP_LEVEL = 0.5
STEP_RATE = 0.5

@jax.custom_vjp
def low(v):
    return lax.optimization_barrier(v.astype(jnp.bfloat16)).astype(jnp.float32)

@jax.custom_vjp
def low_back(v):
    return v

def low_keep(v):
    return (low(v), None)

def low_pass(kept, grad):
    return (grad,)

def back_keep(v):
    return (v, None)

def back_low(kept, grad):
    return (low(grad),)
low.defvjp(low_keep, low_pass)
low_back.defvjp(back_keep, back_low)

def legendre_table():
    angles = (jnp.arange(NLAT, dtype=jnp.float32) + 0.5) * (math.pi / NLAT)
    cosine = jnp.cos(angles)
    sine_lat = jnp.sin(angles)
    orders = jnp.arange(M, dtype=jnp.float32)[:, None]
    factors = jnp.arange(1, M, dtype=jnp.float32)
    growth = jnp.concatenate([jnp.zeros((1,), jnp.float32), jnp.cumsum(0.5 * jnp.log((2.0 * factors + 1.0) / (2.0 * factors)))])
    diagonal = jnp.exp(0.5 * math.log(0.5) + growth[:, None] + orders * jnp.log(sine_lat)[None, :])

    def advance(state_pair, degree):
        latest, earlier = state_pair
        degree_f = degree.astype(jnp.float32)
        previous = degree_f - 1.0
        first_coef = jnp.sqrt((4.0 * degree_f * degree_f - 1.0) / jnp.maximum(degree_f * degree_f - orders * orders, 1.0))
        second_coef = jnp.sqrt(jnp.maximum(previous * previous - orders * orders, 0.0) / jnp.maximum(4.0 * previous * previous - 1.0, 1.0))
        general = first_coef * (cosine[None, :] * latest - second_coef * earlier)
        values = jnp.where(degree_f < orders, 0.0, jnp.where(degree_f == orders, diagonal, general))
        return ((values, latest), values)
    zeroes = jnp.zeros((M, NLAT), jnp.float32)
    _, stacked = lax.scan(advance, (zeroes, zeroes), jnp.arange(L, dtype=jnp.int32))
    return (jnp.transpose(stacked, (1, 0, 2)), math.pi / NLAT * sine_lat)

def dft_tables():
    points = jnp.arange(NLON, dtype=jnp.int32)[:, None]
    orders = jnp.arange(M, dtype=jnp.int32)[None, :]
    phases = (points * orders % NLON).astype(jnp.float32) * (2.0 * math.pi / NLON)
    cosine = jnp.cos(phases)
    sine_part = jnp.sin(phases)
    forward = jnp.stack([cosine, -sine_part], axis=2).reshape(NLON, 2 * M) / NLON
    doubling = jnp.where(orders == 0, 1.0, 2.0).astype(jnp.float32)
    inverse = jnp.transpose(jnp.stack([doubling * cosine, -doubling * sine_part], axis=2).reshape(NLON, 2 * M))
    return (forward, inverse)

def rms_norm(values, scaling):
    return values * lax.rsqrt(lax.optimization_barrier(jnp.mean(values * values, axis=-1, keepdims=True)) + NORM_EPS) * scaling

def spectral(normed, response, tables):
    legendre, quadrature, forward, inverse = tables
    paired = jnp.repeat(legendre, 2, axis=0)
    spectra = low(low_back(jnp.einsum('bjkc,kq->bqjc', normed, forward, precision=HIGHEST)))
    coefficients = low_back(jnp.einsum('qlj,bqjc->blqc', paired * quadrature, spectra, precision=HIGHEST))
    filtered = low(response[None, :, None, :] * coefficients)
    synthesis = low(low_back(jnp.einsum('qlj,blqc->bqjc', paired, filtered, precision=HIGHEST)))
    return low(low_back(jnp.einsum('bqjc,qk->bjkc', synthesis, inverse, precision=HIGHEST)))

def adafactor_matrix(weight_now, gradient, rows_old, columns_old, decay_rate):
    squares = gradient * gradient + FIRST_EPS
    rows_new = decay_rate * rows_old + (1.0 - decay_rate) * lax.optimization_barrier(jnp.mean(squares, axis=1))
    columns_new = decay_rate * columns_old + (1.0 - decay_rate) * lax.optimization_barrier(jnp.mean(squares, axis=0))
    estimate = rows_new[:, None] * columns_new[None, :] / jnp.mean(rows_new)
    update = gradient * lax.rsqrt(estimate)
    update = update / jnp.maximum(1.0, jnp.sqrt(jnp.mean(update * update)) / CLIP_LEVEL)
    scale_now = STEP_RATE * jnp.maximum(SECOND_EPS, jnp.sqrt(jnp.mean(weight_now * weight_now)))
    return (weight_now - scale_now * update, rows_new, columns_new)

def adafactor_vector(weight_now, gradient, moments_old, decay_rate):
    moments_new = decay_rate * moments_old + (1.0 - decay_rate) * (gradient * gradient + FIRST_EPS)
    update = gradient * lax.rsqrt(moments_new)
    update = update / jnp.maximum(1.0, jnp.sqrt(lax.optimization_barrier(jnp.mean(update * update, axis=1, keepdims=True))) / CLIP_LEVEL)
    scale_now = STEP_RATE * jnp.maximum(SECOND_EPS, jnp.sqrt(lax.optimization_barrier(jnp.mean(weight_now * weight_now, axis=1, keepdims=True))))
    return (weight_now - scale_now * update, moments_new)

def reference(fields_in, cotangent, member_dates, date_table, norm_gains, spectral_filter, weight_in, weight_out, gain_moments, in_row_stats, in_column_stats, out_row_stats, out_column_stats, filter_row_stats, filter_column_stats):
    tables = legendre_table() + dft_tables()
    offsets = date_table[member_dates.astype(jnp.int32)][:, None, None, :]

    def forward_pass(inputs, gains_now, response, inner_weight, outer_weight):
        shifted = inputs + offsets
        normed = low(low_back(rms_norm(shifted, gains_now[0])))
        hidden_state = shifted + spectral(normed, response, tables)
        second_normed = low(rms_norm(hidden_state, gains_now[1]))
        preact = low_back(jnp.einsum('bjkc,ch->bjkh', second_normed, low(inner_weight), precision=HIGHEST))
        activation = low(jax.nn.gelu(preact, approximate=False))
        return hidden_state + jnp.einsum('bjkh,hc->bjkc', activation, low(outer_weight), precision=HIGHEST)
    output, pullback = jax.vjp(forward_pass, fields_in.astype(jnp.float32), norm_gains, spectral_filter, weight_in, weight_out)
    input_grad, grad_gains, grad_filter, grad_weight_in, grad_weight_out = pullback(cotangent.astype(jnp.float32))
    decay_rate = 1.0 - STEP ** (-0.8)
    new_weight_in, new_in_rows, new_in_columns = adafactor_matrix(weight_in, grad_weight_in, in_row_stats, in_column_stats, decay_rate)
    new_weight_out, new_out_rows, new_out_columns = adafactor_matrix(weight_out, grad_weight_out, out_row_stats, out_column_stats, decay_rate)
    new_filter, new_filter_rows, new_filter_columns = adafactor_matrix(spectral_filter, grad_filter, filter_row_stats, filter_column_stats, decay_rate)
    new_gains, new_moments = adafactor_vector(norm_gains, grad_gains, gain_moments, decay_rate)
    return (output.astype(jnp.bfloat16), input_grad, grad_weight_in, grad_weight_out, grad_filter, grad_gains, new_weight_in, new_weight_out, new_filter, new_gains, new_in_rows, new_in_columns, new_out_rows, new_out_columns, new_filter_rows, new_filter_columns, new_moments)
```

```python
import math

import jax
import jax.numpy as jnp
import numpy as np
from jax import lax
from jax.experimental import pallas as pl
from jax.experimental.pallas import tpu as pltpu
from jax.sharding import PartitionSpec as P

NLAT = 128
NLON = 256
L = 128
M = 96
Q = 2 * M
STEP = 3
LANES = 128

NORM_EPS = 1e-06
FIRST_EPS = 1e-30
SECOND_EPS = 0.001
CLIP_LEVEL = 0.5
STEP_RATE = 0.5
F32 = jnp.float32
LOW = jnp.bfloat16
VMEM_LIMIT = 48 * 1024 * 1024


def legendre_table():
    angles = math.pi * (np.arange(NLAT) + 0.5) / NLAT
    cosine, sine = np.cos(angles), np.sin(angles)
    table = np.zeros((M, L, NLAT))
    for m in range(M):
        factors = np.arange(1, m + 1)
        scale = math.sqrt(0.5 * np.prod((2.0 * factors + 1.0) / (2.0 * factors)))
        table[m, m] = scale * sine**m
        for l in range(m + 1, L):
            a = math.sqrt((4.0 * l * l - 1.0) / (l * l - m * m))
            b = math.sqrt(((l - 1.0) ** 2 - m * m) / (4.0 * (l - 1.0) ** 2 - 1.0))
            earlier = table[m, l - 2] if l >= m + 2 else 0.0
            table[m, l] = a * (cosine * table[m, l - 1] - b * earlier)
    return table, math.pi / NLAT * sine


def dft_tables():
    phases = 2.0 * math.pi * (np.outer(np.arange(NLON), np.arange(M)) % NLON) / NLON
    cosine, sine = np.cos(phases), np.sin(phases)
    doubling = np.where(np.arange(M) == 0, 1.0, 2.0)
    forward = np.stack([cosine, -sine], axis=2).reshape(NLON, Q) / NLON
    inverse = np.stack([doubling * cosine, -doubling * sine], axis=2).reshape(NLON, Q).T
    return forward, inverse


def dft_kernel(rows, points, table_ref, *refs):
    slots, out_ref, scratch = refs[:-2], refs[-2], refs[-1]
    table = table_ref[...]
    for j in range(rows):
        circle = jnp.concatenate([slot[j] for slot in slots], axis=0)
        scratch[pl.ds(j, Q, stride=rows), :] = jnp.dot(
            table, circle, preferred_element_type=F32
        )
    out_ref[...] = scratch[...].astype(LOW)


def dft(table, slots):
    rows, points, lanes = slots[0].shape
    return pl.pallas_call(
        lambda *refs: dft_kernel(rows, points, *refs),
        out_shape=jax.ShapeDtypeStruct((Q * rows, lanes), LOW),
        scratch_shapes=[pltpu.VMEM((Q * rows, lanes), F32)],
        compiler_params=pltpu.CompilerParams(vmem_limit_bytes=VMEM_LIMIT),
        cost_estimate=pl.CostEstimate(
            flops=2 * Q * NLON * rows * 256, bytes_accessed=4 * rows * NLON * lanes * 4, transcendentals=0
        ),
        name="dft",
    )(table, *slots)


def idft_kernel(rows, points, table_ref, spectra_ref, *refs):
    outs, scratch = refs[:-1], refs[-1]
    scratch[...] = spectra_ref[...].astype(F32)
    table = table_ref[...]
    for j in range(rows):
        circle = jnp.dot(
            table,
            scratch[pl.ds(j, Q, stride=rows), :].astype(LOW),
            preferred_element_type=F32,
        ).astype(LOW)
        for s, out in enumerate(outs):
            out[j] = circle[s * points : (s + 1) * points]


def idft(table, spectra, rows, points, count):
    lanes = spectra.shape[1]
    return pl.pallas_call(
        lambda *refs: idft_kernel(rows, points, *refs),
        out_shape=[jax.ShapeDtypeStruct((rows, points, lanes), LOW)] * count,
        scratch_shapes=[pltpu.VMEM((Q * rows, lanes), F32)],
        compiler_params=pltpu.CompilerParams(vmem_limit_bytes=VMEM_LIMIT),
        cost_estimate=pl.CostEstimate(
            flops=2 * Q * NLON * rows * 256, bytes_accessed=4 * rows * NLON * lanes * 4, transcendentals=0
        ),
        name="idft",
    )(table, spectra)


def filter_forward_kernel(tile_ref, analysis_ref, synthesis_ref, response_ref, s_ref, out_ref, coef_ref):
    response = response_ref[0]
    shape = s_ref.shape
    for q in range(shape[1]):
        spectra = s_ref[:, q].reshape(NLAT, LANES)
        coef = jnp.dot(analysis_ref[q], spectra, preferred_element_type=F32)
        coef_ref[q] = coef
        filtered = (response * coef).astype(LOW)
        values = jnp.dot(synthesis_ref[q], filtered, preferred_element_type=F32)
        out_ref[:, q] = values.astype(LOW).reshape(shape[0], shape[2], LANES)


def filter_backward_kernel(
    tile_ref, analysis_ref, synthesis_ref, response_ref, s_ref, coef_ref, out_ref, grad_ref
):
    response = response_ref[0]
    shape = s_ref.shape
    grad = jnp.zeros((L, LANES), F32)
    for q in range(shape[1]):
        spectra = s_ref[:, q].reshape(NLAT, LANES)
        back = jnp.dot(analysis_ref[q], spectra, preferred_element_type=F32)
        grad = grad + coef_ref[q] * back
        filtered = (response * back).astype(LOW)
        values = jnp.dot(synthesis_ref[q], filtered, preferred_element_type=F32)
        out_ref[:, q] = values.astype(LOW).reshape(shape[0], shape[2], LANES)
    grad_ref[...] = grad


def whole_block(array):
    zeros = (0,) * array.ndim
    return pl.BlockSpec(array.shape, lambda i, tile: zeros)


def filter_call(kernel, name, tile, tables, response, spectra, extra, outs):
    arrays = [*tables, response, spectra, *extra]
    specs = [whole_block(a) for a in arrays]
    specs[2] = pl.BlockSpec((1, L, LANES), lambda i, tile: (tile[0], 0, 0))
    return pl.pallas_call(
        kernel,
        out_shape=outs,
        grid_spec=pltpu.PrefetchScalarGridSpec(
            num_scalar_prefetch=1,
            grid=(1,),
            in_specs=specs,
            out_specs=[whole_block(o) for o in outs],
        ),
        compiler_params=pltpu.CompilerParams(vmem_limit_bytes=VMEM_LIMIT),
        cost_estimate=pl.CostEstimate(
            flops=4 * spectra.shape[1] * L * NLAT * 256,
            bytes_accessed=8 * 1024 * 1024,
            transcendentals=0,
        ),
        name=name,
    )(tile, *arrays)


def exact_gelu(values):
    return jax.nn.gelu(values, approximate=False)


def inverse_rms(values):
    return lax.rsqrt(jnp.mean(values * values, axis=-1, keepdims=True) + NORM_EPS)


def norm_backward(values, inverse, gain, upstream):
    scaled = upstream * gain
    inner = jnp.mean(values * scaled, axis=-1, keepdims=True)
    grad = inverse * scaled - values * (inverse * inverse * inverse) * inner
    return grad, jnp.sum(upstream * values * inverse, axis=0)


def adafactor_matrix(weight_now, gradient, rows_old, columns_old, decay_rate):
    squares = gradient * gradient + FIRST_EPS
    rows_new = decay_rate * rows_old + (1.0 - decay_rate) * jnp.mean(squares, axis=1)
    columns_new = decay_rate * columns_old + (1.0 - decay_rate) * jnp.mean(squares, axis=0)
    estimate = rows_new[:, None] * columns_new[None, :] / jnp.mean(rows_new)
    update = gradient * lax.rsqrt(estimate)
    update = update / jnp.maximum(1.0, jnp.sqrt(jnp.mean(update * update)) / CLIP_LEVEL)
    scale_now = STEP_RATE * jnp.maximum(SECOND_EPS, jnp.sqrt(jnp.mean(weight_now * weight_now)))
    return (weight_now - scale_now * update, rows_new, columns_new)


def adafactor_vector(weight_now, gradient, moments_old, decay_rate):
    moments_new = decay_rate * moments_old + (1.0 - decay_rate) * (gradient * gradient + FIRST_EPS)
    update = gradient * lax.rsqrt(moments_new)
    update = update / jnp.maximum(
        1.0, jnp.sqrt(jnp.mean(update * update, axis=1, keepdims=True)) / CLIP_LEVEL
    )
    scale_now = STEP_RATE * jnp.maximum(
        SECOND_EPS, jnp.sqrt(jnp.mean(weight_now * weight_now, axis=1, keepdims=True))
    )
    return (weight_now - scale_now * update, moments_new)


def take(array, index):
    return lax.dynamic_index_in_dim(array, index, 0, keepdims=False)


def body(
    fields_in,
    cotangent,
    member_dates,
    date_table,
    norm_gains,
    spectral_filter,
    weight_in,
    weight_out,
    gain_moments,
    in_row_stats,
    in_column_stats,
    out_row_stats,
    out_column_stats,
    filter_row_stats,
    filter_column_stats,
):
    members, rows, points, channels = fields_in.shape
    tiles = channels // LANES
    wide = tiles * LANES
    lat, lon = lax.axis_size("lat"), lax.axis_size("lon")
    lat_me, lon_me = lax.axis_index("lat"), lax.axis_index("lon")
    chunks = members * tiles // lon
    share = Q // lat
    grid = rows * points

    legendre, quadrature = legendre_table()
    forward, inverse = dft_tables()
    own_q = (lat_me * share + jnp.arange(share, dtype=jnp.int32)) // 2
    plain = jnp.take(jnp.asarray(legendre, LOW), own_q, axis=0)
    weighted = jnp.take(jnp.asarray(legendre * quadrature, LOW), own_q, axis=0)
    plain_t = jnp.swapaxes(plain, 1, 2)
    weighted_t = jnp.swapaxes(weighted, 1, 2)

    def arrived(table):
        blocks = table.reshape(lon, points, Q)
        orders = [np.concatenate([blocks[(me - s) % lon] for s in range(lon)]).T for me in range(lon)]
        return take(jnp.asarray(np.stack(orders), LOW), lon_me)

    def leaving(table):
        blocks = table.reshape(lon, points, Q)
        orders = [np.concatenate([blocks[(me + s) % lon] for s in range(lon)]) for me in range(lon)]
        return take(jnp.asarray(np.stack(orders), LOW), lon_me)

    analysis, back_analysis = arrived(forward), arrived(inverse.T)
    synthesis, back_synthesis = leaving(inverse.T), leaving(forward)
    responses = jnp.swapaxes(spectral_filter[:, :wide].reshape(L, tiles, LANES), 0, 1)

    def exchange_lon(slots):
        return [
            slot
            if s == 0
            else lax.ppermute(slot, "lon", [(i, (i + s) % lon) for i in range(lon)])
            for s, slot in enumerate(slots)
        ]

    def send_units(units, r):
        stacked = jnp.stack(units)
        return exchange_lon([take(stacked, (lon_me + s) % lon) for s in range(lon)])

    def exchange_lat(blocks):
        return lax.all_to_all(blocks, "lat", split_axis=0, concat_axis=0, tiled=True)

    def to_degrees(spectra):
        got = exchange_lat(spectra.reshape(lat, share * rows, LANES)).reshape(lat, share, rows, LANES)
        if rows % 16:
            got = jnp.swapaxes(got, 0, 1).reshape(1, share, NLAT, LANES)
        return got

    def to_rows(values):
        if rows % 16:
            values = jnp.swapaxes(values.reshape(share, lat, rows, LANES), 0, 1)
        return exchange_lat(values.reshape(lat, share * rows, LANES)).reshape(Q * rows, LANES)

    def tile_of(r):
        return ((lon * r + lon_me) % tiles).astype(jnp.int32).reshape(1)

    def spectral_forward(slots, r):
        spectra = to_degrees(dft(analysis, [s.reshape(rows, points, LANES) for s in slots]))
        values, coefs = filter_call(
            filter_forward_kernel,
            "filter_forward",
            tile_of(r),
            (weighted, plain_t),
            responses,
            spectra,
            (),
            [
                jax.ShapeDtypeStruct(spectra.shape, LOW),
                jax.ShapeDtypeStruct((share, L, LANES), F32),
            ],
        )
        return idft(synthesis, to_rows(values), rows, points, lon), coefs

    def spectral_backward(slots, coefs, r):
        spectra = to_degrees(dft(back_analysis, [s.reshape(rows, points, LANES) for s in slots]))
        values, grad = filter_call(
            filter_backward_kernel,
            "filter_backward",
            tile_of(r),
            (plain, weighted_t),
            responses,
            spectra,
            (coefs,),
            [
                jax.ShapeDtypeStruct(spectra.shape, LOW),
                jax.ShapeDtypeStruct((L, LANES), F32),
            ],
        )
        return idft(back_synthesis, to_rows(values), rows, points, lon), grad

    rest = channels - wide
    response_rest = spectral_filter[:, wide:]
    own_points = lon_me * points

    def rest_in(values, table):
        whole = lax.all_gather(values, "lon", axis=2, tiled=True)
        spectra = jnp.einsum(
            "bjkc,kq->bcjq", whole, jnp.asarray(table, LOW), preferred_element_type=F32
        ).astype(LOW)
        spectra = lax.all_gather(spectra, "lat", axis=2, tiled=True)
        return lax.dynamic_slice_in_dim(spectra, lat_me * share, share, 3)

    def rest_out(filtered, degrees, table):
        values = jnp.einsum(
            "qjl,qlbc->bcjq", degrees, filtered, preferred_element_type=F32
        ).astype(LOW)
        values = lax.all_gather(values, "lat", axis=3, tiled=True)
        values = lax.dynamic_slice_in_dim(values, lat_me * rows, rows, 2)
        own = lax.dynamic_slice_in_dim(jnp.asarray(table, LOW), own_points, points, 0)
        return jnp.einsum("bcjq,kq->bjkc", values, own, preferred_element_type=F32).astype(LOW)

    date_selector = (
        member_dates[:, None] == jnp.arange(date_table.shape[0], dtype=jnp.int32)[None, :]
    ).astype(F32)
    offsets = jnp.dot(date_selector, date_table, precision=lax.Precision.HIGHEST)
    shifted, first_inverse, normed = [], [], []
    for b in range(members):
        moved = fields_in[b].reshape(grid, channels).astype(F32) + offsets[b]
        scale = inverse_rms(moved)
        shifted.append(moved)
        first_inverse.append(scale)
        normed.append((moved * scale * norm_gains[0]).astype(LOW))

    def units_of(member_values):
        return [
            values[:, t * LANES : (t + 1) * LANES] for values in member_values for t in range(tiles)
        ]

    def rest_of(member_values):
        return jnp.stack([v[:, wide:].reshape(rows, points, rest) for v in member_values])

    def gather_member(arrivals, rest_values, b):
        pieces = []
        for t in range(tiles):
            r, owner = divmod(b * tiles + t, lon)
            pieces.append(take(arrivals[r], (lon_me - owner) % lon).reshape(grid, LANES))
        return jnp.concatenate([*pieces, rest_values[b].reshape(grid, rest)], axis=1)

    units = units_of(normed)
    coefs, arrivals = [], []
    for r in range(chunks):
        slots = send_units(units[r * lon : (r + 1) * lon], r)
        out, coef = spectral_forward(slots, r)
        coefs.append(coef)
        arrivals.append(jnp.stack(exchange_lon(out)))
    spectra_rest = rest_in(rest_of(normed), forward)
    coefs_rest = jnp.einsum("qlj,bcjq->qlbc", weighted, spectra_rest, preferred_element_type=F32)
    filtered_rest = (response_rest[None, :, None, :] * coefs_rest).astype(LOW)
    branch_rest = rest_out(filtered_rest, plain_t, inverse.T)

    inner_low = weight_in.astype(LOW)
    outer_low = weight_out.astype(LOW)
    block_output, back_hidden, back_low = [], [], []
    grad_in_part = grad_out_part = gain_two_part = 0.0
    for b in range(members):
        branch = gather_member(arrivals, branch_rest, b)
        upstream = cotangent[b].reshape(grid, channels)
        hidden = shifted[b] + branch.astype(F32)
        second_inverse = inverse_rms(hidden)
        second_low = (hidden * second_inverse * norm_gains[1]).astype(LOW)
        preact = jnp.dot(second_low, inner_low, preferred_element_type=F32)
        activation, gelu_pull = jax.vjp(exact_gelu, preact)
        active_low = activation.astype(LOW)
        block_output.append(
            (hidden + jnp.dot(active_low, outer_low, preferred_element_type=F32)).astype(LOW)
        )
        grad_out_part += jnp.einsum("gh,gc->hc", active_low, upstream, preferred_element_type=F32)
        back_active = jnp.einsum("gc,hc->gh", upstream, outer_low, preferred_element_type=F32)
        back_preact = gelu_pull(back_active)[0].astype(LOW)
        grad_in_part += jnp.einsum("gc,gh->ch", second_low, back_preact, preferred_element_type=F32)
        back_second = jnp.einsum("gh,ch->gc", back_preact, inner_low, preferred_element_type=F32)
        grad, gain_part = norm_backward(hidden, second_inverse, norm_gains[1], back_second)
        gain_two_part += gain_part
        grad = grad + upstream.astype(F32)
        back_hidden.append(grad)
        back_low.append(grad.astype(LOW))

    units = units_of(back_low)
    arrivals, grads = [], []
    for r in range(chunks):
        slots = send_units(units[r * lon : (r + 1) * lon], r)
        out, grad = spectral_backward(slots, coefs[r], r)
        grads.append(grad)
        arrivals.append(jnp.stack(exchange_lon(out)))
    spectra_rest = rest_in(rest_of(back_low), inverse.T)
    back_rest = jnp.einsum("qlj,bcjq->qlbc", plain, spectra_rest, preferred_element_type=F32)
    grad_rest = jnp.sum(coefs_rest * back_rest, axis=(0, 2)) / lon
    filtered_rest = (response_rest[None, :, None, :] * back_rest).astype(LOW)
    normed_rest = rest_out(filtered_rest, weighted_t, forward)

    input_grad, gain_one_part = [], 0.0
    for b in range(members):
        back_normed = gather_member(arrivals, normed_rest, b).astype(F32)
        grad, gain_part = norm_backward(shifted[b], first_inverse[b], norm_gains[0], back_normed)
        gain_one_part += gain_part
        input_grad.append((back_hidden[b] + grad).reshape(rows, points, channels))

    stacked = jnp.stack(grads)
    ordered = []
    for t in range(tiles):
        hits = jnp.stack([(tile_of(r)[0] == t) for r in range(chunks)])
        ordered.append(jnp.sum(jnp.where(hits[:, None, None], stacked, 0.0), axis=0))
    filter_part = jnp.concatenate([*ordered, grad_rest], axis=1)

    grad_weight_in, grad_weight_out = lax.psum((grad_in_part, grad_out_part), ("lat", "lon"))
    grad_filter, grad_gains = lax.psum(
        (filter_part, jnp.stack([gain_one_part, gain_two_part])), ("lat", "lon")
    )
    decay_rate = 1.0 - STEP ** (-0.8)
    new_weight_in, new_in_rows, new_in_columns = adafactor_matrix(
        weight_in, grad_weight_in, in_row_stats, in_column_stats, decay_rate
    )
    new_weight_out, new_out_rows, new_out_columns = adafactor_matrix(
        weight_out, grad_weight_out, out_row_stats, out_column_stats, decay_rate
    )
    new_filter, new_filter_rows, new_filter_columns = adafactor_matrix(
        spectral_filter, grad_filter, filter_row_stats, filter_column_stats, decay_rate
    )
    new_gains, new_moments = adafactor_vector(norm_gains, grad_gains, gain_moments, decay_rate)
    return (
        jnp.stack(block_output).reshape(fields_in.shape),
        jnp.stack(input_grad),
        grad_weight_in,
        grad_weight_out,
        grad_filter,
        grad_gains,
        new_weight_in,
        new_weight_out,
        new_filter,
        new_gains,
        new_in_rows,
        new_in_columns,
        new_out_rows,
        new_out_columns,
        new_filter_rows,
        new_filter_columns,
        new_moments,
    )


def solution(mesh):
    spread = P(None, "lat", "lon", None)
    return jax.shard_map(
        body,
        mesh=mesh,
        in_specs=(spread, spread) + (P(),) * 13,
        out_specs=(spread, spread) + (P(),) * 15,
        check_vma=False,
    )
```

```python
import math

import jax
import jax.numpy as jnp
import numpy as np
from jax import lax
from jax.experimental import pallas as pl
from jax.experimental.pallas import tpu as pltpu
from jax.sharding import PartitionSpec as P

NLAT = 128
NLON = 256
L = 128
M = 96
Q = 2 * M
STEP = 3
LANES = 128

NORM_EPS = 1e-06
FIRST_EPS = 1e-30
SECOND_EPS = 0.001
CLIP_LEVEL = 0.5
STEP_RATE = 0.5
F32 = jnp.float32
LOW = jnp.bfloat16
VMEM_LIMIT = 60 * 1024 * 1024


def legendre_table():
    angles = math.pi * (np.arange(NLAT) + 0.5) / NLAT
    cosine, sine = np.cos(angles), np.sin(angles)
    table = np.zeros((M, L, NLAT))
    for m in range(M):
        factors = np.arange(1, m + 1)
        scale = math.sqrt(0.5 * np.prod((2.0 * factors + 1.0) / (2.0 * factors)))
        table[m, m] = scale * sine**m
        for l in range(m + 1, L):
            a = math.sqrt((4.0 * l * l - 1.0) / (l * l - m * m))
            b = math.sqrt(((l - 1.0) ** 2 - m * m) / (4.0 * (l - 1.0) ** 2 - 1.0))
            earlier = table[m, l - 2] if l >= m + 2 else 0.0
            table[m, l] = a * (cosine * table[m, l - 1] - b * earlier)
    return table, math.pi / NLAT * sine


def dft_tables():
    phases = 2.0 * math.pi * (np.outer(np.arange(NLON), np.arange(M)) % NLON) / NLON
    cosine, sine = np.cos(phases), np.sin(phases)
    doubling = np.where(np.arange(M) == 0, 1.0, 2.0)
    forward = np.stack([cosine, -sine], axis=2).reshape(NLON, Q) / NLON
    inverse = np.stack([doubling * cosine, -doubling * sine], axis=2).reshape(NLON, Q).T
    return forward, inverse


EXTRA = 16


def point_masks(n, points):
    row_of = lax.broadcasted_iota(jnp.int32, (n, EXTRA), 0) // points
    sel = (row_of == lax.broadcasted_iota(jnp.int32, (n, EXTRA), 1)).astype(F32).astype(LOW)
    place = lax.broadcasted_iota(jnp.int32, (n, LANES), 0) % points
    lane = lax.broadcasted_iota(jnp.int32, (n, LANES), 1)
    return sel, place == lane, lane == 0


def load_points(ref, n, points):
    tiles = ref.shape[0] // n
    sel, diagonal, first = point_masks(n, points)
    extra = jnp.dot(sel, ref[tiles * n : tiles * n + EXTRA, :], preferred_element_type=F32)
    column = jnp.sum(jnp.where(diagonal, extra, 0.0), axis=1, keepdims=True)
    pieces = [ref[t * n : (t + 1) * n, :].astype(F32) for t in range(tiles)]
    return jnp.concatenate([*pieces, jnp.where(first, column, 0.0)], axis=1)


def store_points(ref, values, last, points):
    n = values.shape[0]
    tiles = ref.shape[0] // n
    _, diagonal, _ = point_masks(n, points)
    for t in range(tiles):
        ref[t * n : (t + 1) * n, :] = values[:, t * LANES : (t + 1) * LANES]
    spread = jnp.where(diagonal, last, 0.0).astype(LOW)
    row_of = lax.broadcasted_iota(jnp.int32, (EXTRA, n), 1) // points
    pick = (row_of == lax.broadcasted_iota(jnp.int32, (EXTRA, n), 0)).astype(F32).astype(LOW)
    ref[tiles * n : tiles * n + EXTRA, :] = jnp.dot(
        pick, spread, preferred_element_type=F32
    ).astype(LOW)


def params():
    return pltpu.CompilerParams(vmem_limit_bytes=VMEM_LIMIT)


def cost(flops, size, transcendentals=0):
    return pl.CostEstimate(flops=1024, bytes_accessed=400_000_000, transcendentals=0)


def fixed(array):
    zeros = (0,) * len(array.shape)
    return pl.BlockSpec(array.shape, lambda *_: zeros)


def once(array):
    zeros = (0,) * len(array.shape)
    return pl.BlockSpec(array.shape, lambda *_: zeros, pipeline_mode=pl.Buffered(1))


def slot_table(table, count):
    return pl.BlockSpec(
        (1, *table.shape[1:]), lambda s, me_ref: ((me_ref[0] + (count - s)) % count, 0, 0)
    )


def pack(me, source, chunk, depth, count):
    _, _, points, channels = source.shape
    n = depth * points
    tiles = channels // LANES

    def kernel(me_ref, source_ref, *outs):
        step = pl.program_id(0)
        values = source_ref[0].reshape(n, channels)
        last = values[:, tiles * LANES :].astype(F32)
        for s, out in enumerate(outs):

            @pl.when(step == s)
            def _():
                store_points(out, values, last, points)

    shape = jax.ShapeDtypeStruct((tiles * n + EXTRA, LANES), LOW)
    return pl.pallas_call(
        kernel,
        out_shape=[shape] * count,
        grid_spec=pltpu.PrefetchScalarGridSpec(
            num_scalar_prefetch=1,
            grid=(count,),
            in_specs=[
                pl.BlockSpec(
                    (1, depth, points, channels),
                    lambda s, me_ref: ((me_ref[0] + s) % count, chunk, 0, 0),
                )
            ],
            out_specs=[fixed(shape)] * count,
        ),
        compiler_params=params(),
        cost_estimate=cost(0, 4 * count * n * channels),
        name="pack",
    )(me, source)


def unpack(me, slots, target, chunk, depth, shape, dtype):
    members, rows, points, channels = shape
    n = depth * points
    count = len(slots)

    def kernel(me_ref, *refs):
        out = refs[-1]
        step = pl.program_id(0)
        for s in range(count):

            @pl.when(step == s)
            def _():
                values = load_points(refs[s], n, points)[:, :channels]
                out[0] = values.astype(dtype).reshape(depth, points, channels)

    specs = [fixed(s) for s in slots]
    arrays = list(slots)
    aliases = {}
    if target is not None:
        specs.append(pl.BlockSpec(memory_space=pl.ANY))
        arrays.append(target)
        aliases = {count + 1: 0}
    return pl.pallas_call(
        kernel,
        out_shape=jax.ShapeDtypeStruct(shape, dtype),
        grid_spec=pltpu.PrefetchScalarGridSpec(
            num_scalar_prefetch=1,
            grid=(count,),
            in_specs=specs,
            out_specs=pl.BlockSpec(
                (1, depth, points, channels),
                lambda s, me_ref: ((me_ref[0] + s) % count, chunk, 0, 0),
            ),
        ),
        input_output_aliases=aliases,
        compiler_params=params(),
        cost_estimate=cost(0, 6 * count * n * channels),
        name="unpack",
    )(me, *arrays)


def first_forward(me, table, slots, offset, gain, depth, points, channels):
    n = depth * points
    count = len(slots)

    def kernel(me_ref, table_ref, offset_ref, gain_ref, *refs):
        out, total = refs[-2:]
        for s, slot in enumerate(refs[:-2]):
            shifted = load_points(slot, n, points) + offset_ref[...]
            square = jnp.sum(shifted * shifted, axis=1, keepdims=True)
            scale = lax.rsqrt(square * (1.0 / channels) + NORM_EPS)
            normed = (shifted * scale * gain_ref[...]).astype(LOW)
            owner = (me_ref[0] + (count - s)) % count
            part = jnp.dot(table_ref[owner], normed, preferred_element_type=F32)
            if s == 0:
                total[...] = part
            else:
                total[...] += part
        out[...] = total[...].astype(LOW)

    width = gain.shape[1]
    size = table.shape[1]
    arrays = [table, offset, gain, *slots]
    shape = jax.ShapeDtypeStruct((size, width), LOW)
    return pl.pallas_call(
        kernel,
        out_shape=shape,
        grid_spec=pltpu.PrefetchScalarGridSpec(
            num_scalar_prefetch=1,
            grid=(1,),
            in_specs=[fixed(a) for a in arrays],
            out_specs=fixed(shape),
            scratch_shapes=[pltpu.VMEM((size, width), F32)],
        ),
        compiler_params=params(),
        cost_estimate=cost(2 * size * count * n * width, 6 * 1024 * 1024),
        name="first_forward",
    )(me, *arrays)


def degree_blocks(refs, counts, lat, step, groups):
    for ref, count in zip(refs, counts):
        size = ref.shape[0]
        if groups == 1 and count == 1:
            yield ref, slice(0, size)
            continue
        part = size // lat // count // groups
        for c in range(count):
            for i in range(lat):
                start = (i * count + c) * (part * groups) + step * part
                yield ref, pl.ds(pl.multiple_of(start, part), part)


def degree_tables(to_ref, back_ref, spots_ref, spots_back_ref, each):
    group = spots_ref.shape[0]
    to = [
        jnp.dot(to_ref[q // each], spots_ref[q], preferred_element_type=F32).astype(LOW)
        for q in range(group)
    ]
    back = [
        jnp.dot(spots_back_ref[q], back_ref[q // each], preferred_element_type=F32).astype(LOW)
        for q in range(group)
    ]
    return jnp.concatenate(to, axis=0), jnp.concatenate(back, axis=1)


def filter_call(kernel, name, first, tables, spots, response, extra, spectra, each, groups, outs):
    part = tables[0].shape[0]
    block = spots[0].shape[0] // each
    tabled = pl.BlockSpec((block, L, NLAT), lambda g, first: (first[0] + g, 0, 0))
    grouped = lambda a: pl.BlockSpec((1, *a.shape[1:]), lambda g, first: (g, 0, 0))
    spec = lambda a: grouped(a) if len(a.shape) == 3 else fixed(a)
    arrays = [*tables, *spots, response, *extra, *spectra]
    return pl.pallas_call(
        kernel,
        out_shape=outs,
        grid_spec=pltpu.PrefetchScalarGridSpec(
            num_scalar_prefetch=1,
            grid=(groups,),
            in_specs=[tabled, tabled, fixed(spots[0]), fixed(spots[1]), fixed(response)]
            + [spec(a) for a in (*extra, *spectra)],
            out_specs=[spec(o) for o in outs],
        ),
        compiler_params=params(),
        cost_estimate=cost(16 * part, 24 * 1024 * 1024),
        name=name,
    )(first, *arrays)


def filter_forward(
    first, tables, spots, response, spectra, counts, out_counts, lat, each, groups
):
    size = spots[0].shape[2]
    width = response.shape[1]
    count = len(spectra)

    def kernel(first_ref, to_ref, back_ref, spots_ref, spots_back_ref, response_ref, *refs):
        step = pl.program_id(0)
        ins, outs, coefs = refs[:count], refs[count:-1], refs[-1]
        to, back = degree_tables(to_ref, back_ref, spots_ref, spots_back_ref, each)
        values = jnp.concatenate(
            [ref[rows, :] for ref, rows in degree_blocks(ins, counts, lat, step, groups)], axis=0
        )
        coef = jnp.dot(to, values, preferred_element_type=F32)
        coefs[0] = coef
        scale = jnp.concatenate([response_ref[...]] * (size // L), axis=0)
        filtered = (scale * coef).astype(LOW)
        result = jnp.dot(back, filtered, preferred_element_type=F32).astype(LOW)
        begin = 0
        for ref, rows in degree_blocks(outs, out_counts, lat, step, groups):
            length = rows.stop if isinstance(rows, slice) else rows.size
            ref[rows, :] = result[begin : begin + length]
            begin += length

    height = sum(s.shape[0] for s in spectra) // sum(counts)
    outs = [jax.ShapeDtypeStruct((height * c, width), LOW) for c in out_counts]
    outs.append(jax.ShapeDtypeStruct((groups, size, width), F32))
    return filter_call(
        kernel, "filter_forward", first, tables, spots, response, (), spectra, each, groups, outs
    )


def filter_backward(
    first, tables, spots, response, coefs, spectra, counts, out_counts, lat, each, groups
):
    size = spots[0].shape[2]
    width = response.shape[1]
    count = len(spectra)

    def kernel(
        first_ref, to_ref, back_ref, spots_ref, spots_back_ref, response_ref, coefs_ref, *refs
    ):
        step = pl.program_id(0)
        ins, outs, grad_ref = refs[:count], refs[count:-1], refs[-1]
        to, back = degree_tables(to_ref, back_ref, spots_ref, spots_back_ref, each)
        values = jnp.concatenate(
            [ref[rows, :] for ref, rows in degree_blocks(ins, counts, lat, step, groups)], axis=0
        )
        upstream = jnp.dot(to, values, preferred_element_type=F32)
        product = coefs_ref[0] * upstream
        grad = product[:L]
        for q in range(1, size // L):
            grad = grad + product[q * L : (q + 1) * L]

        @pl.when(step == 0)
        def _():
            grad_ref[...] = jnp.zeros_like(grad_ref)

        grad_ref[...] += grad
        scale = jnp.concatenate([response_ref[...]] * (size // L), axis=0)
        filtered = (scale * upstream).astype(LOW)
        result = jnp.dot(back, filtered, preferred_element_type=F32).astype(LOW)
        begin = 0
        for ref, rows in degree_blocks(outs, out_counts, lat, step, groups):
            length = rows.stop if isinstance(rows, slice) else rows.size
            ref[rows, :] = result[begin : begin + length]
            begin += length

    height = sum(s.shape[0] for s in spectra) // sum(counts)
    outs = [jax.ShapeDtypeStruct((height * c, width), LOW) for c in out_counts]
    outs.append(jax.ShapeDtypeStruct((L, width), F32))
    return filter_call(
        kernel,
        "filter_backward",
        first,
        tables,
        spots,
        response,
        (coefs,),
        spectra,
        each,
        groups,
        outs,
    )


def prepare_weights(weight_in, weight_out, width, hidden_width):
    channels, units = weight_in.shape

    def kernel(in_ref, out_ref, w_in, w_out, w_in_t, w_out_t):
        w_in[...] = jnp.zeros_like(w_in)
        w_out_t[...] = jnp.zeros_like(w_out_t)
        w_in[:channels, :units] = in_ref[...].astype(LOW)
        w_out_t[:channels, :units] = out_ref[...].astype(LOW)
        w_in_t[...] = w_in[...].T
        w_out[...] = w_out_t[...].T

    outs = [
        jax.ShapeDtypeStruct(shape, LOW)
        for shape in [(width, hidden_width), (hidden_width, width)] * 2
    ]
    outs = [outs[0], outs[1], outs[1], outs[0]]
    return pl.pallas_call(
        kernel, out_shape=outs, compiler_params=params(), name="prepare_weights"
    )(weight_in, weight_out.T)


def feed_forward(
    me, tables, weights, offset, gain, spectra, slots, upstreams, lat, depth, points, channels
):
    n = depth * points
    pair, count = len(slots), len(slots[0])
    flat = [slot for chunk in slots for slot in chunk]
    width, hidden_width = weights[0].shape
    size = spectra.shape[0] // pair
    part = size // lat
    inverse_channels = 1.0 / channels

    def kernel(
        me_ref, out_table, back_table, w_in, w_out, w_in_t, w_out_t, offset_ref, gain_ref, y, *refs
    ):
        ins, ups = refs[: pair * count], refs[pair * count : (pair + 1) * count]
        refs = refs[(pair + 1) * count :]
        outs = refs[:count]
        grad_ref, second_ref, active_ref, pre_ref, cot_ref, gain_part, back_ref = refs[count:-4]
        x_now, up_now, y_now, total = refs[-4:]
        step = pl.program_id(0)

        @pl.when(step == 0)
        def _():
            gain_part[...] = jnp.zeros_like(gain_part)
            total[...] = jnp.zeros_like(total)
            for c in range(pair):
                for i in range(lat):
                    y_now[c, i * part : (i + 1) * part] = y[
                        (i * pair + c) * part : (i * pair + c + 1) * part
                    ]

        for s in range(count):

            @pl.when(step == s)
            def _():
                for c in range(pair):
                    x_now[c] = ins[c * count + s][...]
                up_now[...] = ups[s][...]

        rows = lambda parts: jnp.concatenate(parts, axis=0) if pair > 1 else parts[0]
        branch = rows(
            [
                jnp.dot(out_table[0], y_now[c], preferred_element_type=F32).astype(LOW)
                for c in range(pair)
            ]
        )
        shifted = rows([load_points(x_now.at[c], n, points) for c in range(pair)])
        hidden = shifted + offset_ref[...] + branch.astype(F32)
        square = jnp.sum(hidden * hidden, axis=1, keepdims=True)
        scale = lax.rsqrt(square * inverse_channels + NORM_EPS)
        second = (hidden * scale * gain_ref[...]).astype(LOW)
        second_ref[...] = second
        upstream = load_points(up_now, pair * n, points)
        upstream_low = upstream.astype(LOW)
        cot_ref[...] = upstream_low
        preact = jnp.dot(second, w_in[...], preferred_element_type=F32)
        back_active = jnp.dot(upstream_low, w_out_t[...], preferred_element_type=F32)
        share = 0.5 + 0.5 * lax.erf(preact * math.sqrt(0.5))
        density = jnp.exp(-0.5 * preact * preact) * (1.0 / math.sqrt(2.0 * math.pi))
        active = (preact * share).astype(LOW)
        active_ref[...] = active
        back_preact = (back_active * (share + preact * density)).astype(LOW)
        pre_ref[...] = back_preact
        output = hidden + jnp.dot(active, w_out[...], preferred_element_type=F32)
        back_second = jnp.dot(back_preact, w_in_t[...], preferred_element_type=F32)
        scaled = back_second * gain_ref[...]
        inner = jnp.sum(hidden * scaled, axis=1, keepdims=True) * inverse_channels
        grad = scale * scaled - hidden * (scale * scale * scale * inner) + upstream
        grad_ref[...] = grad
        grad_low = grad.astype(LOW)
        for c in range(pair):
            total[c] += jnp.dot(
                back_table[0], grad_low[c * n : (c + 1) * n], preferred_element_type=F32
            )
        gain_part[...] += jnp.sum(
            (back_second * (hidden * scale)).reshape(pair * n // 8, 8, width), axis=0
        )

        @pl.when(step == count - 1)
        def _():
            for c in range(pair):
                for i in range(lat):
                    back_ref[(i * pair + c) * part : (i * pair + c + 1) * part] = total[
                        c, i * part : (i + 1) * part
                    ].astype(LOW)

        store_points(up_now, output.astype(LOW), output[:, channels - 1 : channels], points)
        for s in range(count):

            @pl.when(step == s)
            def _():
                outs[s][...] = up_now[...]

    rows = lambda w: pl.BlockSpec((pair * n, w), lambda s, me_ref: (s, 0))
    slot = jax.ShapeDtypeStruct(upstreams[0].shape, LOW)
    height = count * pair * n
    outs = [slot] * count + [
        jax.ShapeDtypeStruct((height, width), F32),
        jax.ShapeDtypeStruct((height, width), LOW),
        jax.ShapeDtypeStruct((height, hidden_width), LOW),
        jax.ShapeDtypeStruct((height, hidden_width), LOW),
        jax.ShapeDtypeStruct((height, width), LOW),
        jax.ShapeDtypeStruct((8, width), F32),
        jax.ShapeDtypeStruct(spectra.shape, LOW),
    ]
    out_specs = [fixed(slot)] * count + [
        rows(width),
        rows(width),
        rows(hidden_width),
        rows(hidden_width),
        rows(width),
        fixed(outs[-2]),
        fixed(outs[-1]),
    ]
    arrays = [*tables, *weights, offset, gain, spectra, *flat, *upstreams]
    return pl.pallas_call(
        kernel,
        out_shape=outs,
        grid_spec=pltpu.PrefetchScalarGridSpec(
            num_scalar_prefetch=1,
            grid=(count,),
            in_specs=[slot_table(t, count) for t in tables] + [once(a) for a in arrays[2:]],
            out_specs=out_specs,
            scratch_shapes=[
                pltpu.VMEM((pair, *flat[0].shape), LOW),
                pltpu.VMEM(slot.shape, LOW),
                pltpu.VMEM((pair, size, width), LOW),
                pltpu.VMEM((pair, size, width), F32),
            ],
        ),
        compiler_params=params(),
        cost_estimate=cost(0, 0),
        name="feed_forward",
    )(me, *arrays)


def first_backward(
    me, table, spectra, slots, grads, place, pair, offset, gain, depth, points, channels
):
    n = depth * points
    count = len(slots)
    width = gain.shape[1]
    inverse_channels = 1.0 / channels

    def kernel(me_ref, table_ref, y, grad_ref, offset_ref, gain_ref, *refs):
        ins, outs, now = refs[:count], refs[count:-1], refs[-1]
        step = pl.program_id(0)
        for s in range(count):

            @pl.when(step == s)
            def _():
                now[...] = ins[s][...]

        back = jnp.dot(table_ref[0], y[...], preferred_element_type=F32).astype(LOW).astype(F32)
        shifted = load_points(now, n, points) + offset_ref[...]
        square = jnp.sum(shifted * shifted, axis=1, keepdims=True)
        scale = lax.rsqrt(square * inverse_channels + NORM_EPS)
        scaled = back * gain_ref[...]
        inner = jnp.sum(shifted * scaled, axis=1, keepdims=True) * inverse_channels
        result = grad_ref[...] + scale * scaled - shifted * (scale * scale * scale * inner)
        store_points(now, result.astype(LOW), result[:, channels - 1 : channels], points)
        for s in range(count):

            @pl.when(step == s)
            def _():
                outs[s][...] = now[...]

    slot = jax.ShapeDtypeStruct(slots[0].shape, LOW)
    outs = [slot] * count
    return pl.pallas_call(
        kernel,
        out_shape=outs,
        grid_spec=pltpu.PrefetchScalarGridSpec(
            num_scalar_prefetch=1,
            grid=(count,),
            in_specs=[
                slot_table(table, count),
                fixed(spectra),
                pl.BlockSpec((n, width), lambda s, me_ref: (s * pair + place, 0)),
                fixed(offset),
                fixed(gain),
            ]
            + [fixed(s) for s in slots],
            out_specs=[fixed(o) for o in outs],
            scratch_shapes=[pltpu.VMEM(slot.shape, LOW)],
        ),
        compiler_params=params(),
        cost_estimate=cost(2 * count * n * width * spectra.shape[0], 12 * 1024 * 1024),
        name="first_backward",
    )(me, table, spectra, grads, offset, gain, *slots)


def adafactor_matrix(weight_now, gradient, rows_old, columns_old, decay_rate):
    squares = gradient * gradient + FIRST_EPS
    rows_new = decay_rate * rows_old + (1.0 - decay_rate) * jnp.mean(squares, axis=1)
    columns_new = decay_rate * columns_old + (1.0 - decay_rate) * jnp.mean(squares, axis=0)
    estimate = rows_new[:, None] * columns_new[None, :] / jnp.mean(rows_new)
    update = gradient * lax.rsqrt(estimate)
    update = update / jnp.maximum(1.0, jnp.sqrt(jnp.mean(update * update)) / CLIP_LEVEL)
    scale_now = STEP_RATE * jnp.maximum(SECOND_EPS, jnp.sqrt(jnp.mean(weight_now * weight_now)))
    return (weight_now - scale_now * update, rows_new, columns_new)


def adafactor_vector(weight_now, gradient, moments_old, decay_rate):
    moments_new = decay_rate * moments_old + (1.0 - decay_rate) * (gradient * gradient + FIRST_EPS)
    update = gradient * lax.rsqrt(moments_new)
    update = update / jnp.maximum(
        1.0, jnp.sqrt(jnp.mean(update * update, axis=1, keepdims=True)) / CLIP_LEVEL
    )
    scale_now = STEP_RATE * jnp.maximum(
        SECOND_EPS, jnp.sqrt(jnp.mean(weight_now * weight_now, axis=1, keepdims=True))
    )
    return (weight_now - scale_now * update, moments_new)


def tie(*groups):
    return lax.optimization_barrier(groups)


def take(array, index):
    return lax.dynamic_index_in_dim(array, index, 0, keepdims=False)


def chunk_rows(rows):
    return rows // 4 if rows % 4 == 0 else rows


def group_size(share, depth):
    for size in range(1, share):
        if share % size == 0 and size * depth % 16 == 0:
            return size
    return share


def body(
    fields_in,
    cotangent,
    member_dates,
    date_table,
    norm_gains,
    spectral_filter,
    weight_in,
    weight_out,
    gain_moments,
    in_row_stats,
    in_column_stats,
    out_row_stats,
    out_column_stats,
    filter_row_stats,
    filter_column_stats,
):
    members, rows, points, channels = fields_in.shape
    units = weight_in.shape[1]
    width = -(-channels // LANES) * LANES
    hidden_width = -(-units // LANES) * LANES
    lat, lon = lax.axis_size("lat"), lax.axis_size("lon")
    lat_me, lon_me = lax.axis_index("lat"), lax.axis_index("lon")
    me = lon_me.astype(jnp.int32).reshape(1)
    share = Q // lat
    depth = chunk_rows(rows)
    chunks = rows // depth
    pair = 2 if chunks % 2 == 0 else 1
    mids = chunks // pair
    n = depth * points

    def wider(array, *sizes):
        return jnp.pad(array, [(0, s - d) for s, d in zip(sizes, array.shape)])

    def exchange_lon(name, slots, sign):
        with jax.named_scope(name):
            return [
                slot
                if s == 0
                else lax.ppermute(slot, "lon", [(i, (i + sign * s) % lon) for i in range(lon)])
                for s, slot in enumerate(slots)
            ]

    def exchange_lat(name, *spectra):
        blocks = [a.reshape(lat, -1, width) for a in spectra]
        blocks = jnp.concatenate(blocks, axis=1) if len(blocks) > 1 else blocks[0]
        with jax.named_scope(name):
            blocks = lax.all_to_all(blocks, "lat", split_axis=0, concat_axis=0, tiled=True)
        return blocks.reshape(-1, width)

    inside = lat_me < lat

    def unit(function, *arrays):
        shapes = jax.eval_shape(function, *arrays)
        blank = lambda *_: jax.tree.map(lambda a: jnp.zeros(a.shape, a.dtype), shapes)
        return lax.cond(inside, function, blank, *arrays)

    def spread(values):
        height = -(-values.shape[0] // (8 * lat)) * 8
        return wider(values, height * lat, values.shape[1])

    def gathered(part):
        return exchange_lat("gather", jnp.broadcast_to(part[None], (lat, *part.shape)))

    forward, inverse = dft_tables()

    def by_device(table):
        blocks = table.reshape(lon, points, Q).transpose(0, 2, 1)
        return np.einsum("zqk,ab->zqabk", blocks, np.eye(depth)).reshape(lon, Q * depth, n)

    analysis = jnp.asarray(by_device(forward), LOW)
    back_analysis = jnp.asarray(by_device(inverse.T), LOW)
    synthesis = jnp.asarray(by_device(inverse.T).transpose(0, 2, 1), LOW)
    back_synthesis = jnp.asarray(by_device(forward).transpose(0, 2, 1), LOW)

    legendre, quadrature = legendre_table()
    group = group_size(share, depth)
    groups = share // group
    places = np.arange(NLAT).reshape(lat, chunks, depth).transpose(1, 0, 2)
    spots = np.zeros((group, NLAT, chunks, lat, group, depth))
    for q in range(group):
        for c in range(chunks):
            for i in range(lat):
                spots[q, places[c, i], c, i, q, np.arange(depth)] = 1.0
    spots = spots.reshape(group, NLAT, group * NLAT)
    spots = (jnp.asarray(spots, LOW), jnp.asarray(spots.transpose(0, 2, 1), LOW))
    each = 2 if group % 2 == 0 else 1
    first = (lat_me * groups if each == 2 else 0 * lat_me).astype(jnp.int32).reshape(1)

    def own_degrees(table):
        table = jnp.asarray(table, LOW)
        if each == 2:
            return table
        own_q = (lat_me * share + jnp.arange(share, dtype=jnp.int32)) // 2
        return jnp.take(table, own_q, axis=0)

    plain = own_degrees(legendre)
    weighted = own_degrees(legendre * quadrature)
    plain_back = own_degrees(legendre.transpose(0, 2, 1))
    weighted_back = own_degrees((legendre * quadrature).transpose(0, 2, 1))

    date_selector = (
        member_dates[:, None] == jnp.arange(date_table.shape[0], dtype=jnp.int32)[None, :]
    ).astype(F32)
    offsets = jnp.dot(date_selector, date_table, precision=lax.Precision.HIGHEST)
    offset = wider(take(offsets, lon_me)[None], 1, width)
    gain_one = wider(norm_gains[:1], 1, width)
    gain_two = wider(norm_gains[1:], 1, width)
    response = wider(spectral_filter, L, width)
    fields = [pack(me, fields_in, c, depth, lon) for c in range(chunks)]
    upstreams = [None] * mids
    waiting = [(f"fields_{c}", fields, c) for c in range(chunks)]
    waiting += [(f"upstream_{c}", upstreams, c) for c in range(mids)]

    def send_next(after):
        if not waiting or waiting[0][1][waiting[0][2]] is None:
            return after
        name, packs, c = waiting.pop(0)
        after, slots = tie(after, packs[c])
        packs[c] = exchange_lon(name, slots, 1)
        return after

    fields[0] = exchange_lon("fields_0", fields[0], 1)
    del waiting[0]
    fields[0], fields[1:], offset, gain_one, gain_two, response = tie(
        fields[0], fields[1:], offset, gain_one, gain_two, response
    )

    spectra = []
    for c in range(chunks):

        def to_spectra(cotangent, *slots):
            rows_now = first_forward(me, analysis, slots, offset, gain_one, depth, points, channels)
            rows_now = exchange_lat(f"spectra_{c}", rows_now)
            return rows_now, [pack(me, a, c, depth * pair, lon) for a in cotangent]

        if c > 0:
            fields[c], spectra[c - 1] = tie(fields[c], spectra[c - 1])
        fields[c] = send_next(fields[c])
        rows_now, packed = unit(to_spectra, [cotangent] if c < mids else [], *fields[c])
        upstreams[c : c + 1] = packed if c < mids else upstreams[c : c + 1]
        spectra.append(rows_now)

    def to_coefficients(weight_in, weight_out, *spectra):
        *values, coefs = filter_forward(
            first,
            (weighted, plain_back),
            spots,
            response,
            spectra,
            [1] * chunks,
            [pair] * mids,
            lat,
            each,
            groups,
        )
        values[0] = exchange_lat("synthesis_0", values[0])
        return values, coefs, prepare_weights(weight_in, weight_out, width, hidden_width)

    spectra[-1] = send_next(spectra[-1])
    values, coefs, weights = unit(to_coefficients, weight_in, weight_out, *spectra)

    backs, grads, parts, outputs = [], [], [], []
    gain_parts = []
    for c in range(mids):

        def step(spectrum, slots, upstream, following, before):
            out = feed_forward(
                me,
                (synthesis, back_analysis),
                weights,
                offset,
                gain_two,
                spectrum,
                slots,
                upstream,
                lat,
                depth,
                points,
                channels,
            )
            following = [exchange_lat(f"synthesis_{c + 1}", a) for a in following]
            before = [exchange_lat(f"back_synthesis_{c - 1}", a) for a in before]
            return out, following, before

        out, values[c + 1 : c + 2], backs[c - 1 : c] = unit(
            step,
            values[c],
            fields[c * pair : (c + 1) * pair],
            upstreams[c],
            values[c + 1 : c + 2],
            backs[c - 1 : c],
        )
        outputs.append(exchange_lon(f"output_{c}", out[:lon], -1))
        grads.append(out[lon])
        parts.append(tuple(out[lon + 1 : lon + 5]))
        gain_parts.append(out[lon + 5])
        backs.append(out[lon + 6])

    def to_gradients(before, late, coefs, parts, gain_parts):
        late = exchange_lat(f"back_synthesis_{mids - 1}", late)
        weight_part = None
        for second, active, pre, cot in parts:
            terms = (
                jnp.einsum("gc,gh->ch", second, pre, preferred_element_type=F32),
                jnp.einsum("gc,gh->ch", cot, active, preferred_element_type=F32),
            )
            weight_part = terms if weight_part is None else tuple(map(jnp.add, weight_part, terms))
        *values, filter_part = filter_backward(
            first,
            (plain, weighted_back),
            spots,
            response,
            coefs,
            [*before, late],
            [pair] * mids,
            [1] * chunks,
            lat,
            each,
            groups,
        )
        gain_part = sum(jnp.sum(a, axis=0) for a in gain_parts)
        small = spread(jnp.concatenate([filter_part, gain_part[None]], axis=0))
        return values, small, weight_part

    outputs[:-1], backs[-1] = tie(outputs[:-1], backs[-1])
    values, small, weight_part = unit(
        to_gradients, backs[:-1], backs[-1], coefs, parts, gain_parts
    )
    outputs[-1], values[0] = tie(outputs[-1], values[0])
    values[0] = unit(lambda a: exchange_lat("back_spectra_0", a), values[0])

    gradients = []
    with jax.named_scope("weights_lat"):
        part = [
            lax.psum_scatter(a, "lat", scatter_dimension=0, tiled=True) for a in weight_part
        ]

    def sum_quarters(part):
        part = jnp.concatenate(part, axis=0)
        quarters = part.reshape(lon, -1, hidden_width)
        pieces = [take(quarters, (lon_me + s) % lon).astype(LOW) for s in range(lon)]
        return take(quarters, lon_me), exchange_lon("weights_sum", pieces, 1)[1:]

    def gather_quarters(own, pieces):
        own = (own + sum(piece.astype(F32) for piece in pieces)).astype(LOW)
        return exchange_lon("weights_gather", [own] * lon, 1)

    for c in range(chunks):
        if c == 2:
            gradients[0], part, values[2] = tie(gradients[0], part, values[2])
            quarters = sum_quarters(part)
        if c == 3:
            gradients[1], quarters, values[3] = tie(gradients[1], quarters, values[3])
            quarters = gather_quarters(*quarters)

        def to_input(spectrum, slots, grad, following, small):
            out = first_backward(
                me,
                back_synthesis,
                spectrum,
                slots,
                grad,
                c % pair,
                pair,
                offset,
                gain_one,
                depth,
                points,
                channels,
            )
            following = [exchange_lat(f"back_spectra_{c + 1}", a) for a in following]
            if c == chunks - 1:
                part = exchange_lat("small", small).reshape(lat, -1, width)
                small = jnp.sum(part, axis=0)
            return out, following, small

        following = values[c + 1 : c + 2] if c > 0 else []
        out, following, small = unit(
            to_input, values[c], fields[c], grads[c // pair], following, small
        )
        gradients.append(exchange_lon(f"input_grad_{c}", out, -1))
        if c > 0:
            values[c + 1 : c + 2] = following
        elif chunks > 1:
            values[1] = unit(lambda a: exchange_lat("back_spectra_1", a), values[1])

    if chunks < 4:
        quarters = gather_quarters(*sum_quarters(part))
    with jax.named_scope("small"):
        bit = 1
        while bit < lon:
            small = small + lax.ppermute(small, "lon", [(i, i ^ bit) for i in range(lon)])
            bit *= 2
    gradients[:-1], quarters, small = tie(gradients[:-1], quarters, small)
    small = unit(gathered, small)
    gradients[-1], small = tie(gradients[-1], small)

    block_output = input_grad = None
    for c in range(mids):
        block_output = unpack(me, outputs[c], block_output, c, depth * pair, fields_in.shape, LOW)
    for c in range(chunks):
        input_grad = unpack(me, gradients[c], input_grad, c, depth, fields_in.shape, F32)

    quarters = jnp.stack(quarters)
    part = jnp.concatenate([take(quarters, (lon_me - z) % lon) for z in range(lon)], axis=0)
    with jax.named_scope("weights_lat"):
        summed = lax.all_gather(part, "lat", axis=0, tiled=False).astype(F32)
    summed = summed.reshape(lat, 2, -1, hidden_width).swapaxes(0, 1).reshape(2, width, hidden_width)
    grad_weight_in = summed[0, :channels, :units]
    grad_weight_out = summed[1, :channels, :units].T
    grad_filter = small[:L, :channels]
    grad_one = jnp.sum(spectral_filter * grad_filter, axis=0) / norm_gains[0]
    grad_gains = jnp.stack([grad_one, small[L, :channels]])
    decay_rate = 1.0 - STEP ** (-0.8)
    new_weight_in, new_in_rows, new_in_columns = adafactor_matrix(
        weight_in, grad_weight_in, in_row_stats, in_column_stats, decay_rate
    )
    new_weight_out, new_out_rows, new_out_columns = adafactor_matrix(
        weight_out, grad_weight_out, out_row_stats, out_column_stats, decay_rate
    )
    new_filter, new_filter_rows, new_filter_columns = adafactor_matrix(
        spectral_filter, grad_filter, filter_row_stats, filter_column_stats, decay_rate
    )
    new_gains, new_moments = adafactor_vector(norm_gains, grad_gains, gain_moments, decay_rate)
    return (
        block_output,
        input_grad,
        grad_weight_in,
        grad_weight_out,
        grad_filter,
        grad_gains,
        new_weight_in,
        new_weight_out,
        new_filter,
        new_gains,
        new_in_rows,
        new_in_columns,
        new_out_rows,
        new_out_columns,
        new_filter_rows,
        new_filter_columns,
        new_moments,
    )


def solution(mesh):
    spread = P(None, "lat", "lon", None)
    return jax.shard_map(
        body,
        mesh=mesh,
        in_specs=(spread, spread) + (P(),) * 13,
        out_specs=(spread, spread) + (P(),) * 15,
        check_vma=False,
    )
```

```python
import math

import jax
import jax.numpy as jnp
import numpy as np
from jax import lax
from jax.experimental import pallas as pl
from jax.experimental.pallas import tpu as pltpu
from jax.sharding import PartitionSpec as P

NLAT = 128
NLON = 256
L = 128
M = 96
Q = 2 * M
STEP = 3
LANES = 128

NORM_EPS = 1e-06
FIRST_EPS = 1e-30
SECOND_EPS = 0.001
CLIP_LEVEL = 0.5
STEP_RATE = 0.5
F32 = jnp.float32
LOW = jnp.bfloat16
VMEM_LIMIT = 60 * 1024 * 1024


def legendre_table():
    angles = math.pi * (np.arange(NLAT) + 0.5) / NLAT
    cosine, sine = np.cos(angles), np.sin(angles)
    table = np.zeros((M, L, NLAT))
    for m in range(M):
        factors = np.arange(1, m + 1)
        scale = math.sqrt(0.5 * np.prod((2.0 * factors + 1.0) / (2.0 * factors)))
        table[m, m] = scale * sine**m
        for l in range(m + 1, L):
            a = math.sqrt((4.0 * l * l - 1.0) / (l * l - m * m))
            b = math.sqrt(((l - 1.0) ** 2 - m * m) / (4.0 * (l - 1.0) ** 2 - 1.0))
            earlier = table[m, l - 2] if l >= m + 2 else 0.0
            table[m, l] = a * (cosine * table[m, l - 1] - b * earlier)
    return table, math.pi / NLAT * sine


def dft_tables():
    phases = 2.0 * math.pi * (np.outer(np.arange(NLON), np.arange(M)) % NLON) / NLON
    cosine, sine = np.cos(phases), np.sin(phases)
    doubling = np.where(np.arange(M) == 0, 1.0, 2.0)
    forward = np.stack([cosine, -sine], axis=2).reshape(NLON, Q) / NLON
    inverse = np.stack([doubling * cosine, -doubling * sine], axis=2).reshape(NLON, Q).T
    return forward, inverse


EXTRA = 16


def point_masks(n, points):
    row_of = lax.broadcasted_iota(jnp.int32, (n, EXTRA), 0) // points
    sel = (row_of == lax.broadcasted_iota(jnp.int32, (n, EXTRA), 1)).astype(F32).astype(LOW)
    place = lax.broadcasted_iota(jnp.int32, (n, LANES), 0) % points
    lane = lax.broadcasted_iota(jnp.int32, (n, LANES), 1)
    return sel, place == lane, lane == 0


def load_points(ref, n, points):
    tiles = ref.shape[0] // n
    sel, diagonal, first = point_masks(n, points)
    extra = jnp.dot(sel, ref[tiles * n : tiles * n + EXTRA, :], preferred_element_type=F32)
    column = jnp.sum(jnp.where(diagonal, extra, 0.0), axis=1, keepdims=True)
    pieces = [ref[t * n : (t + 1) * n, :].astype(F32) for t in range(tiles)]
    return jnp.concatenate([*pieces, jnp.where(first, column, 0.0)], axis=1)


def store_points(ref, values, last, points):
    n = values.shape[0]
    tiles = ref.shape[0] // n
    _, diagonal, _ = point_masks(n, points)
    for t in range(tiles):
        ref[t * n : (t + 1) * n, :] = values[:, t * LANES : (t + 1) * LANES]
    spread = jnp.where(diagonal, last, 0.0).astype(LOW)
    row_of = lax.broadcasted_iota(jnp.int32, (EXTRA, n), 1) // points
    pick = (row_of == lax.broadcasted_iota(jnp.int32, (EXTRA, n), 0)).astype(F32).astype(LOW)
    ref[tiles * n : tiles * n + EXTRA, :] = jnp.dot(
        pick, spread, preferred_element_type=F32
    ).astype(LOW)


def params():
    return pltpu.CompilerParams(vmem_limit_bytes=VMEM_LIMIT)


def cost(flops, size, transcendentals=0):
    return pl.CostEstimate(flops=1024, bytes_accessed=400_000_000, transcendentals=0)


def fixed(array):
    zeros = (0,) * len(array.shape)
    return pl.BlockSpec(array.shape, lambda *_: zeros)


def once(array):
    zeros = (0,) * len(array.shape)
    return pl.BlockSpec(array.shape, lambda *_: zeros, pipeline_mode=pl.Buffered(1))


def slot_table(table, count):
    return pl.BlockSpec(
        (1, *table.shape[1:]), lambda s, me_ref: ((me_ref[0] + (count - s)) % count, 0, 0)
    )


def pack(me, source, chunk, depth, count):
    _, _, points, channels = source.shape
    n = depth * points
    tiles = channels // LANES

    def kernel(me_ref, source_ref, *outs):
        step = pl.program_id(0)
        values = source_ref[0].reshape(n, channels)
        last = values[:, tiles * LANES :].astype(F32)
        for s, out in enumerate(outs):

            @pl.when(step == s)
            def _():
                store_points(out, values, last, points)

    shape = jax.ShapeDtypeStruct((tiles * n + EXTRA, LANES), LOW)
    return pl.pallas_call(
        kernel,
        out_shape=[shape] * count,
        grid_spec=pltpu.PrefetchScalarGridSpec(
            num_scalar_prefetch=1,
            grid=(count,),
            in_specs=[
                pl.BlockSpec(
                    (1, depth, points, channels),
                    lambda s, me_ref: ((me_ref[0] + s) % count, chunk, 0, 0),
                )
            ],
            out_specs=[fixed(shape)] * count,
        ),
        compiler_params=params(),
        cost_estimate=cost(0, 4 * count * n * channels),
        name="pack",
    )(me, source)


def unpack(me, slots, target, chunk, depth, shape, dtype):
    members, rows, points, channels = shape
    n = depth * points
    count = len(slots)

    def kernel(me_ref, *refs):
        out = refs[-1]
        step = pl.program_id(0)
        for s in range(count):

            @pl.when(step == s)
            def _():
                values = load_points(refs[s], n, points)[:, :channels]
                out[0] = values.astype(dtype).reshape(depth, points, channels)

    specs = [fixed(s) for s in slots]
    arrays = list(slots)
    aliases = {}
    if target is not None:
        specs.append(pl.BlockSpec(memory_space=pl.ANY))
        arrays.append(target)
        aliases = {count + 1: 0}
    return pl.pallas_call(
        kernel,
        out_shape=jax.ShapeDtypeStruct(shape, dtype),
        grid_spec=pltpu.PrefetchScalarGridSpec(
            num_scalar_prefetch=1,
            grid=(count,),
            in_specs=specs,
            out_specs=pl.BlockSpec(
                (1, depth, points, channels),
                lambda s, me_ref: ((me_ref[0] + s) % count, chunk, 0, 0),
            ),
        ),
        input_output_aliases=aliases,
        compiler_params=params(),
        cost_estimate=cost(0, 6 * count * n * channels),
        name="unpack",
    )(me, *arrays)


def first_forward(me, table, slots, offset, gain, depth, points, channels):
    n = depth * points
    count = len(slots)

    def kernel(me_ref, table_ref, offset_ref, gain_ref, *refs):
        out, total = refs[-2:]
        for s, slot in enumerate(refs[:-2]):
            shifted = load_points(slot, n, points) + offset_ref[...]
            square = jnp.sum(shifted * shifted, axis=1, keepdims=True)
            scale = lax.rsqrt(square * (1.0 / channels) + NORM_EPS)
            normed = (shifted * scale * gain_ref[...]).astype(LOW)
            owner = (me_ref[0] + (count - s)) % count
            part = jnp.dot(table_ref[owner], normed, preferred_element_type=F32)
            if s == 0:
                total[...] = part
            else:
                total[...] += part
        out[...] = total[...].astype(LOW)

    width = gain.shape[1]
    size = table.shape[1]
    arrays = [table, offset, gain, *slots]
    shape = jax.ShapeDtypeStruct((size, width), LOW)
    return pl.pallas_call(
        kernel,
        out_shape=shape,
        grid_spec=pltpu.PrefetchScalarGridSpec(
            num_scalar_prefetch=1,
            grid=(1,),
            in_specs=[fixed(a) for a in arrays],
            out_specs=fixed(shape),
            scratch_shapes=[pltpu.VMEM((size, width), F32)],
        ),
        compiler_params=params(),
        cost_estimate=cost(2 * size * count * n * width, 6 * 1024 * 1024),
        name="first_forward",
    )(me, *arrays)


def degree_blocks(refs, counts, lat, step, groups):
    for ref, count in zip(refs, counts):
        size = ref.shape[0]
        if groups == 1 and count == 1:
            yield ref, slice(0, size)
            continue
        part = size // lat // count // groups
        for c in range(count):
            for i in range(lat):
                start = (i * count + c) * (part * groups) + step * part
                yield ref, pl.ds(pl.multiple_of(start, part), part)


def degree_tables(to_ref, back_ref, spots_ref, spots_back_ref, each):
    group = spots_ref.shape[0]
    to = [
        jnp.dot(to_ref[q // each], spots_ref[q], preferred_element_type=F32).astype(LOW)
        for q in range(group)
    ]
    back = [
        jnp.dot(spots_back_ref[q], back_ref[q // each], preferred_element_type=F32).astype(LOW)
        for q in range(group)
    ]
    return jnp.concatenate(to, axis=0), jnp.concatenate(back, axis=1)


def filter_call(kernel, name, first, tables, spots, response, extra, spectra, each, groups, outs):
    part = tables[0].shape[0]
    block = spots[0].shape[0] // each
    tabled = pl.BlockSpec((block, L, NLAT), lambda g, first: (first[0] + g, 0, 0))
    grouped = lambda a: pl.BlockSpec((1, *a.shape[1:]), lambda g, first: (g, 0, 0))
    spec = lambda a: grouped(a) if len(a.shape) == 3 else fixed(a)
    arrays = [*tables, *spots, response, *extra, *spectra]
    return pl.pallas_call(
        kernel,
        out_shape=outs,
        grid_spec=pltpu.PrefetchScalarGridSpec(
            num_scalar_prefetch=1,
            grid=(groups,),
            in_specs=[tabled, tabled, fixed(spots[0]), fixed(spots[1]), fixed(response)]
            + [spec(a) for a in (*extra, *spectra)],
            out_specs=[spec(o) for o in outs],
        ),
        compiler_params=params(),
        cost_estimate=cost(16 * part, 24 * 1024 * 1024),
        name=name,
    )(first, *arrays)


def filter_forward(
    first, tables, spots, response, spectra, counts, out_counts, lat, each, groups
):
    size = spots[0].shape[2]
    width = response.shape[1]
    count = len(spectra)

    def kernel(first_ref, to_ref, back_ref, spots_ref, spots_back_ref, response_ref, *refs):
        step = pl.program_id(0)
        ins, outs, coefs = refs[:count], refs[count:-1], refs[-1]
        to, back = degree_tables(to_ref, back_ref, spots_ref, spots_back_ref, each)
        values = jnp.concatenate(
            [ref[rows, :] for ref, rows in degree_blocks(ins, counts, lat, step, groups)], axis=0
        )
        coef = jnp.dot(to, values, preferred_element_type=F32)
        coefs[0] = coef
        scale = jnp.concatenate([response_ref[...]] * (size // L), axis=0)
        filtered = (scale * coef).astype(LOW)
        result = jnp.dot(back, filtered, preferred_element_type=F32).astype(LOW)
        begin = 0
        for ref, rows in degree_blocks(outs, out_counts, lat, step, groups):
            length = rows.stop if isinstance(rows, slice) else rows.size
            ref[rows, :] = result[begin : begin + length]
            begin += length

    height = sum(s.shape[0] for s in spectra) // sum(counts)
    outs = [jax.ShapeDtypeStruct((height * c, width), LOW) for c in out_counts]
    outs.append(jax.ShapeDtypeStruct((groups, size, width), F32))
    return filter_call(
        kernel, "filter_forward", first, tables, spots, response, (), spectra, each, groups, outs
    )


def filter_backward(
    first, tables, spots, response, coefs, spectra, counts, out_counts, lat, each, groups
):
    size = spots[0].shape[2]
    width = response.shape[1]
    count = len(spectra)

    def kernel(
        first_ref, to_ref, back_ref, spots_ref, spots_back_ref, response_ref, coefs_ref, *refs
    ):
        step = pl.program_id(0)
        ins, outs, grad_ref = refs[:count], refs[count:-1], refs[-1]
        to, back = degree_tables(to_ref, back_ref, spots_ref, spots_back_ref, each)
        values = jnp.concatenate(
            [ref[rows, :] for ref, rows in degree_blocks(ins, counts, lat, step, groups)], axis=0
        )
        upstream = jnp.dot(to, values, preferred_element_type=F32)
        product = coefs_ref[0] * upstream
        grad = product[:L]
        for q in range(1, size // L):
            grad = grad + product[q * L : (q + 1) * L]

        @pl.when(step == 0)
        def _():
            grad_ref[...] = jnp.zeros_like(grad_ref)

        grad_ref[...] += grad
        scale = jnp.concatenate([response_ref[...]] * (size // L), axis=0)
        filtered = (scale * upstream).astype(LOW)
        result = jnp.dot(back, filtered, preferred_element_type=F32).astype(LOW)
        begin = 0
        for ref, rows in degree_blocks(outs, out_counts, lat, step, groups):
            length = rows.stop if isinstance(rows, slice) else rows.size
            ref[rows, :] = result[begin : begin + length]
            begin += length

    height = sum(s.shape[0] for s in spectra) // sum(counts)
    outs = [jax.ShapeDtypeStruct((height * c, width), LOW) for c in out_counts]
    outs.append(jax.ShapeDtypeStruct((L, width), F32))
    return filter_call(
        kernel,
        "filter_backward",
        first,
        tables,
        spots,
        response,
        (coefs,),
        spectra,
        each,
        groups,
        outs,
    )


def prepare_weights(weight_in, weight_out, width, hidden_width):
    channels, units = weight_in.shape

    def kernel(in_ref, out_ref, w_in, w_out, w_in_t, w_out_t):
        w_in[...] = jnp.zeros_like(w_in)
        w_out_t[...] = jnp.zeros_like(w_out_t)
        w_in[:channels, :units] = in_ref[...].astype(LOW)
        w_out_t[:channels, :units] = out_ref[...].astype(LOW)
        w_in_t[...] = w_in[...].T
        w_out[...] = w_out_t[...].T

    outs = [
        jax.ShapeDtypeStruct(shape, LOW)
        for shape in [(width, hidden_width), (hidden_width, width)] * 2
    ]
    outs = [outs[0], outs[1], outs[1], outs[0]]
    return pl.pallas_call(
        kernel, out_shape=outs, compiler_params=params(), name="prepare_weights"
    )(weight_in, weight_out.T)


def feed_forward(
    me, tables, weights, offset, gain, spectra, slots, upstreams, lat, depth, points, channels, split
):
    n = depth * points
    pair, count = len(slots), len(slots[0])
    flat = [slot for chunk in slots for slot in chunk]
    width, hidden_width = weights[0].shape
    size = spectra.shape[0] // pair
    part = size // lat
    inverse_channels = 1.0 / channels

    def kernel(
        me_ref, out_table, back_table, w_in, w_out, w_in_t, w_out_t, offset_ref, gain_ref, y, *refs
    ):
        ins, ups = refs[: pair * count], refs[pair * count : (pair + 1) * count]
        refs = refs[(pair + 1) * count :]
        outs = refs[: split * count]
        refs = refs[split * count :]
        grad_ref, second_ref, active_ref, pre_ref, cot_ref, gain_part, back_ref = refs[:-4]
        x_now, up_now, y_now, total = refs[-4:]
        step = pl.program_id(0)

        @pl.when(step == 0)
        def _():
            gain_part[...] = jnp.zeros_like(gain_part)
            total[...] = jnp.zeros_like(total)
            for c in range(pair):
                for i in range(lat):
                    y_now[c, i * part : (i + 1) * part] = y[
                        (i * pair + c) * part : (i * pair + c + 1) * part
                    ]

        for s in range(count):

            @pl.when(step == s)
            def _():
                for c in range(pair):
                    x_now[c] = ins[c * count + s][...]
                up_now[...] = ups[s][...]

        rows = lambda parts: jnp.concatenate(parts, axis=0) if pair > 1 else parts[0]
        branch = rows(
            [
                jnp.dot(out_table[0], y_now[c], preferred_element_type=F32).astype(LOW)
                for c in range(pair)
            ]
        )
        shifted = rows([load_points(x_now.at[c], n, points) for c in range(pair)])
        hidden = shifted + offset_ref[...] + branch.astype(F32)
        square = jnp.sum(hidden * hidden, axis=1, keepdims=True)
        scale = lax.rsqrt(square * inverse_channels + NORM_EPS)
        second = (hidden * scale * gain_ref[...]).astype(LOW)
        second_ref[...] = second
        upstream = load_points(up_now, pair * n, points)
        upstream_low = upstream.astype(LOW)
        cot_ref[...] = upstream_low
        preact = jnp.dot(second, w_in[...], preferred_element_type=F32)
        back_active = jnp.dot(upstream_low, w_out_t[...], preferred_element_type=F32)
        share = 0.5 + 0.5 * lax.erf(preact * math.sqrt(0.5))
        density = jnp.exp(-0.5 * preact * preact) * (1.0 / math.sqrt(2.0 * math.pi))
        active = (preact * share).astype(LOW)
        active_ref[...] = active
        back_preact = (back_active * (share + preact * density)).astype(LOW)
        pre_ref[...] = back_preact
        output = hidden + jnp.dot(active, w_out[...], preferred_element_type=F32)
        back_second = jnp.dot(back_preact, w_in_t[...], preferred_element_type=F32)
        scaled = back_second * gain_ref[...]
        inner = jnp.sum(hidden * scaled, axis=1, keepdims=True) * inverse_channels
        grad = scale * scaled - hidden * (scale * scale * scale * inner) + upstream
        grad_ref[...] = grad
        grad_low = grad.astype(LOW)
        for c in range(pair):
            total[c] += jnp.dot(
                back_table[0], grad_low[c * n : (c + 1) * n], preferred_element_type=F32
            )
        gain_part[...] += jnp.sum(
            (back_second * (hidden * scale)).reshape(pair * n // 8, 8, width), axis=0
        )

        @pl.when(step == count - 1)
        def _():
            for c in range(pair):
                for i in range(lat):
                    back_ref[(i * pair + c) * part : (i * pair + c + 1) * part] = total[
                        c, i * part : (i + 1) * part
                    ].astype(LOW)

        m = pair * n // split
        leaving = [x_now.at[c] for c in range(pair)] if split > 1 else [up_now]
        for c in range(split):
            block = output[c * m : (c + 1) * m]
            store_points(leaving[c], block.astype(LOW), block[:, channels - 1 : channels], points)
        for s in range(count):

            @pl.when(step == s)
            def _():
                for c in range(split):
                    outs[c * count + s][...] = leaving[c][...]

    rows = lambda w: pl.BlockSpec((pair * n, w), lambda s, me_ref: (s, 0))
    slot = jax.ShapeDtypeStruct((flat if split > 1 else upstreams)[0].shape, LOW)
    height = count * pair * n
    outs = [slot] * (split * count) + [
        jax.ShapeDtypeStruct((height, width), F32),
        jax.ShapeDtypeStruct((height, width), LOW),
        jax.ShapeDtypeStruct((height, hidden_width), LOW),
        jax.ShapeDtypeStruct((height, hidden_width), LOW),
        jax.ShapeDtypeStruct((height, width), LOW),
        jax.ShapeDtypeStruct((8, width), F32),
        jax.ShapeDtypeStruct(spectra.shape, LOW),
    ]
    out_specs = [fixed(slot)] * (split * count) + [
        rows(width),
        rows(width),
        rows(hidden_width),
        rows(hidden_width),
        rows(width),
        fixed(outs[-2]),
        fixed(outs[-1]),
    ]
    arrays = [*tables, *weights, offset, gain, spectra, *flat, *upstreams]
    return pl.pallas_call(
        kernel,
        out_shape=outs,
        grid_spec=pltpu.PrefetchScalarGridSpec(
            num_scalar_prefetch=1,
            grid=(count,),
            in_specs=[slot_table(t, count) for t in tables] + [once(a) for a in arrays[2:]],
            out_specs=out_specs,
            scratch_shapes=[
                pltpu.VMEM((pair, *flat[0].shape), LOW),
                pltpu.VMEM(upstreams[0].shape, LOW),
                pltpu.VMEM((pair, size, width), LOW),
                pltpu.VMEM((pair, size, width), F32),
            ],
        ),
        compiler_params=params(),
        cost_estimate=cost(0, 0),
        name="feed_forward",
    )(me, *arrays)


def weight_sums(parts, block=512):
    count = len(parts)
    height, width = parts[0][0].shape
    hidden_width = parts[0][1].shape[1]
    block = min(block, height)
    steps = height // block

    def kernel(*refs):
        ins, out = refs[:-1], refs[-1]
        step = pl.program_id(0)

        @pl.when(step == 0)
        def _():
            out[...] = jnp.zeros_like(out)

        def add(row, left, right):
            out[row : row + width, :] += lax.dot_general(
                left[...], right[...], (((0,), (0,)), ((), ())), preferred_element_type=F32
            )

        for m in range(count):

            @pl.when((step >= m * steps) & (step < (m + 1) * steps))
            def _():
                second, active, pre, cot = ins[4 * m : 4 * m + 4]
                add(0, second, pre)
                add(width, cot, active)

    def spec(array, m):
        return pl.BlockSpec(
            (block, array.shape[1]),
            lambda k: (jnp.clip(k - m * steps, 0, steps - 1), 0),
        )

    shape = jax.ShapeDtypeStruct((2 * width, hidden_width), F32)
    return pl.pallas_call(
        kernel,
        out_shape=shape,
        grid=(count * steps,),
        in_specs=[spec(a, m) for m, part in enumerate(parts) for a in part],
        out_specs=fixed(shape),
        compiler_params=params(),
        cost_estimate=cost(0, 0),
        name="weight_sums",
    )(*[a for part in parts for a in part])


def first_backward(
    me, table, spectra, slots, grads, place, pair, offset, gain, depth, points, channels
):
    n = depth * points
    count = len(slots)
    width = gain.shape[1]
    inverse_channels = 1.0 / channels

    def kernel(me_ref, table_ref, y, grad_ref, offset_ref, gain_ref, *refs):
        ins, outs, now = refs[:count], refs[count:-1], refs[-1]
        step = pl.program_id(0)
        for s in range(count):

            @pl.when(step == s)
            def _():
                now[...] = ins[s][...]

        back = jnp.dot(table_ref[0], y[...], preferred_element_type=F32).astype(LOW).astype(F32)
        shifted = load_points(now, n, points) + offset_ref[...]
        square = jnp.sum(shifted * shifted, axis=1, keepdims=True)
        scale = lax.rsqrt(square * inverse_channels + NORM_EPS)
        scaled = back * gain_ref[...]
        inner = jnp.sum(shifted * scaled, axis=1, keepdims=True) * inverse_channels
        result = grad_ref[...] + scale * scaled - shifted * (scale * scale * scale * inner)
        store_points(now, result.astype(LOW), result[:, channels - 1 : channels], points)
        for s in range(count):

            @pl.when(step == s)
            def _():
                outs[s][...] = now[...]

    slot = jax.ShapeDtypeStruct(slots[0].shape, LOW)
    outs = [slot] * count
    return pl.pallas_call(
        kernel,
        out_shape=outs,
        grid_spec=pltpu.PrefetchScalarGridSpec(
            num_scalar_prefetch=1,
            grid=(count,),
            in_specs=[
                slot_table(table, count),
                fixed(spectra),
                pl.BlockSpec((n, width), lambda s, me_ref: (s * pair + place, 0)),
                fixed(offset),
                fixed(gain),
            ]
            + [fixed(s) for s in slots],
            out_specs=[fixed(o) for o in outs],
            scratch_shapes=[pltpu.VMEM(slot.shape, LOW)],
        ),
        compiler_params=params(),
        cost_estimate=cost(2 * count * n * width * spectra.shape[0], 12 * 1024 * 1024),
        name="first_backward",
    )(me, table, spectra, grads, offset, gain, *slots)


def adafactor_matrix(weight_now, gradient, rows_old, columns_old, decay_rate):
    squares = gradient * gradient + FIRST_EPS
    rows_new = decay_rate * rows_old + (1.0 - decay_rate) * jnp.mean(squares, axis=1)
    columns_new = decay_rate * columns_old + (1.0 - decay_rate) * jnp.mean(squares, axis=0)
    estimate = rows_new[:, None] * columns_new[None, :] / jnp.mean(rows_new)
    update = gradient * lax.rsqrt(estimate)
    update = update / jnp.maximum(1.0, jnp.sqrt(jnp.mean(update * update)) / CLIP_LEVEL)
    scale_now = STEP_RATE * jnp.maximum(SECOND_EPS, jnp.sqrt(jnp.mean(weight_now * weight_now)))
    return (weight_now - scale_now * update, rows_new, columns_new)


def adafactor_call(gradients, place, weight_now, rows_old, columns_old, by_rows, decay_rate):
    height, width = weight_now.shape

    def kernel(grad_ref, weight_ref, rows_ref, columns_ref, grad_out, new, rows_out, columns_out):
        gradient = grad_ref[:height, :width].astype(F32)
        grad_out[...] = gradient
        squares = gradient * gradient + FIRST_EPS
        rows_mean = jnp.sum(squares, axis=1, keepdims=True) * (1.0 / width)
        columns_mean = jnp.sum(squares, axis=0, keepdims=True) * (1.0 / height)
        rows_new = decay_rate * rows_ref[...] + (1.0 - decay_rate) * rows_mean
        columns_new = decay_rate * columns_ref[...] + (1.0 - decay_rate) * columns_mean
        rows_out[...] = rows_new
        columns_out[...] = columns_new
        mean = jnp.mean(rows_new) if by_rows else jnp.mean(columns_new)
        update = gradient * (lax.rsqrt(rows_new / mean) * lax.rsqrt(columns_new))
        weight = weight_ref[...]
        size = 1.0 / (height * width)
        clip = jnp.maximum(1.0, jnp.sqrt(jnp.sum(update * update) * size) / CLIP_LEVEL)
        rate = STEP_RATE * jnp.maximum(SECOND_EPS, jnp.sqrt(jnp.sum(weight * weight) * size))
        new[...] = weight - update * (rate / clip)

    whole = lambda a: pl.BlockSpec(a.shape, lambda i: (0, 0))
    tall, wide = gradients.shape
    matrix = jax.ShapeDtypeStruct((height, width), F32)
    outs = [matrix, matrix]
    outs += [jax.ShapeDtypeStruct((height, 1), F32), jax.ShapeDtypeStruct((1, width), F32)]
    arrays = [weight_now, rows_old[:, None], columns_old[None]]
    return pl.pallas_call(
        kernel,
        out_shape=outs,
        grid=(1,),
        in_specs=[pl.BlockSpec((tall // 2, wide), lambda i: (place, 0))]
        + [whole(a) for a in arrays],
        out_specs=[whole(o) for o in outs],
        compiler_params=params(),
        cost_estimate=cost(0, 0),
        name="adafactor",
    )(gradients, *arrays)


def adafactor_vector(weight_now, gradient, moments_old, decay_rate):
    moments_new = decay_rate * moments_old + (1.0 - decay_rate) * (gradient * gradient + FIRST_EPS)
    update = gradient * lax.rsqrt(moments_new)
    update = update / jnp.maximum(
        1.0, jnp.sqrt(jnp.mean(update * update, axis=1, keepdims=True)) / CLIP_LEVEL
    )
    scale_now = STEP_RATE * jnp.maximum(
        SECOND_EPS, jnp.sqrt(jnp.mean(weight_now * weight_now, axis=1, keepdims=True))
    )
    return (weight_now - scale_now * update, moments_new)


def tie(*groups):
    return lax.optimization_barrier(groups)


def take(array, index):
    return lax.dynamic_index_in_dim(array, index, 0, keepdims=False)


def chunk_rows(rows):
    return rows // 4 if rows % 4 == 0 else rows


def group_size(share, depth):
    for size in range(1, share):
        if share % size == 0 and size * depth % 16 == 0:
            return size
    return share


def body(
    fields_in,
    cotangent,
    member_dates,
    date_table,
    norm_gains,
    spectral_filter,
    weight_in,
    weight_out,
    gain_moments,
    in_row_stats,
    in_column_stats,
    out_row_stats,
    out_column_stats,
    filter_row_stats,
    filter_column_stats,
):
    members, rows, points, channels = fields_in.shape
    units = weight_in.shape[1]
    width = -(-channels // LANES) * LANES
    hidden_width = -(-units // LANES) * LANES
    lat, lon = lax.axis_size("lat"), lax.axis_size("lon")
    lat_me, lon_me = lax.axis_index("lat"), lax.axis_index("lon")
    me = lon_me.astype(jnp.int32).reshape(1)
    share = Q // lat
    depth = chunk_rows(rows)
    chunks = rows // depth
    pair = 2 if chunks % 2 == 0 else 1
    mids = chunks // pair
    n = depth * points

    def wider(array, *sizes):
        return jnp.pad(array, [(0, s - d) for s, d in zip(sizes, array.shape)])

    def exchange_lon(name, slots, sign):
        with jax.named_scope(name):
            return [
                slot
                if s == 0
                else lax.ppermute(slot, "lon", [(i, (i + sign * s) % lon) for i in range(lon)])
                for s, slot in enumerate(slots)
            ]

    def exchange_lat(name, *spectra):
        blocks = [a.reshape(lat, -1, width) for a in spectra]
        blocks = jnp.concatenate(blocks, axis=1) if len(blocks) > 1 else blocks[0]
        with jax.named_scope(name):
            blocks = lax.all_to_all(blocks, "lat", split_axis=0, concat_axis=0, tiled=True)
        return blocks.reshape(-1, width)

    inside = lat_me < lat

    order = [norm_gains[:1, :LANES]]

    def unit(function, *arrays):
        run = lambda token, *arrays: tie(token, function(*arrays))
        shapes = jax.eval_shape(run, order[0], *arrays)
        blank = lambda *_: jax.tree.map(lambda a: jnp.zeros(a.shape, a.dtype), shapes)
        order[0], out = lax.cond(inside, run, blank, order[0], *arrays)
        return out

    def spread(values):
        height = -(-values.shape[0] // (8 * lat)) * 8
        return wider(values, height * lat, values.shape[1])

    def gathered(part):
        return exchange_lat("gather", jnp.broadcast_to(part[None], (lat, *part.shape)))

    forward, inverse = dft_tables()

    def by_device(table):
        blocks = table.reshape(lon, points, Q).transpose(0, 2, 1)
        return np.einsum("zqk,ab->zqabk", blocks, np.eye(depth)).reshape(lon, Q * depth, n)

    analysis = jnp.asarray(by_device(forward), LOW)
    back_analysis = jnp.asarray(by_device(inverse.T), LOW)
    synthesis = jnp.asarray(by_device(inverse.T).transpose(0, 2, 1), LOW)
    back_synthesis = jnp.asarray(by_device(forward).transpose(0, 2, 1), LOW)

    legendre, quadrature = legendre_table()
    group = group_size(share, depth)
    groups = share // group
    places = np.arange(NLAT).reshape(lat, chunks, depth).transpose(1, 0, 2)
    spots = np.zeros((group, NLAT, chunks, lat, group, depth))
    for q in range(group):
        for c in range(chunks):
            for i in range(lat):
                spots[q, places[c, i], c, i, q, np.arange(depth)] = 1.0
    spots = spots.reshape(group, NLAT, group * NLAT)
    spots = (jnp.asarray(spots, LOW), jnp.asarray(spots.transpose(0, 2, 1), LOW))
    each = 2 if group % 2 == 0 else 1
    first = (lat_me * groups if each == 2 else 0 * lat_me).astype(jnp.int32).reshape(1)

    def own_degrees(table):
        table = jnp.asarray(table, LOW)
        if each == 2:
            return table
        own_q = (lat_me * share + jnp.arange(share, dtype=jnp.int32)) // 2
        return jnp.take(table, own_q, axis=0)

    plain = own_degrees(legendre)
    weighted = own_degrees(legendre * quadrature)
    plain_back = own_degrees(legendre.transpose(0, 2, 1))
    weighted_back = own_degrees((legendre * quadrature).transpose(0, 2, 1))

    date_selector = (
        member_dates[:, None] == jnp.arange(date_table.shape[0], dtype=jnp.int32)[None, :]
    ).astype(F32)
    offsets = jnp.dot(date_selector, date_table, precision=lax.Precision.HIGHEST)
    offset = wider(take(offsets, lon_me)[None], 1, width)
    gain_one = wider(norm_gains[:1], 1, width)
    gain_two = wider(norm_gains[1:], 1, width)
    response = wider(spectral_filter, L, width)
    fields = [pack(me, fields_in, c, depth, lon) for c in range(chunks)]
    upstreams = [None] * mids
    waiting = [(f"fields_{c}", fields, c) for c in range(chunks)]
    waiting += [(f"upstream_{c}", upstreams, c) for c in range(mids)]

    def send_next(after):
        if not waiting or waiting[0][1][waiting[0][2]] is None:
            return after
        name, packs, c = waiting.pop(0)
        after, slots = tie(after, packs[c])
        packs[c] = exchange_lon(name, slots, 1)
        return after

    fields[0] = exchange_lon("fields_0", fields[0], 1)
    del waiting[0]
    fields[0], fields[1:], offset, gain_one, gain_two, response = tie(
        fields[0], fields[1:], offset, gain_one, gain_two, response
    )

    spectra = []
    for c in range(chunks):

        def to_spectra(cotangent, *slots):
            rows_now = first_forward(me, analysis, slots, offset, gain_one, depth, points, channels)
            rows_now = exchange_lat(f"spectra_{c}", rows_now)
            return rows_now, [pack(me, a, c, depth * pair, lon) for a in cotangent]

        if c > 0:
            fields[c], spectra[c - 1] = tie(fields[c], spectra[c - 1])
        fields[c] = send_next(fields[c])
        rows_now, packed = unit(to_spectra, [cotangent] if c < mids else [], *fields[c])
        upstreams[c : c + 1] = packed if c < mids else upstreams[c : c + 1]
        spectra.append(rows_now)

    def to_coefficients(weight_in, weight_out, *spectra):
        *values, coefs = filter_forward(
            first,
            (weighted, plain_back),
            spots,
            response,
            spectra,
            [1] * chunks,
            [pair] * mids,
            lat,
            each,
            groups,
        )
        values[0] = exchange_lat("synthesis_0", values[0])
        return values, coefs, prepare_weights(weight_in, weight_out, width, hidden_width)

    spectra[-1] = send_next(spectra[-1])
    values, coefs, weights = unit(to_coefficients, weight_in, weight_out, *spectra)

    splits = [1] * (mids - 1) + [pair]
    backs, grads, parts, outputs = [], [], [], []
    gain_parts = []
    for c in range(mids):

        def step(spectrum, slots, upstream, following, before):
            out = feed_forward(
                me,
                (synthesis, back_analysis),
                weights,
                offset,
                gain_two,
                spectrum,
                slots,
                upstream,
                lat,
                depth,
                points,
                channels,
                splits[c],
            )
            following = [exchange_lat(f"synthesis_{c + 1}", a) for a in following]
            before = [exchange_lat(f"back_synthesis_{c - 1}", a) for a in before]
            return out, following, before

        out, values[c + 1 : c + 2], backs[c - 1 : c] = unit(
            step,
            values[c],
            fields[c * pair : (c + 1) * pair],
            upstreams[c],
            values[c + 1 : c + 2],
            backs[c - 1 : c],
        )
        for p in range(splits[c]):
            leaving = out[p * lon : (p + 1) * lon]
            outputs.append(exchange_lon(f"output_{c}_{p}", leaving, -1))
        grad, *part, gain_part, back = out[splits[c] * lon :]
        grads.append(grad)
        parts.append(part)
        gain_parts.append(gain_part)
        backs.append(back)

    def to_weights(late, parts):
        return exchange_lat(f"back_synthesis_{mids - 1}", late), weight_sums(parts)

    def to_gradients(backs, coefs, gain_parts):
        *values, filter_part = filter_backward(
            first,
            (plain, weighted_back),
            spots,
            response,
            coefs,
            backs,
            [pair] * mids,
            [1] * chunks,
            lat,
            each,
            groups,
        )
        gain_part = sum(jnp.sum(a, axis=0) for a in gain_parts)
        return values, spread(jnp.concatenate([filter_part, gain_part[None]], axis=0))

    early = mids - 1
    outputs[:early], backs[-1] = tie(outputs[:early], backs[-1])
    backs[-1], weight_part = unit(to_weights, backs[-1], parts)
    outputs[early:-1], backs[-1], weight_part = tie(outputs[early:-1], backs[-1], weight_part)
    values, small = unit(to_gradients, backs, coefs, gain_parts)

    gradients = []
    with jax.named_scope("weights_lat"):
        part = lax.psum_scatter(weight_part, "lat", scatter_dimension=0, tiled=True)

    for c in range(chunks):
        if c == min(1, chunks - 1):
            outputs[-1], order[0] = tie(outputs[-1], order[0])
        if c == min(2, chunks - 1):
            part, order[0] = tie(part, order[0])
            with jax.named_scope("weights_lon"):
                part = lax.psum(part.astype(LOW), "lon")
        if c >= 2:
            gradients[c - 2], order[0] = tie(gradients[c - 2], order[0])

        def to_input(spectrum, slots, grad, outputs):
            block_output, row = None, 0
            for arrived in outputs:
                tall = depth * pair if arrived[0].shape[0] > slots[0].shape[0] else depth
                block_output = unpack(
                    me, arrived, block_output, row // tall, tall, fields_in.shape, LOW
                )
                row += tall
            out = first_backward(
                me,
                back_synthesis,
                exchange_lat(f"back_spectra_{c}", spectrum),
                slots,
                grad,
                c % pair,
                pair,
                offset,
                gain_one,
                depth,
                points,
                channels,
            )
            return out, block_output

        out, block_output = unit(
            to_input, values[c], fields[c], grads[c // pair], outputs if c == chunks - 1 else []
        )
        gradients.append(exchange_lon(f"input_grad_{c}", out, -1))

    def to_small(small, gradients):
        input_grad = None
        for c, arrived in enumerate(gradients):
            input_grad = unpack(me, arrived, input_grad, c, depth, fields_in.shape, F32)
        part = exchange_lat("small", small).reshape(lat, -1, width)
        return jnp.sum(part, axis=0), input_grad

    part, gradients[-2:-1], order[0] = tie(part, gradients[-2:-1], order[0])
    small, input_grad = unit(to_small, small, gradients[:-1])
    with jax.named_scope("small"):
        bit = 1
        while bit < lon:
            small = small + lax.ppermute(small, "lon", [(i, i ^ bit) for i in range(lon)])
            bit *= 2
    small = unit(gathered, small)
    gradients[-1], small = tie(gradients[-1], small)
    input_grad = unpack(
        me, gradients[-1], input_grad, chunks - 1, depth, fields_in.shape, F32
    )

    with jax.named_scope("weights_lat"):
        summed = lax.all_gather(part, "lat", axis=0, tiled=True)
    grad_filter = small[:L, :channels]
    grad_one = jnp.sum(spectral_filter * grad_filter, axis=0) / norm_gains[0]
    grad_gains = jnp.stack([grad_one, small[L, :channels]])
    decay_rate = 1.0 - STEP ** (-0.8)
    grad_weight_in, new_weight_in, new_in_rows, new_in_columns = adafactor_call(
        summed, 0, weight_in, in_row_stats, in_column_stats, True, decay_rate
    )
    grad_weight_out, new_weight_out, new_out_columns, new_out_rows = adafactor_call(
        summed, 1, weight_out.T, out_column_stats, out_row_stats, False, decay_rate
    )
    grad_weight_out, new_weight_out = grad_weight_out.T, new_weight_out.T
    new_in_rows, new_in_columns = new_in_rows[:, 0], new_in_columns[0]
    new_out_rows, new_out_columns = new_out_rows[0], new_out_columns[:, 0]
    new_filter, new_filter_rows, new_filter_columns = adafactor_matrix(
        spectral_filter, grad_filter, filter_row_stats, filter_column_stats, decay_rate
    )
    new_gains, new_moments = adafactor_vector(norm_gains, grad_gains, gain_moments, decay_rate)
    return (
        block_output,
        input_grad,
        grad_weight_in,
        grad_weight_out,
        grad_filter,
        grad_gains,
        new_weight_in,
        new_weight_out,
        new_filter,
        new_gains,
        new_in_rows,
        new_in_columns,
        new_out_rows,
        new_out_columns,
        new_filter_rows,
        new_filter_columns,
        new_moments,
    )


def solution(mesh):
    spread = P(None, "lat", "lon", None)
    return jax.shard_map(
        body,
        mesh=mesh,
        in_specs=(spread, spread) + (P(),) * 13,
        out_specs=(spread, spread) + (P(),) * 15,
        check_vma=False,
    )
```

```python
import math

import jax
import jax.numpy as jnp
import numpy as np
from jax import lax
from jax.experimental import pallas as pl
from jax.experimental.pallas import tpu as pltpu
from jax.sharding import PartitionSpec as P

NLAT = 128
NLON = 256
L = 128
M = 96
Q = 2 * M
STEP = 3
LANES = 128

NORM_EPS = 1e-06
FIRST_EPS = 1e-30
SECOND_EPS = 0.001
CLIP_LEVEL = 0.5
STEP_RATE = 0.5
F32 = jnp.float32
LOW = jnp.bfloat16
VMEM_LIMIT = 60 * 1024 * 1024


def legendre_table():
    angles = math.pi * (np.arange(NLAT) + 0.5) / NLAT
    cosine, sine = np.cos(angles), np.sin(angles)
    table = np.zeros((M, L, NLAT))
    for m in range(M):
        factors = np.arange(1, m + 1)
        scale = math.sqrt(0.5 * np.prod((2.0 * factors + 1.0) / (2.0 * factors)))
        table[m, m] = scale * sine**m
        for l in range(m + 1, L):
            a = math.sqrt((4.0 * l * l - 1.0) / (l * l - m * m))
            b = math.sqrt(((l - 1.0) ** 2 - m * m) / (4.0 * (l - 1.0) ** 2 - 1.0))
            earlier = table[m, l - 2] if l >= m + 2 else 0.0
            table[m, l] = a * (cosine * table[m, l - 1] - b * earlier)
    return table, math.pi / NLAT * sine


def dft_tables():
    phases = 2.0 * math.pi * (np.outer(np.arange(NLON), np.arange(M)) % NLON) / NLON
    cosine, sine = np.cos(phases), np.sin(phases)
    doubling = np.where(np.arange(M) == 0, 1.0, 2.0)
    forward = np.stack([cosine, -sine], axis=2).reshape(NLON, Q) / NLON
    inverse = np.stack([doubling * cosine, -doubling * sine], axis=2).reshape(NLON, Q).T
    return forward, inverse


EXTRA = 16


def point_masks(n, points):
    row_of = lax.broadcasted_iota(jnp.int32, (n, EXTRA), 0) // points
    sel = (row_of == lax.broadcasted_iota(jnp.int32, (n, EXTRA), 1)).astype(F32).astype(LOW)
    place = lax.broadcasted_iota(jnp.int32, (n, LANES), 0) % points
    lane = lax.broadcasted_iota(jnp.int32, (n, LANES), 1)
    return sel, place == lane, lane == 0


def load_points(ref, n, points):
    tiles = ref.shape[0] // n
    sel, diagonal, first = point_masks(n, points)
    extra = jnp.dot(sel, ref[tiles * n : tiles * n + EXTRA, :], preferred_element_type=F32)
    column = jnp.sum(jnp.where(diagonal, extra, 0.0), axis=1, keepdims=True)
    pieces = [ref[t * n : (t + 1) * n, :].astype(F32) for t in range(tiles)]
    return jnp.concatenate([*pieces, jnp.where(first, column, 0.0)], axis=1)


def store_points(ref, values, last, points):
    n = values.shape[0]
    tiles = ref.shape[0] // n
    _, diagonal, _ = point_masks(n, points)
    for t in range(tiles):
        ref[t * n : (t + 1) * n, :] = values[:, t * LANES : (t + 1) * LANES]
    spread = jnp.where(diagonal, last, 0.0).astype(LOW)
    row_of = lax.broadcasted_iota(jnp.int32, (EXTRA, n), 1) // points
    pick = (row_of == lax.broadcasted_iota(jnp.int32, (EXTRA, n), 0)).astype(F32).astype(LOW)
    ref[tiles * n : tiles * n + EXTRA, :] = jnp.dot(
        pick, spread, preferred_element_type=F32
    ).astype(LOW)


def params():
    return pltpu.CompilerParams(vmem_limit_bytes=VMEM_LIMIT)


def cost(flops, size, transcendentals=0):
    return pl.CostEstimate(flops=1024, bytes_accessed=400_000_000, transcendentals=0)


def fixed(array):
    zeros = (0,) * len(array.shape)
    return pl.BlockSpec(array.shape, lambda *_: zeros)


def once(array):
    zeros = (0,) * len(array.shape)
    return pl.BlockSpec(array.shape, lambda *_: zeros, pipeline_mode=pl.Buffered(1))


def slot_table(table, count):
    return pl.BlockSpec(
        (1, *table.shape[1:]), lambda s, me_ref: ((me_ref[0] + (count - s)) % count, 0, 0)
    )


def pack(me, source, chunk, depth, count):
    _, _, points, channels = source.shape
    n = depth * points
    tiles = channels // LANES

    def kernel(me_ref, source_ref, *outs):
        step = pl.program_id(0)
        values = source_ref[0].reshape(n, channels)
        last = values[:, tiles * LANES :].astype(F32)
        for s, out in enumerate(outs):

            @pl.when(step == s)
            def _():
                store_points(out, values, last, points)

    shape = jax.ShapeDtypeStruct((tiles * n + EXTRA, LANES), LOW)
    return pl.pallas_call(
        kernel,
        out_shape=[shape] * count,
        grid_spec=pltpu.PrefetchScalarGridSpec(
            num_scalar_prefetch=1,
            grid=(count,),
            in_specs=[
                pl.BlockSpec(
                    (1, depth, points, channels),
                    lambda s, me_ref: ((me_ref[0] + s) % count, chunk, 0, 0),
                )
            ],
            out_specs=[fixed(shape)] * count,
        ),
        compiler_params=params(),
        cost_estimate=cost(0, 4 * count * n * channels),
        name="pack",
    )(me, source)


def unpack(me, slots, target, chunk, depth, shape, dtype):
    members, rows, points, channels = shape
    n = depth * points
    count = len(slots)

    def kernel(me_ref, *refs):
        out = refs[-1]
        step = pl.program_id(0)
        for s in range(count):

            @pl.when(step == s)
            def _():
                values = load_points(refs[s], n, points)[:, :channels]
                out[0] = values.astype(dtype).reshape(depth, points, channels)

    specs = [fixed(s) for s in slots]
    arrays = list(slots)
    aliases = {}
    if target is not None:
        specs.append(pl.BlockSpec(memory_space=pl.ANY))
        arrays.append(target)
        aliases = {count + 1: 0}
    return pl.pallas_call(
        kernel,
        out_shape=jax.ShapeDtypeStruct(shape, dtype),
        grid_spec=pltpu.PrefetchScalarGridSpec(
            num_scalar_prefetch=1,
            grid=(count,),
            in_specs=specs,
            out_specs=pl.BlockSpec(
                (1, depth, points, channels),
                lambda s, me_ref: ((me_ref[0] + s) % count, chunk, 0, 0),
            ),
        ),
        input_output_aliases=aliases,
        compiler_params=params(),
        cost_estimate=cost(0, 6 * count * n * channels),
        name="unpack",
    )(me, *arrays)


def first_forward(me, table, slots, offset, gain, depth, points, channels):
    n = depth * points
    count = len(slots)

    def kernel(me_ref, table_ref, offset_ref, gain_ref, *refs):
        out, total = refs[-2:]
        for s, slot in enumerate(refs[:-2]):
            shifted = load_points(slot, n, points) + offset_ref[...]
            square = jnp.sum(shifted * shifted, axis=1, keepdims=True)
            scale = lax.rsqrt(square * (1.0 / channels) + NORM_EPS)
            normed = (shifted * scale * gain_ref[...]).astype(LOW)
            owner = (me_ref[0] + (count - s)) % count
            part = jnp.dot(table_ref[owner], normed, preferred_element_type=F32)
            if s == 0:
                total[...] = part
            else:
                total[...] += part
        out[...] = total[...].astype(LOW)

    width = gain.shape[1]
    size = table.shape[1]
    arrays = [table, offset, gain, *slots]
    shape = jax.ShapeDtypeStruct((size, width), LOW)
    return pl.pallas_call(
        kernel,
        out_shape=shape,
        grid_spec=pltpu.PrefetchScalarGridSpec(
            num_scalar_prefetch=1,
            grid=(1,),
            in_specs=[fixed(a) for a in arrays],
            out_specs=fixed(shape),
            scratch_shapes=[pltpu.VMEM((size, width), F32)],
        ),
        compiler_params=params(),
        cost_estimate=cost(2 * size * count * n * width, 6 * 1024 * 1024),
        name="first_forward",
    )(me, *arrays)


def degree_blocks(refs, counts, lat, step, groups):
    for ref, count in zip(refs, counts):
        size = ref.shape[0]
        if groups == 1 and count == 1:
            yield ref, slice(0, size)
            continue
        part = size // lat // count // groups
        for c in range(count):
            for i in range(lat):
                start = (i * count + c) * (part * groups) + step * part
                yield ref, pl.ds(pl.multiple_of(start, part), part)


def degree_tables(to_ref, back_ref, spots_ref, spots_back_ref, each):
    group = spots_ref.shape[0]
    to = [
        jnp.dot(to_ref[q // each], spots_ref[q], preferred_element_type=F32).astype(LOW)
        for q in range(group)
    ]
    back = [
        jnp.dot(spots_back_ref[q], back_ref[q // each], preferred_element_type=F32).astype(LOW)
        for q in range(group)
    ]
    return jnp.concatenate(to, axis=0), jnp.concatenate(back, axis=1)


def filter_call(kernel, name, first, tables, spots, response, extra, spectra, each, groups, outs):
    part = tables[0].shape[0]
    block = spots[0].shape[0] // each
    tabled = pl.BlockSpec((block, L, NLAT), lambda g, first: (first[0] + g, 0, 0))
    grouped = lambda a: pl.BlockSpec((1, *a.shape[1:]), lambda g, first: (g, 0, 0))
    spec = lambda a: grouped(a) if len(a.shape) == 3 else fixed(a)
    arrays = [*tables, *spots, response, *extra, *spectra]
    return pl.pallas_call(
        kernel,
        out_shape=outs,
        grid_spec=pltpu.PrefetchScalarGridSpec(
            num_scalar_prefetch=1,
            grid=(groups,),
            in_specs=[tabled, tabled, fixed(spots[0]), fixed(spots[1]), fixed(response)]
            + [spec(a) for a in (*extra, *spectra)],
            out_specs=[spec(o) for o in outs],
        ),
        compiler_params=params(),
        cost_estimate=cost(16 * part, 24 * 1024 * 1024),
        name=name,
    )(first, *arrays)


def filter_forward(
    first, tables, spots, response, spectra, counts, out_counts, lat, each, groups
):
    size = spots[0].shape[2]
    width = response.shape[1]
    count = len(spectra)

    def kernel(first_ref, to_ref, back_ref, spots_ref, spots_back_ref, response_ref, *refs):
        step = pl.program_id(0)
        ins, outs, coefs = refs[:count], refs[count:-1], refs[-1]
        to, back = degree_tables(to_ref, back_ref, spots_ref, spots_back_ref, each)
        values = jnp.concatenate(
            [ref[rows, :] for ref, rows in degree_blocks(ins, counts, lat, step, groups)], axis=0
        )
        coef = jnp.dot(to, values, preferred_element_type=F32)
        coefs[0] = coef
        scale = jnp.concatenate([response_ref[...]] * (size // L), axis=0)
        filtered = (scale * coef).astype(LOW)
        result = jnp.dot(back, filtered, preferred_element_type=F32).astype(LOW)
        begin = 0
        for ref, rows in degree_blocks(outs, out_counts, lat, step, groups):
            length = rows.stop if isinstance(rows, slice) else rows.size
            ref[rows, :] = result[begin : begin + length]
            begin += length

    height = sum(s.shape[0] for s in spectra) // sum(counts)
    outs = [jax.ShapeDtypeStruct((height * c, width), LOW) for c in out_counts]
    outs.append(jax.ShapeDtypeStruct((groups, size, width), F32))
    return filter_call(
        kernel, "filter_forward", first, tables, spots, response, (), spectra, each, groups, outs
    )


def filter_backward(
    first, tables, spots, response, coefs, spectra, counts, out_counts, lat, each, groups
):
    size = spots[0].shape[2]
    width = response.shape[1]
    count = len(spectra)

    def kernel(
        first_ref, to_ref, back_ref, spots_ref, spots_back_ref, response_ref, coefs_ref, *refs
    ):
        step = pl.program_id(0)
        ins, outs, grad_ref = refs[:count], refs[count:-1], refs[-1]
        to, back = degree_tables(to_ref, back_ref, spots_ref, spots_back_ref, each)
        values = jnp.concatenate(
            [ref[rows, :] for ref, rows in degree_blocks(ins, counts, lat, step, groups)], axis=0
        )
        upstream = jnp.dot(to, values, preferred_element_type=F32)
        product = coefs_ref[0] * upstream
        grad = product[:L]
        for q in range(1, size // L):
            grad = grad + product[q * L : (q + 1) * L]

        @pl.when(step == 0)
        def _():
            grad_ref[...] = jnp.zeros_like(grad_ref)

        grad_ref[...] += grad
        scale = jnp.concatenate([response_ref[...]] * (size // L), axis=0)
        filtered = (scale * upstream).astype(LOW)
        result = jnp.dot(back, filtered, preferred_element_type=F32).astype(LOW)
        begin = 0
        for ref, rows in degree_blocks(outs, out_counts, lat, step, groups):
            length = rows.stop if isinstance(rows, slice) else rows.size
            ref[rows, :] = result[begin : begin + length]
            begin += length

    height = sum(s.shape[0] for s in spectra) // sum(counts)
    outs = [jax.ShapeDtypeStruct((height * c, width), LOW) for c in out_counts]
    outs.append(jax.ShapeDtypeStruct((L, width), F32))
    return filter_call(
        kernel,
        "filter_backward",
        first,
        tables,
        spots,
        response,
        (coefs,),
        spectra,
        each,
        groups,
        outs,
    )


def prepare_weights(weight_in, weight_out, width, hidden_width):
    channels, units = weight_in.shape

    def kernel(in_ref, out_ref, w_in, w_out, w_in_t, w_out_t):
        w_in[...] = jnp.zeros_like(w_in)
        w_out_t[...] = jnp.zeros_like(w_out_t)
        w_in[:channels, :units] = in_ref[...].astype(LOW)
        w_out_t[:channels, :units] = out_ref[...].astype(LOW)
        w_in_t[...] = w_in[...].T
        w_out[...] = w_out_t[...].T

    outs = [
        jax.ShapeDtypeStruct(shape, LOW)
        for shape in [(width, hidden_width), (hidden_width, width)] * 2
    ]
    outs = [outs[0], outs[1], outs[1], outs[0]]
    return pl.pallas_call(
        kernel, out_shape=outs, compiler_params=params(), name="prepare_weights"
    )(weight_in, weight_out.T)


def feed_forward(
    me, tables, weights, offset, gain, spectra, slots, upstreams, lat, depth, points, channels, split
):
    n = depth * points
    pair, count = len(slots), len(slots[0])
    flat = [slot for chunk in slots for slot in chunk]
    width, hidden_width = weights[0].shape
    size = spectra.shape[0] // pair
    part = size // lat
    inverse_channels = 1.0 / channels

    def kernel(
        me_ref, out_table, back_table, w_in, w_out, w_in_t, w_out_t, offset_ref, gain_ref, y, *refs
    ):
        ins, ups = refs[: pair * count], refs[pair * count : (pair + 1) * count]
        refs = refs[(pair + 1) * count :]
        outs = refs[: split * count]
        refs = refs[split * count :]
        grad_ref, second_ref, active_ref, pre_ref, cot_ref, gain_part, back_ref = refs[:-4]
        x_now, up_now, y_now, total = refs[-4:]
        step = pl.program_id(0)

        @pl.when(step == 0)
        def _():
            gain_part[...] = jnp.zeros_like(gain_part)
            total[...] = jnp.zeros_like(total)
            for c in range(pair):
                for i in range(lat):
                    y_now[c, i * part : (i + 1) * part] = y[
                        (i * pair + c) * part : (i * pair + c + 1) * part
                    ]

        for s in range(count):

            @pl.when(step == s)
            def _():
                for c in range(pair):
                    x_now[c] = ins[c * count + s][...]
                up_now[...] = ups[s][...]

        rows = lambda parts: jnp.concatenate(parts, axis=0) if pair > 1 else parts[0]
        branch = rows(
            [
                jnp.dot(out_table[0], y_now[c], preferred_element_type=F32).astype(LOW)
                for c in range(pair)
            ]
        )
        shifted = rows([load_points(x_now.at[c], n, points) for c in range(pair)])
        hidden = shifted + offset_ref[...] + branch.astype(F32)
        square = jnp.sum(hidden * hidden, axis=1, keepdims=True)
        scale = lax.rsqrt(square * inverse_channels + NORM_EPS)
        second = (hidden * scale * gain_ref[...]).astype(LOW)
        second_ref[...] = second
        upstream = load_points(up_now, pair * n, points)
        upstream_low = upstream.astype(LOW)
        cot_ref[...] = upstream_low
        preact = jnp.dot(second, w_in[...], preferred_element_type=F32)
        back_active = jnp.dot(upstream_low, w_out_t[...], preferred_element_type=F32)
        share = 0.5 + 0.5 * lax.erf(preact * math.sqrt(0.5))
        density = jnp.exp(-0.5 * preact * preact) * (1.0 / math.sqrt(2.0 * math.pi))
        active = (preact * share).astype(LOW)
        active_ref[...] = active
        back_preact = (back_active * (share + preact * density)).astype(LOW)
        pre_ref[...] = back_preact
        output = hidden + jnp.dot(active, w_out[...], preferred_element_type=F32)
        back_second = jnp.dot(back_preact, w_in_t[...], preferred_element_type=F32)
        scaled = back_second * gain_ref[...]
        inner = jnp.sum(hidden * scaled, axis=1, keepdims=True) * inverse_channels
        grad = scale * scaled - hidden * (scale * scale * scale * inner) + upstream
        grad_ref[...] = grad
        grad_low = grad.astype(LOW)
        for c in range(pair):
            total[c] += jnp.dot(
                back_table[0], grad_low[c * n : (c + 1) * n], preferred_element_type=F32
            )
        gain_part[...] += jnp.sum(
            (back_second * (hidden * scale)).reshape(pair * n // 8, 8, width), axis=0
        )

        @pl.when(step == count - 1)
        def _():
            for c in range(pair):
                for i in range(lat):
                    back_ref[(i * pair + c) * part : (i * pair + c + 1) * part] = total[
                        c, i * part : (i + 1) * part
                    ].astype(LOW)

        m = pair * n // split
        leaving = [x_now.at[c] for c in range(pair)] if split > 1 else [up_now]
        for c in range(split):
            block = output[c * m : (c + 1) * m]
            store_points(leaving[c], block.astype(LOW), block[:, channels - 1 : channels], points)
        for s in range(count):

            @pl.when(step == s)
            def _():
                for c in range(split):
                    outs[c * count + s][...] = leaving[c][...]

    rows = lambda w: pl.BlockSpec((pair * n, w), lambda s, me_ref: (s, 0))
    slot = jax.ShapeDtypeStruct((flat if split > 1 else upstreams)[0].shape, LOW)
    height = count * pair * n
    outs = [slot] * (split * count) + [
        jax.ShapeDtypeStruct((height, width), F32),
        jax.ShapeDtypeStruct((height, width), LOW),
        jax.ShapeDtypeStruct((height, hidden_width), LOW),
        jax.ShapeDtypeStruct((height, hidden_width), LOW),
        jax.ShapeDtypeStruct((height, width), LOW),
        jax.ShapeDtypeStruct((8, width), F32),
        jax.ShapeDtypeStruct(spectra.shape, LOW),
    ]
    out_specs = [fixed(slot)] * (split * count) + [
        rows(width),
        rows(width),
        rows(hidden_width),
        rows(hidden_width),
        rows(width),
        fixed(outs[-2]),
        fixed(outs[-1]),
    ]
    arrays = [*tables, *weights, offset, gain, spectra, *flat, *upstreams]
    return pl.pallas_call(
        kernel,
        out_shape=outs,
        grid_spec=pltpu.PrefetchScalarGridSpec(
            num_scalar_prefetch=1,
            grid=(count,),
            in_specs=[slot_table(t, count) for t in tables] + [once(a) for a in arrays[2:]],
            out_specs=out_specs,
            scratch_shapes=[
                pltpu.VMEM((pair, *flat[0].shape), LOW),
                pltpu.VMEM(upstreams[0].shape, LOW),
                pltpu.VMEM((pair, size, width), LOW),
                pltpu.VMEM((pair, size, width), F32),
            ],
        ),
        compiler_params=params(),
        cost_estimate=cost(0, 0),
        name="feed_forward",
    )(me, *arrays)


def weight_sums(parts, block=512):
    count = len(parts)
    height, width = parts[0][0].shape
    hidden_width = parts[0][1].shape[1]
    block = min(block, height)
    steps = height // block

    def kernel(*refs):
        ins, out = refs[:-1], refs[-1]
        step = pl.program_id(0)

        @pl.when(step == 0)
        def _():
            out[...] = jnp.zeros_like(out)

        def add(row, left, right):
            out[row : row + width, :] += lax.dot_general(
                left[...], right[...], (((0,), (0,)), ((), ())), preferred_element_type=F32
            )

        for m in range(count):

            @pl.when((step >= m * steps) & (step < (m + 1) * steps))
            def _():
                second, active, pre, cot = ins[4 * m : 4 * m + 4]
                add(0, second, pre)
                add(width, cot, active)

    def spec(array, m):
        return pl.BlockSpec(
            (block, array.shape[1]),
            lambda k: (jnp.clip(k - m * steps, 0, steps - 1), 0),
        )

    shape = jax.ShapeDtypeStruct((2 * width, hidden_width), F32)
    return pl.pallas_call(
        kernel,
        out_shape=shape,
        grid=(count * steps,),
        in_specs=[spec(a, m) for m, part in enumerate(parts) for a in part],
        out_specs=fixed(shape),
        compiler_params=params(),
        cost_estimate=cost(0, 0),
        name="weight_sums",
    )(*[a for part in parts for a in part])


def first_backward(
    me, table, spectra, slots, grads, place, pair, offset, gain, depth, points, channels
):
    n = depth * points
    count = len(slots)
    width = gain.shape[1]
    inverse_channels = 1.0 / channels

    def kernel(me_ref, table_ref, y, grad_ref, offset_ref, gain_ref, *refs):
        ins, outs, now = refs[:count], refs[count:-1], refs[-1]
        step = pl.program_id(0)
        for s in range(count):

            @pl.when(step == s)
            def _():
                now[...] = ins[s][...]

        back = jnp.dot(table_ref[0], y[...], preferred_element_type=F32).astype(LOW).astype(F32)
        shifted = load_points(now, n, points) + offset_ref[...]
        square = jnp.sum(shifted * shifted, axis=1, keepdims=True)
        scale = lax.rsqrt(square * inverse_channels + NORM_EPS)
        scaled = back * gain_ref[...]
        inner = jnp.sum(shifted * scaled, axis=1, keepdims=True) * inverse_channels
        result = grad_ref[...] + scale * scaled - shifted * (scale * scale * scale * inner)
        store_points(now, result.astype(LOW), result[:, channels - 1 : channels], points)
        for s in range(count):

            @pl.when(step == s)
            def _():
                outs[s][...] = now[...]

    slot = jax.ShapeDtypeStruct(slots[0].shape, LOW)
    outs = [slot] * count
    return pl.pallas_call(
        kernel,
        out_shape=outs,
        grid_spec=pltpu.PrefetchScalarGridSpec(
            num_scalar_prefetch=1,
            grid=(count,),
            in_specs=[
                slot_table(table, count),
                fixed(spectra),
                pl.BlockSpec((n, width), lambda s, me_ref: (s * pair + place, 0)),
                fixed(offset),
                fixed(gain),
            ]
            + [fixed(s) for s in slots],
            out_specs=[fixed(o) for o in outs],
            scratch_shapes=[pltpu.VMEM(slot.shape, LOW)],
        ),
        compiler_params=params(),
        cost_estimate=cost(2 * count * n * width * spectra.shape[0], 12 * 1024 * 1024),
        name="first_backward",
    )(me, table, spectra, grads, offset, gain, *slots)


def adafactor_matrix(weight_now, gradient, rows_old, columns_old, decay_rate):
    squares = gradient * gradient + FIRST_EPS
    rows_new = decay_rate * rows_old + (1.0 - decay_rate) * jnp.mean(squares, axis=1)
    columns_new = decay_rate * columns_old + (1.0 - decay_rate) * jnp.mean(squares, axis=0)
    estimate = rows_new[:, None] * columns_new[None, :] / jnp.mean(rows_new)
    update = gradient * lax.rsqrt(estimate)
    update = update / jnp.maximum(1.0, jnp.sqrt(jnp.mean(update * update)) / CLIP_LEVEL)
    scale_now = STEP_RATE * jnp.maximum(SECOND_EPS, jnp.sqrt(jnp.mean(weight_now * weight_now)))
    return (weight_now - scale_now * update, rows_new, columns_new)


def adafactor_call(gradients, place, weight_now, rows_old, columns_old, by_rows, decay_rate):
    height, width = weight_now.shape

    def kernel(grad_ref, weight_ref, rows_ref, columns_ref, grad_out, new, rows_out, columns_out):
        gradient = grad_ref[:height, :width].astype(F32)
        grad_out[...] = gradient
        squares = gradient * gradient + FIRST_EPS
        rows_mean = jnp.sum(squares, axis=1, keepdims=True) * (1.0 / width)
        columns_mean = jnp.sum(squares, axis=0, keepdims=True) * (1.0 / height)
        rows_new = decay_rate * rows_ref[...] + (1.0 - decay_rate) * rows_mean
        columns_new = decay_rate * columns_ref[...] + (1.0 - decay_rate) * columns_mean
        across = lax.broadcasted_iota(jnp.int32, (height, height), 0)
        along = lax.broadcasted_iota(jnp.int32, (height, height), 1)
        turned = jnp.sum(jnp.where(across == along, rows_new, 0.0), axis=0, keepdims=True)
        rows_out[...] = turned[0]
        columns_out[...] = columns_new[0]
        mean = jnp.mean(rows_new) if by_rows else jnp.mean(columns_new)
        update = gradient * (lax.rsqrt(rows_new / mean) * lax.rsqrt(columns_new))
        weight = weight_ref[...]
        size = 1.0 / (height * width)
        clip = jnp.maximum(1.0, jnp.sqrt(jnp.sum(update * update) * size) / CLIP_LEVEL)
        rate = STEP_RATE * jnp.maximum(SECOND_EPS, jnp.sqrt(jnp.sum(weight * weight) * size))
        new[...] = weight - update * (rate / clip)

    whole = lambda a: pl.BlockSpec(a.shape, lambda i: (0,) * len(a.shape))
    tall, wide = gradients.shape
    matrix = jax.ShapeDtypeStruct((height, width), F32)
    outs = [matrix, matrix]
    outs += [jax.ShapeDtypeStruct((height,), F32), jax.ShapeDtypeStruct((width,), F32)]
    arrays = [weight_now, rows_old[:, None], columns_old[None]]
    return pl.pallas_call(
        kernel,
        out_shape=outs,
        grid=(1,),
        in_specs=[pl.BlockSpec((tall // 2, wide), lambda i: (place, 0))]
        + [whole(a) for a in arrays],
        out_specs=[whole(o) for o in outs],
        compiler_params=params(),
        cost_estimate=cost(0, 0),
        name="adafactor",
    )(gradients, *arrays)


def adafactor_vector(weight_now, gradient, moments_old, decay_rate):
    moments_new = decay_rate * moments_old + (1.0 - decay_rate) * (gradient * gradient + FIRST_EPS)
    update = gradient * lax.rsqrt(moments_new)
    update = update / jnp.maximum(
        1.0, jnp.sqrt(jnp.mean(update * update, axis=1, keepdims=True)) / CLIP_LEVEL
    )
    scale_now = STEP_RATE * jnp.maximum(
        SECOND_EPS, jnp.sqrt(jnp.mean(weight_now * weight_now, axis=1, keepdims=True))
    )
    return (weight_now - scale_now * update, moments_new)


def tie(*groups):
    return lax.optimization_barrier(groups)


def take(array, index):
    return lax.dynamic_index_in_dim(array, index, 0, keepdims=False)


def chunk_rows(rows):
    return rows // 4 if rows % 4 == 0 else rows


def group_size(share, depth):
    for size in range(1, share):
        if share % size == 0 and size * depth % 16 == 0:
            return size
    return share


def body(
    fields_in,
    cotangent,
    member_dates,
    date_table,
    norm_gains,
    spectral_filter,
    weight_in,
    weight_out,
    gain_moments,
    in_row_stats,
    in_column_stats,
    out_row_stats,
    out_column_stats,
    filter_row_stats,
    filter_column_stats,
):
    members, rows, points, channels = fields_in.shape
    units = weight_in.shape[1]
    width = -(-channels // LANES) * LANES
    hidden_width = -(-units // LANES) * LANES
    lat, lon = lax.axis_size("lat"), lax.axis_size("lon")
    lat_me, lon_me = lax.axis_index("lat"), lax.axis_index("lon")
    me = lon_me.astype(jnp.int32).reshape(1)
    share = Q // lat
    depth = chunk_rows(rows)
    chunks = rows // depth
    pair = 2 if chunks % 2 == 0 else 1
    mids = chunks // pair
    n = depth * points

    def wider(array, *sizes):
        return jnp.pad(array, [(0, s - d) for s, d in zip(sizes, array.shape)])

    def exchange_lon(name, slots, sign):
        with jax.named_scope(name):
            return [
                slot
                if s == 0
                else lax.ppermute(slot, "lon", [(i, (i + sign * s) % lon) for i in range(lon)])
                for s, slot in enumerate(slots)
            ]

    def exchange_lat(name, *spectra):
        blocks = [a.reshape(lat, -1, width) for a in spectra]
        blocks = jnp.concatenate(blocks, axis=1) if len(blocks) > 1 else blocks[0]
        with jax.named_scope(name):
            blocks = lax.all_to_all(blocks, "lat", split_axis=0, concat_axis=0, tiled=True)
        return blocks.reshape(-1, width)

    inside = lat_me < lat

    order = [norm_gains[:1, :LANES]]

    def unit(function, *arrays):
        run = lambda token, *arrays: tie(token, function(*arrays))
        shapes = jax.eval_shape(run, order[0], *arrays)
        blank = lambda *_: jax.tree.map(lambda a: jnp.zeros(a.shape, a.dtype), shapes)
        order[0], out = lax.cond(inside, run, blank, order[0], *arrays)
        return out

    def spread(values):
        height = -(-values.shape[0] // (8 * lat)) * 8
        return wider(values, height * lat, values.shape[1])

    def gathered(part):
        return exchange_lat("gather", jnp.broadcast_to(part[None], (lat, *part.shape)))

    forward, inverse = dft_tables()

    def by_device(table):
        blocks = table.reshape(lon, points, Q).transpose(0, 2, 1)
        return np.einsum("zqk,ab->zqabk", blocks, np.eye(depth)).reshape(lon, Q * depth, n)

    analysis = jnp.asarray(by_device(forward), LOW)
    back_analysis = jnp.asarray(by_device(inverse.T), LOW)
    synthesis = jnp.asarray(by_device(inverse.T).transpose(0, 2, 1), LOW)
    back_synthesis = jnp.asarray(by_device(forward).transpose(0, 2, 1), LOW)

    legendre, quadrature = legendre_table()
    group = group_size(share, depth)
    groups = share // group
    places = np.arange(NLAT).reshape(lat, chunks, depth).transpose(1, 0, 2)
    spots = np.zeros((group, NLAT, chunks, lat, group, depth))
    for q in range(group):
        for c in range(chunks):
            for i in range(lat):
                spots[q, places[c, i], c, i, q, np.arange(depth)] = 1.0
    spots = spots.reshape(group, NLAT, group * NLAT)
    spots = (jnp.asarray(spots, LOW), jnp.asarray(spots.transpose(0, 2, 1), LOW))
    each = 2 if group % 2 == 0 else 1
    first = (lat_me * groups if each == 2 else 0 * lat_me).astype(jnp.int32).reshape(1)

    def own_degrees(table):
        table = jnp.asarray(table, LOW)
        if each == 2:
            return table
        own_q = (lat_me * share + jnp.arange(share, dtype=jnp.int32)) // 2
        return jnp.take(table, own_q, axis=0)

    plain = own_degrees(legendre)
    weighted = own_degrees(legendre * quadrature)
    plain_back = own_degrees(legendre.transpose(0, 2, 1))
    weighted_back = own_degrees((legendre * quadrature).transpose(0, 2, 1))

    date_selector = (
        member_dates[:, None] == jnp.arange(date_table.shape[0], dtype=jnp.int32)[None, :]
    ).astype(F32)
    offsets = jnp.dot(date_selector, date_table, precision=lax.Precision.HIGHEST)
    offset = wider(take(offsets, lon_me)[None], 1, width)
    gain_one = wider(norm_gains[:1], 1, width)
    gain_two = wider(norm_gains[1:], 1, width)
    response = wider(spectral_filter, L, width)
    fields = [pack(me, fields_in, c, depth, lon) for c in range(chunks)]
    upstreams = [None] * mids
    waiting = [(f"fields_{c}", fields, c) for c in range(chunks)]
    waiting += [(f"upstream_{c}", upstreams, c) for c in range(mids)]

    def send_next(after):
        if not waiting or waiting[0][1][waiting[0][2]] is None:
            return after
        name, packs, c = waiting.pop(0)
        after, slots = tie(after, packs[c])
        packs[c] = exchange_lon(name, slots, 1)
        return after

    fields[0] = exchange_lon("fields_0", fields[0], 1)
    del waiting[0]
    fields[0], fields[1:], offset, gain_one, gain_two, response = tie(
        fields[0], fields[1:], offset, gain_one, gain_two, response
    )

    spectra = []
    for c in range(chunks):

        def to_spectra(cotangent, *slots):
            rows_now = first_forward(me, analysis, slots, offset, gain_one, depth, points, channels)
            rows_now = exchange_lat(f"spectra_{c}", rows_now)
            return rows_now, [pack(me, a, c, depth * pair, lon) for a in cotangent]

        if c > 0:
            fields[c], spectra[c - 1] = tie(fields[c], spectra[c - 1])
        fields[c] = send_next(fields[c])
        rows_now, packed = unit(to_spectra, [cotangent] if c < mids else [], *fields[c])
        upstreams[c : c + 1] = packed if c < mids else upstreams[c : c + 1]
        spectra.append(rows_now)

    def to_coefficients(weight_in, weight_out, *spectra):
        *values, coefs = filter_forward(
            first,
            (weighted, plain_back),
            spots,
            response,
            spectra,
            [1] * chunks,
            [pair] * mids,
            lat,
            each,
            groups,
        )
        values[0] = exchange_lat("synthesis_0", values[0])
        return values, coefs, prepare_weights(weight_in, weight_out, width, hidden_width)

    spectra[-1] = send_next(spectra[-1])
    values, coefs, weights = unit(to_coefficients, weight_in, weight_out, *spectra)

    splits = [1] * (mids - 1) + [pair]
    backs, grads, parts, outputs = [], [], [], []
    gain_parts = []
    for c in range(mids):

        def step(spectrum, slots, upstream, following, before):
            out = feed_forward(
                me,
                (synthesis, back_analysis),
                weights,
                offset,
                gain_two,
                spectrum,
                slots,
                upstream,
                lat,
                depth,
                points,
                channels,
                splits[c],
            )
            following = [exchange_lat(f"synthesis_{c + 1}", a) for a in following]
            before = [exchange_lat(f"back_synthesis_{c - 1}", a) for a in before]
            return out, following, before

        out, values[c + 1 : c + 2], backs[c - 1 : c] = unit(
            step,
            values[c],
            fields[c * pair : (c + 1) * pair],
            upstreams[c],
            values[c + 1 : c + 2],
            backs[c - 1 : c],
        )
        for p in range(splits[c]):
            leaving = out[p * lon : (p + 1) * lon]
            outputs.append(exchange_lon(f"output_{c}_{p}", leaving, -1))
        grad, *part, gain_part, back = out[splits[c] * lon :]
        grads.append(grad)
        parts.append(part)
        gain_parts.append(gain_part)
        backs.append(back)

    def to_weights(late, parts):
        return exchange_lat(f"back_synthesis_{mids - 1}", late), weight_sums(parts)

    def to_gradients(backs, coefs, gain_parts):
        *values, filter_part = filter_backward(
            first,
            (plain, weighted_back),
            spots,
            response,
            coefs,
            backs,
            [pair] * mids,
            [1] * chunks,
            lat,
            each,
            groups,
        )
        gain_part = sum(jnp.sum(a, axis=0) for a in gain_parts)
        return values, spread(jnp.concatenate([filter_part, gain_part[None]], axis=0))

    early = mids - 1
    backs[-1], weight_part = unit(to_weights, backs[-1], parts)
    outputs[:early], order[0], weight_part = tie(outputs[:early], order[0], weight_part)
    values, small = unit(to_gradients, backs, coefs, gain_parts)
    outputs[early:-1], order[0] = tie(outputs[early:-1], order[0])

    gradients = []
    with jax.named_scope("weights_lat"):
        part = lax.psum_scatter(weight_part, "lat", scatter_dimension=0, tiled=True)

    for c in range(chunks):
        if c == min(1, chunks - 1):
            outputs[-1], order[0] = tie(outputs[-1], order[0])
        if c == min(2, chunks - 1):
            part, order[0] = tie(part, order[0])
            with jax.named_scope("weights_lon"):
                part = lax.psum(part.astype(LOW), "lon")
        if c >= 2:
            gradients[c - 2], order[0] = tie(gradients[c - 2], order[0])

        def to_input(spectrum, slots, grad, outputs):
            block_output, row = None, 0
            for arrived in outputs:
                tall = depth * pair if arrived[0].shape[0] > slots[0].shape[0] else depth
                block_output = unpack(
                    me, arrived, block_output, row // tall, tall, fields_in.shape, LOW
                )
                row += tall
            out = first_backward(
                me,
                back_synthesis,
                exchange_lat(f"back_spectra_{c}", spectrum),
                slots,
                grad,
                c % pair,
                pair,
                offset,
                gain_one,
                depth,
                points,
                channels,
            )
            return out, block_output

        out, block_output = unit(
            to_input, values[c], fields[c], grads[c // pair], outputs if c == chunks - 1 else []
        )
        gradients.append(exchange_lon(f"input_grad_{c}", out, -1))

    def to_small(small, gradients):
        input_grad = None
        for c, arrived in enumerate(gradients):
            input_grad = unpack(me, arrived, input_grad, c, depth, fields_in.shape, F32)
        part = exchange_lat("small", small).reshape(lat, -1, width)
        return jnp.sum(part, axis=0), input_grad

    part, gradients[-2:-1], order[0] = tie(part, gradients[-2:-1], order[0])
    small, input_grad = unit(to_small, small, gradients[:-1])
    with jax.named_scope("small"):
        bit = 1
        while bit < lon:
            small = small + lax.ppermute(small, "lon", [(i, i ^ bit) for i in range(lon)])
            bit *= 2
    with jax.named_scope("weights_lat"):
        summed = lax.all_gather(part, "lat", axis=0, tiled=True)
    decay_rate = 1.0 - STEP ** (-0.8)

    def to_updates(small, summed, weight_in, weight_out):
        inner = adafactor_call(
            summed, 0, weight_in, in_row_stats, in_column_stats, True, decay_rate
        )
        outer = adafactor_call(
            summed, 1, weight_out.T, out_column_stats, out_row_stats, False, decay_rate
        )
        return gathered(small), inner, outer

    small, inner, outer = unit(to_updates, small, summed, weight_in, weight_out)
    grad_weight_in, new_weight_in, new_in_rows, new_in_columns = inner
    grad_weight_out, new_weight_out, new_out_columns, new_out_rows = outer
    gradients[-1], small = tie(gradients[-1], small)
    input_grad = unpack(
        me, gradients[-1], input_grad, chunks - 1, depth, fields_in.shape, F32
    )

    grad_filter = small[:L, :channels]
    grad_one = jnp.sum(spectral_filter * grad_filter, axis=0) / norm_gains[0]
    grad_gains = jnp.stack([grad_one, small[L, :channels]])
    grad_weight_out, new_weight_out = grad_weight_out.T, new_weight_out.T
    new_filter, new_filter_rows, new_filter_columns = adafactor_matrix(
        spectral_filter, grad_filter, filter_row_stats, filter_column_stats, decay_rate
    )
    new_gains, new_moments = adafactor_vector(norm_gains, grad_gains, gain_moments, decay_rate)
    return (
        block_output,
        input_grad,
        grad_weight_in,
        grad_weight_out,
        grad_filter,
        grad_gains,
        new_weight_in,
        new_weight_out,
        new_filter,
        new_gains,
        new_in_rows,
        new_in_columns,
        new_out_rows,
        new_out_columns,
        new_filter_rows,
        new_filter_columns,
        new_moments,
    )


def solution(mesh):
    spread = P(None, "lat", "lon", None)
    return jax.shard_map(
        body,
        mesh=mesh,
        in_specs=(spread, spread) + (P(),) * 13,
        out_specs=(spread, spread) + (P(),) * 15,
        check_vma=False,
    )
```

```python
import math

import jax
import jax.numpy as jnp
import numpy as np
from jax import lax
from jax.experimental import pallas as pl
from jax.experimental.pallas import tpu as pltpu
from jax.sharding import PartitionSpec as P

NLAT = 128
NLON = 256
L = 128
M = 96
Q = 2 * M
STEP = 3
LANES = 128

NORM_EPS = 1e-06
FIRST_EPS = 1e-30
SECOND_EPS = 0.001
CLIP_LEVEL = 0.5
STEP_RATE = 0.5
F32 = jnp.float32
LOW = jnp.bfloat16
VMEM_LIMIT = 60 * 1024 * 1024


def legendre_table():
    angles = math.pi * (np.arange(NLAT) + 0.5) / NLAT
    cosine, sine = np.cos(angles), np.sin(angles)
    table = np.zeros((M, L, NLAT))
    for m in range(M):
        factors = np.arange(1, m + 1)
        scale = math.sqrt(0.5 * np.prod((2.0 * factors + 1.0) / (2.0 * factors)))
        table[m, m] = scale * sine**m
        for l in range(m + 1, L):
            a = math.sqrt((4.0 * l * l - 1.0) / (l * l - m * m))
            b = math.sqrt(((l - 1.0) ** 2 - m * m) / (4.0 * (l - 1.0) ** 2 - 1.0))
            earlier = table[m, l - 2] if l >= m + 2 else 0.0
            table[m, l] = a * (cosine * table[m, l - 1] - b * earlier)
    return table, math.pi / NLAT * sine


def dft_tables():
    phases = 2.0 * math.pi * (np.outer(np.arange(NLON), np.arange(M)) % NLON) / NLON
    cosine, sine = np.cos(phases), np.sin(phases)
    doubling = np.where(np.arange(M) == 0, 1.0, 2.0)
    forward = np.stack([cosine, -sine], axis=2).reshape(NLON, Q) / NLON
    inverse = np.stack([doubling * cosine, -doubling * sine], axis=2).reshape(NLON, Q).T
    return forward, inverse


EXTRA = 16


def point_masks(n, points):
    row_of = lax.broadcasted_iota(jnp.int32, (n, EXTRA), 0) // points
    sel = (row_of == lax.broadcasted_iota(jnp.int32, (n, EXTRA), 1)).astype(F32).astype(LOW)
    place = lax.broadcasted_iota(jnp.int32, (n, LANES), 0) % points
    lane = lax.broadcasted_iota(jnp.int32, (n, LANES), 1)
    return sel, place == lane, lane == 0


def load_points(ref, n, points):
    tiles = ref.shape[0] // n
    sel, diagonal, first = point_masks(n, points)
    extra = jnp.dot(sel, ref[tiles * n : tiles * n + EXTRA, :], preferred_element_type=F32)
    column = jnp.sum(jnp.where(diagonal, extra, 0.0), axis=1, keepdims=True)
    pieces = [ref[t * n : (t + 1) * n, :].astype(F32) for t in range(tiles)]
    return jnp.concatenate([*pieces, jnp.where(first, column, 0.0)], axis=1)


def store_points(ref, values, last, points):
    n = values.shape[0]
    tiles = ref.shape[0] // n
    _, diagonal, _ = point_masks(n, points)
    for t in range(tiles):
        ref[t * n : (t + 1) * n, :] = values[:, t * LANES : (t + 1) * LANES]
    spread = jnp.where(diagonal, last, 0.0).astype(LOW)
    row_of = lax.broadcasted_iota(jnp.int32, (EXTRA, n), 1) // points
    pick = (row_of == lax.broadcasted_iota(jnp.int32, (EXTRA, n), 0)).astype(F32).astype(LOW)
    ref[tiles * n : tiles * n + EXTRA, :] = jnp.dot(
        pick, spread, preferred_element_type=F32
    ).astype(LOW)


def params():
    return pltpu.CompilerParams(vmem_limit_bytes=VMEM_LIMIT)


def cost(flops, size, transcendentals=0):
    return pl.CostEstimate(flops=1024, bytes_accessed=400_000_000, transcendentals=0)


def fixed(array):
    zeros = (0,) * len(array.shape)
    return pl.BlockSpec(array.shape, lambda *_: zeros)


def once(array):
    zeros = (0,) * len(array.shape)
    return pl.BlockSpec(array.shape, lambda *_: zeros, pipeline_mode=pl.Buffered(1))


def slot_table(table, count):
    return pl.BlockSpec(
        (1, *table.shape[1:]), lambda s, me_ref: ((me_ref[0] + (count - s)) % count, 0, 0)
    )


def pack(me, source, chunk, depth, count):
    _, _, points, channels = source.shape
    n = depth * points
    tiles = channels // LANES

    def kernel(me_ref, source_ref, *outs):
        step = pl.program_id(0)
        values = source_ref[0].reshape(n, channels)
        last = values[:, tiles * LANES :].astype(F32)
        for s, out in enumerate(outs):

            @pl.when(step == s)
            def _():
                store_points(out, values, last, points)

    shape = jax.ShapeDtypeStruct((tiles * n + EXTRA, LANES), LOW)
    return pl.pallas_call(
        kernel,
        out_shape=[shape] * count,
        grid_spec=pltpu.PrefetchScalarGridSpec(
            num_scalar_prefetch=1,
            grid=(count,),
            in_specs=[
                pl.BlockSpec(
                    (1, depth, points, channels),
                    lambda s, me_ref: ((me_ref[0] + s) % count, chunk, 0, 0),
                )
            ],
            out_specs=[fixed(shape)] * count,
        ),
        compiler_params=params(),
        cost_estimate=cost(0, 4 * count * n * channels),
        name="pack",
    )(me, source)


def unpack(me, slots, target, chunk, depth, shape, dtype):
    members, rows, points, channels = shape
    n = depth * points
    count = len(slots)

    def kernel(me_ref, *refs):
        out = refs[-1]
        step = pl.program_id(0)
        for s in range(count):

            @pl.when(step == s)
            def _():
                values = load_points(refs[s], n, points)[:, :channels]
                out[0] = values.astype(dtype).reshape(depth, points, channels)

    specs = [fixed(s) for s in slots]
    arrays = list(slots)
    aliases = {}
    if target is not None:
        specs.append(pl.BlockSpec(memory_space=pl.ANY))
        arrays.append(target)
        aliases = {count + 1: 0}
    return pl.pallas_call(
        kernel,
        out_shape=jax.ShapeDtypeStruct(shape, dtype),
        grid_spec=pltpu.PrefetchScalarGridSpec(
            num_scalar_prefetch=1,
            grid=(count,),
            in_specs=specs,
            out_specs=pl.BlockSpec(
                (1, depth, points, channels),
                lambda s, me_ref: ((me_ref[0] + s) % count, chunk, 0, 0),
            ),
        ),
        input_output_aliases=aliases,
        compiler_params=params(),
        cost_estimate=cost(0, 6 * count * n * channels),
        name="unpack",
    )(me, *arrays)


def first_forward(me, table, slots, offset, gain, depth, points, channels):
    n = depth * points
    count = len(slots)

    def kernel(me_ref, table_ref, offset_ref, gain_ref, *refs):
        out, total = refs[-2:]
        for s, slot in enumerate(refs[:-2]):
            shifted = load_points(slot, n, points) + offset_ref[...]
            square = jnp.sum(shifted * shifted, axis=1, keepdims=True)
            scale = lax.rsqrt(square * (1.0 / channels) + NORM_EPS)
            normed = (shifted * scale * gain_ref[...]).astype(LOW)
            owner = (me_ref[0] + (count - s)) % count
            part = jnp.dot(table_ref[owner], normed, preferred_element_type=F32)
            if s == 0:
                total[...] = part
            else:
                total[...] += part
        out[...] = total[...].astype(LOW)

    width = gain.shape[1]
    size = table.shape[1]
    arrays = [table, offset, gain, *slots]
    shape = jax.ShapeDtypeStruct((size, width), LOW)
    return pl.pallas_call(
        kernel,
        out_shape=shape,
        grid_spec=pltpu.PrefetchScalarGridSpec(
            num_scalar_prefetch=1,
            grid=(1,),
            in_specs=[fixed(a) for a in arrays],
            out_specs=fixed(shape),
            scratch_shapes=[pltpu.VMEM((size, width), F32)],
        ),
        compiler_params=params(),
        cost_estimate=cost(2 * size * count * n * width, 6 * 1024 * 1024),
        name="first_forward",
    )(me, *arrays)


def degree_blocks(refs, counts, lat, step, groups):
    for ref, count in zip(refs, counts):
        size = ref.shape[0]
        if groups == 1 and count == 1:
            yield ref, slice(0, size)
            continue
        part = size // lat // count // groups
        for c in range(count):
            for i in range(lat):
                start = (i * count + c) * (part * groups) + step * part
                yield ref, pl.ds(pl.multiple_of(start, part), part)


def degree_tables(to_ref, back_ref, spots_ref, spots_back_ref, each):
    group = spots_ref.shape[0]
    to = [
        jnp.dot(to_ref[q // each], spots_ref[q], preferred_element_type=F32).astype(LOW)
        for q in range(group)
    ]
    back = [
        jnp.dot(spots_back_ref[q], back_ref[q // each], preferred_element_type=F32).astype(LOW)
        for q in range(group)
    ]
    return jnp.concatenate(to, axis=0), jnp.concatenate(back, axis=1)


def filter_call(kernel, name, first, tables, spots, response, extra, spectra, each, groups, outs):
    part = tables[0].shape[0]
    block = spots[0].shape[0] // each
    tabled = pl.BlockSpec((block, L, NLAT), lambda g, first: (first[0] + g, 0, 0))
    grouped = lambda a: pl.BlockSpec((1, *a.shape[1:]), lambda g, first: (g, 0, 0))
    spec = lambda a: grouped(a) if len(a.shape) == 3 else fixed(a)
    arrays = [*tables, *spots, response, *extra, *spectra]
    return pl.pallas_call(
        kernel,
        out_shape=outs,
        grid_spec=pltpu.PrefetchScalarGridSpec(
            num_scalar_prefetch=1,
            grid=(groups,),
            in_specs=[tabled, tabled, fixed(spots[0]), fixed(spots[1]), fixed(response)]
            + [spec(a) for a in (*extra, *spectra)],
            out_specs=[spec(o) for o in outs],
        ),
        compiler_params=params(),
        cost_estimate=cost(16 * part, 24 * 1024 * 1024),
        name=name,
    )(first, *arrays)


def filter_forward(
    first, tables, spots, response, spectra, counts, out_counts, lat, each, groups
):
    size = spots[0].shape[2]
    width = response.shape[1]
    count = len(spectra)

    def kernel(first_ref, to_ref, back_ref, spots_ref, spots_back_ref, response_ref, *refs):
        step = pl.program_id(0)
        ins, outs, coefs = refs[:count], refs[count:-1], refs[-1]
        to, back = degree_tables(to_ref, back_ref, spots_ref, spots_back_ref, each)
        values = jnp.concatenate(
            [ref[rows, :] for ref, rows in degree_blocks(ins, counts, lat, step, groups)], axis=0
        )
        coef = jnp.dot(to, values, preferred_element_type=F32)
        coefs[0] = coef
        scale = jnp.concatenate([response_ref[...]] * (size // L), axis=0)
        filtered = (scale * coef).astype(LOW)
        result = jnp.dot(back, filtered, preferred_element_type=F32).astype(LOW)
        begin = 0
        for ref, rows in degree_blocks(outs, out_counts, lat, step, groups):
            length = rows.stop if isinstance(rows, slice) else rows.size
            ref[rows, :] = result[begin : begin + length]
            begin += length

    height = sum(s.shape[0] for s in spectra) // sum(counts)
    outs = [jax.ShapeDtypeStruct((height * c, width), LOW) for c in out_counts]
    outs.append(jax.ShapeDtypeStruct((groups, size, width), F32))
    return filter_call(
        kernel, "filter_forward", first, tables, spots, response, (), spectra, each, groups, outs
    )


def filter_backward(
    first, tables, spots, response, coefs, spectra, counts, out_counts, lat, each, groups
):
    size = spots[0].shape[2]
    width = response.shape[1]
    count = len(spectra)

    def kernel(
        first_ref, to_ref, back_ref, spots_ref, spots_back_ref, response_ref, coefs_ref, *refs
    ):
        step = pl.program_id(0)
        ins, outs, grad_ref = refs[:count], refs[count:-1], refs[-1]
        to, back = degree_tables(to_ref, back_ref, spots_ref, spots_back_ref, each)
        values = jnp.concatenate(
            [ref[rows, :] for ref, rows in degree_blocks(ins, counts, lat, step, groups)], axis=0
        )
        upstream = jnp.dot(to, values, preferred_element_type=F32)
        product = coefs_ref[0] * upstream
        grad = product[:L]
        for q in range(1, size // L):
            grad = grad + product[q * L : (q + 1) * L]

        @pl.when(step == 0)
        def _():
            grad_ref[...] = jnp.zeros_like(grad_ref)

        grad_ref[...] += grad
        scale = jnp.concatenate([response_ref[...]] * (size // L), axis=0)
        filtered = (scale * upstream).astype(LOW)
        result = jnp.dot(back, filtered, preferred_element_type=F32).astype(LOW)
        begin = 0
        for ref, rows in degree_blocks(outs, out_counts, lat, step, groups):
            length = rows.stop if isinstance(rows, slice) else rows.size
            ref[rows, :] = result[begin : begin + length]
            begin += length

    height = sum(s.shape[0] for s in spectra) // sum(counts)
    outs = [jax.ShapeDtypeStruct((height * c, width), LOW) for c in out_counts]
    outs.append(jax.ShapeDtypeStruct((L, width), F32))
    return filter_call(
        kernel,
        "filter_backward",
        first,
        tables,
        spots,
        response,
        (coefs,),
        spectra,
        each,
        groups,
        outs,
    )


def prepare_weights(weight_in, weight_out, width, hidden_width):
    channels, units = weight_in.shape

    def kernel(in_ref, out_ref, w_in, w_out, w_in_t, w_out_t):
        w_in[...] = jnp.zeros_like(w_in)
        w_out_t[...] = jnp.zeros_like(w_out_t)
        w_in[:channels, :units] = in_ref[...].astype(LOW)
        w_out_t[:channels, :units] = out_ref[...].astype(LOW)
        w_in_t[...] = w_in[...].T
        w_out[...] = w_out_t[...].T

    outs = [
        jax.ShapeDtypeStruct(shape, LOW)
        for shape in [(width, hidden_width), (hidden_width, width)] * 2
    ]
    outs = [outs[0], outs[1], outs[1], outs[0]]
    return pl.pallas_call(
        kernel, out_shape=outs, compiler_params=params(), name="prepare_weights"
    )(weight_in, weight_out.T)


def feed_forward(
    me, tables, weights, offset, gain, spectra, slots, upstreams, lat, depth, points, channels, split
):
    n = depth * points
    pair, count = len(slots), len(slots[0])
    flat = [slot for chunk in slots for slot in chunk]
    width, hidden_width = weights[0].shape
    size = spectra.shape[0] // pair
    part = size // lat
    inverse_channels = 1.0 / channels

    def kernel(
        me_ref, out_table, back_table, w_in, w_out, w_in_t, w_out_t, offset_ref, gain_ref, y, *refs
    ):
        ins, ups = refs[: pair * count], refs[pair * count : (pair + 1) * count]
        refs = refs[(pair + 1) * count :]
        outs = refs[: split * count]
        refs = refs[split * count :]
        grad_ref, second_ref, active_ref, pre_ref, cot_ref, gain_part, back_ref = refs[:-4]
        x_now, up_now, y_now, total = refs[-4:]
        step = pl.program_id(0)

        @pl.when(step == 0)
        def _():
            gain_part[...] = jnp.zeros_like(gain_part)
            total[...] = jnp.zeros_like(total)
            for c in range(pair):
                for i in range(lat):
                    y_now[c, i * part : (i + 1) * part] = y[
                        (i * pair + c) * part : (i * pair + c + 1) * part
                    ]

        for s in range(count):

            @pl.when(step == s)
            def _():
                for c in range(pair):
                    x_now[c] = ins[c * count + s][...]
                up_now[...] = ups[s][...]

        rows = lambda parts: jnp.concatenate(parts, axis=0) if pair > 1 else parts[0]
        branch = rows(
            [
                jnp.dot(out_table[0], y_now[c], preferred_element_type=F32).astype(LOW)
                for c in range(pair)
            ]
        )
        shifted = rows([load_points(x_now.at[c], n, points) for c in range(pair)])
        hidden = shifted + offset_ref[...] + branch.astype(F32)
        square = jnp.sum(hidden * hidden, axis=1, keepdims=True)
        scale = lax.rsqrt(square * inverse_channels + NORM_EPS)
        second = (hidden * scale * gain_ref[...]).astype(LOW)
        second_ref[...] = second
        upstream = load_points(up_now, pair * n, points)
        upstream_low = upstream.astype(LOW)
        cot_ref[...] = upstream_low
        preact = jnp.dot(second, w_in[...], preferred_element_type=F32)
        back_active = jnp.dot(upstream_low, w_out_t[...], preferred_element_type=F32)
        share = 0.5 + 0.5 * lax.erf(preact * math.sqrt(0.5))
        density = jnp.exp(-0.5 * preact * preact) * (1.0 / math.sqrt(2.0 * math.pi))
        active = (preact * share).astype(LOW)
        active_ref[...] = active
        back_preact = (back_active * (share + preact * density)).astype(LOW)
        pre_ref[...] = back_preact
        output = hidden + jnp.dot(active, w_out[...], preferred_element_type=F32)
        back_second = jnp.dot(back_preact, w_in_t[...], preferred_element_type=F32)
        scaled = back_second * gain_ref[...]
        inner = jnp.sum(hidden * scaled, axis=1, keepdims=True) * inverse_channels
        grad = scale * scaled - hidden * (scale * scale * scale * inner) + upstream
        grad_ref[...] = grad
        grad_low = grad.astype(LOW)
        for c in range(pair):
            total[c] += jnp.dot(
                back_table[0], grad_low[c * n : (c + 1) * n], preferred_element_type=F32
            )
        gain_part[...] += jnp.sum(
            (back_second * (hidden * scale)).reshape(pair * n // 8, 8, width), axis=0
        )

        @pl.when(step == count - 1)
        def _():
            for c in range(pair):
                for i in range(lat):
                    back_ref[(i * pair + c) * part : (i * pair + c + 1) * part] = total[
                        c, i * part : (i + 1) * part
                    ].astype(LOW)

        m = pair * n // split
        leaving = [x_now.at[c] for c in range(pair)] if split > 1 else [up_now]
        for c in range(split):
            block = output[c * m : (c + 1) * m]
            store_points(leaving[c], block.astype(LOW), block[:, channels - 1 : channels], points)
        for s in range(count):

            @pl.when(step == s)
            def _():
                for c in range(split):
                    outs[c * count + s][...] = leaving[c][...]

    rows = lambda w: pl.BlockSpec((pair * n, w), lambda s, me_ref: (s, 0))
    slot = jax.ShapeDtypeStruct((flat if split > 1 else upstreams)[0].shape, LOW)
    height = count * pair * n
    outs = [slot] * (split * count) + [
        jax.ShapeDtypeStruct((height, width), F32),
        jax.ShapeDtypeStruct((height, width), LOW),
        jax.ShapeDtypeStruct((height, hidden_width), LOW),
        jax.ShapeDtypeStruct((height, hidden_width), LOW),
        jax.ShapeDtypeStruct((height, width), LOW),
        jax.ShapeDtypeStruct((8, width), F32),
        jax.ShapeDtypeStruct(spectra.shape, LOW),
    ]
    out_specs = [fixed(slot)] * (split * count) + [
        rows(width),
        rows(width),
        rows(hidden_width),
        rows(hidden_width),
        rows(width),
        fixed(outs[-2]),
        fixed(outs[-1]),
    ]
    arrays = [*tables, *weights, offset, gain, spectra, *flat, *upstreams]
    return pl.pallas_call(
        kernel,
        out_shape=outs,
        grid_spec=pltpu.PrefetchScalarGridSpec(
            num_scalar_prefetch=1,
            grid=(count,),
            in_specs=[slot_table(t, count) for t in tables] + [once(a) for a in arrays[2:]],
            out_specs=out_specs,
            scratch_shapes=[
                pltpu.VMEM((pair, *flat[0].shape), LOW),
                pltpu.VMEM(upstreams[0].shape, LOW),
                pltpu.VMEM((pair, size, width), LOW),
                pltpu.VMEM((pair, size, width), F32),
            ],
        ),
        compiler_params=params(),
        cost_estimate=cost(0, 0),
        name="feed_forward",
    )(me, *arrays)


def weight_sums(parts, kept, block=512):
    count = len(parts)
    height, width = parts[0][0].shape
    hidden_width = parts[0][1].shape[1]
    block = min(block, height)
    steps = height // block

    def kernel(*refs):
        ins, out = refs[:-1], refs[-1]
        step = pl.program_id(0)

        @pl.when(step == 0)
        def _():
            out[...] = jnp.zeros_like(out)

        def add(row, left, right):
            result = lax.dot_general(
                left[...], right[...], (((0,), (0,)), ((), ())), preferred_element_type=F32
            )
            out[row : row + kept, :] += result[:kept]

        for m in range(count):

            @pl.when((step >= m * steps) & (step < (m + 1) * steps))
            def _():
                second, active, pre, cot = ins[4 * m : 4 * m + 4]
                add(0, second, pre)
                add(kept, cot, active)

    def spec(array, m):
        return pl.BlockSpec(
            (block, array.shape[1]),
            lambda k: (jnp.clip(k - m * steps, 0, steps - 1), 0),
        )

    shape = jax.ShapeDtypeStruct((2 * kept, hidden_width), F32)
    return pl.pallas_call(
        kernel,
        out_shape=shape,
        grid=(count * steps,),
        in_specs=[spec(a, m) for m, part in enumerate(parts) for a in part],
        out_specs=fixed(shape),
        compiler_params=params(),
        cost_estimate=cost(0, 0),
        name="weight_sums",
    )(*[a for part in parts for a in part])


def first_backward(
    me, table, spectra, slots, grads, place, pair, offset, gain, depth, points, channels
):
    n = depth * points
    count = len(slots)
    width = gain.shape[1]
    inverse_channels = 1.0 / channels

    def kernel(me_ref, table_ref, y, grad_ref, offset_ref, gain_ref, *refs):
        ins, outs, now = refs[:count], refs[count:-1], refs[-1]
        step = pl.program_id(0)
        for s in range(count):

            @pl.when(step == s)
            def _():
                now[...] = ins[s][...]

        back = jnp.dot(table_ref[0], y[...], preferred_element_type=F32).astype(LOW).astype(F32)
        shifted = load_points(now, n, points) + offset_ref[...]
        square = jnp.sum(shifted * shifted, axis=1, keepdims=True)
        scale = lax.rsqrt(square * inverse_channels + NORM_EPS)
        scaled = back * gain_ref[...]
        inner = jnp.sum(shifted * scaled, axis=1, keepdims=True) * inverse_channels
        result = grad_ref[...] + scale * scaled - shifted * (scale * scale * scale * inner)
        store_points(now, result.astype(LOW), result[:, channels - 1 : channels], points)
        for s in range(count):

            @pl.when(step == s)
            def _():
                outs[s][...] = now[...]

    slot = jax.ShapeDtypeStruct(slots[0].shape, LOW)
    outs = [slot] * count
    return pl.pallas_call(
        kernel,
        out_shape=outs,
        grid_spec=pltpu.PrefetchScalarGridSpec(
            num_scalar_prefetch=1,
            grid=(count,),
            in_specs=[
                slot_table(table, count),
                fixed(spectra),
                pl.BlockSpec((n, width), lambda s, me_ref: (s * pair + place, 0)),
                fixed(offset),
                fixed(gain),
            ]
            + [fixed(s) for s in slots],
            out_specs=[fixed(o) for o in outs],
            scratch_shapes=[pltpu.VMEM(slot.shape, LOW)],
        ),
        compiler_params=params(),
        cost_estimate=cost(2 * count * n * width * spectra.shape[0], 12 * 1024 * 1024),
        name="first_backward",
    )(me, table, spectra, grads, offset, gain, *slots)


def adafactor_matrix(weight_now, gradient, rows_old, columns_old, decay_rate):
    squares = gradient * gradient + FIRST_EPS
    rows_new = decay_rate * rows_old + (1.0 - decay_rate) * jnp.mean(squares, axis=1)
    columns_new = decay_rate * columns_old + (1.0 - decay_rate) * jnp.mean(squares, axis=0)
    estimate = rows_new[:, None] * columns_new[None, :] / jnp.mean(rows_new)
    update = gradient * lax.rsqrt(estimate)
    update = update / jnp.maximum(1.0, jnp.sqrt(jnp.mean(update * update)) / CLIP_LEVEL)
    scale_now = STEP_RATE * jnp.maximum(SECOND_EPS, jnp.sqrt(jnp.mean(weight_now * weight_now)))
    return (weight_now - scale_now * update, rows_new, columns_new)


def adafactor_call(gradients, place, weight_now, rows_old, columns_old, by_rows, decay_rate):
    height, width = weight_now.shape

    def kernel(grad_ref, weight_ref, rows_ref, columns_ref, grad_out, new, rows_out, columns_out):
        gradient = grad_ref[:height, :width].astype(F32)
        grad_out[...] = gradient
        squares = gradient * gradient + FIRST_EPS
        rows_mean = jnp.sum(squares, axis=1, keepdims=True) * (1.0 / width)
        columns_mean = jnp.sum(squares, axis=0, keepdims=True) * (1.0 / height)
        rows_new = decay_rate * rows_ref[...] + (1.0 - decay_rate) * rows_mean
        columns_new = decay_rate * columns_ref[...] + (1.0 - decay_rate) * columns_mean
        across = lax.broadcasted_iota(jnp.int32, (height, height), 0)
        along = lax.broadcasted_iota(jnp.int32, (height, height), 1)
        turned = jnp.sum(jnp.where(across == along, rows_new, 0.0), axis=0, keepdims=True)
        rows_out[...] = turned[0]
        columns_out[...] = columns_new[0]
        mean = jnp.mean(rows_new) if by_rows else jnp.mean(columns_new)
        update = gradient * (lax.rsqrt(rows_new / mean) * lax.rsqrt(columns_new))
        weight = weight_ref[...]
        size = 1.0 / (height * width)
        clip = jnp.maximum(1.0, jnp.sqrt(jnp.sum(update * update) * size) / CLIP_LEVEL)
        rate = STEP_RATE * jnp.maximum(SECOND_EPS, jnp.sqrt(jnp.sum(weight * weight) * size))
        new[...] = weight - update * (rate / clip)

    whole = lambda a: pl.BlockSpec(a.shape, lambda i: (0,) * len(a.shape))
    tall, wide = gradients.shape
    matrix = jax.ShapeDtypeStruct((height, width), F32)
    outs = [matrix, matrix]
    outs += [jax.ShapeDtypeStruct((height,), F32), jax.ShapeDtypeStruct((width,), F32)]
    arrays = [weight_now, rows_old[:, None], columns_old[None]]
    return pl.pallas_call(
        kernel,
        out_shape=outs,
        grid=(1,),
        in_specs=[pl.BlockSpec((tall // 2, wide), lambda i: (place, 0))]
        + [whole(a) for a in arrays],
        out_specs=[whole(o) for o in outs],
        compiler_params=params(),
        cost_estimate=cost(0, 0),
        name="adafactor",
    )(gradients, *arrays)


def adafactor_vector(weight_now, gradient, moments_old, decay_rate):
    moments_new = decay_rate * moments_old + (1.0 - decay_rate) * (gradient * gradient + FIRST_EPS)
    update = gradient * lax.rsqrt(moments_new)
    update = update / jnp.maximum(
        1.0, jnp.sqrt(jnp.mean(update * update, axis=1, keepdims=True)) / CLIP_LEVEL
    )
    scale_now = STEP_RATE * jnp.maximum(
        SECOND_EPS, jnp.sqrt(jnp.mean(weight_now * weight_now, axis=1, keepdims=True))
    )
    return (weight_now - scale_now * update, moments_new)


def tie(*groups):
    return lax.optimization_barrier(groups)


def take(array, index):
    return lax.dynamic_index_in_dim(array, index, 0, keepdims=False)


def chunk_rows(rows):
    return rows // 4 if rows % 4 == 0 else rows


def group_size(share, depth):
    for size in range(1, share):
        if share % size == 0 and size * depth % 16 == 0:
            return size
    return share


def body(
    fields_in,
    cotangent,
    member_dates,
    date_table,
    norm_gains,
    spectral_filter,
    weight_in,
    weight_out,
    gain_moments,
    in_row_stats,
    in_column_stats,
    out_row_stats,
    out_column_stats,
    filter_row_stats,
    filter_column_stats,
):
    members, rows, points, channels = fields_in.shape
    units = weight_in.shape[1]
    width = -(-channels // LANES) * LANES
    hidden_width = -(-units // LANES) * LANES
    lat, lon = lax.axis_size("lat"), lax.axis_size("lon")
    lat_me, lon_me = lax.axis_index("lat"), lax.axis_index("lon")
    me = lon_me.astype(jnp.int32).reshape(1)
    share = Q // lat
    depth = chunk_rows(rows)
    chunks = rows // depth
    pair = 2 if chunks % 2 == 0 else 1
    mids = chunks // pair
    n = depth * points
    kept = -(-channels // (4 * lat)) * (4 * lat)

    def wider(array, *sizes):
        return jnp.pad(array, [(0, s - d) for s, d in zip(sizes, array.shape)])

    def exchange_lon(name, slots, sign):
        with jax.named_scope(name):
            return [
                slot
                if s == 0
                else lax.ppermute(slot, "lon", [(i, (i + sign * s) % lon) for i in range(lon)])
                for s, slot in enumerate(slots)
            ]

    def exchange_lat(name, *spectra):
        blocks = [a.reshape(lat, -1, width) for a in spectra]
        blocks = jnp.concatenate(blocks, axis=1) if len(blocks) > 1 else blocks[0]
        with jax.named_scope(name):
            blocks = lax.all_to_all(blocks, "lat", split_axis=0, concat_axis=0, tiled=True)
        return blocks.reshape(-1, width)

    inside = lat_me < lat

    order = [norm_gains[:1, :LANES]]

    def unit(function, *arrays):
        run = lambda token, *arrays: tie(token, function(*arrays))
        shapes = jax.eval_shape(run, order[0], *arrays)
        blank = lambda *_: jax.tree.map(lambda a: jnp.zeros(a.shape, a.dtype), shapes)
        order[0], out = lax.cond(inside, run, blank, order[0], *arrays)
        return out

    def spread(values):
        height = -(-values.shape[0] // (8 * lat)) * 8
        return wider(values, height * lat, values.shape[1])

    def gathered(part):
        return exchange_lat("gather", jnp.broadcast_to(part[None], (lat, *part.shape)))

    forward, inverse = dft_tables()

    def by_device(table):
        blocks = table.reshape(lon, points, Q).transpose(0, 2, 1)
        return np.einsum("zqk,ab->zqabk", blocks, np.eye(depth)).reshape(lon, Q * depth, n)

    analysis = jnp.asarray(by_device(forward), LOW)
    back_analysis = jnp.asarray(by_device(inverse.T), LOW)
    synthesis = jnp.asarray(by_device(inverse.T).transpose(0, 2, 1), LOW)
    back_synthesis = jnp.asarray(by_device(forward).transpose(0, 2, 1), LOW)

    legendre, quadrature = legendre_table()
    group = group_size(share, depth)
    groups = share // group
    places = np.arange(NLAT).reshape(lat, chunks, depth).transpose(1, 0, 2)
    spots = np.zeros((group, NLAT, chunks, lat, group, depth))
    for q in range(group):
        for c in range(chunks):
            for i in range(lat):
                spots[q, places[c, i], c, i, q, np.arange(depth)] = 1.0
    spots = spots.reshape(group, NLAT, group * NLAT)
    spots = (jnp.asarray(spots, LOW), jnp.asarray(spots.transpose(0, 2, 1), LOW))
    each = 2 if group % 2 == 0 else 1
    first = (lat_me * groups if each == 2 else 0 * lat_me).astype(jnp.int32).reshape(1)

    def own_degrees(table):
        table = jnp.asarray(table, LOW)
        if each == 2:
            return table
        own_q = (lat_me * share + jnp.arange(share, dtype=jnp.int32)) // 2
        return jnp.take(table, own_q, axis=0)

    plain = own_degrees(legendre)
    weighted = own_degrees(legendre * quadrature)
    plain_back = own_degrees(legendre.transpose(0, 2, 1))
    weighted_back = own_degrees((legendre * quadrature).transpose(0, 2, 1))

    date_selector = (
        member_dates[:, None] == jnp.arange(date_table.shape[0], dtype=jnp.int32)[None, :]
    ).astype(F32)
    offsets = jnp.dot(date_selector, date_table, precision=lax.Precision.HIGHEST)
    offset = wider(take(offsets, lon_me)[None], 1, width)
    gain_one = wider(norm_gains[:1], 1, width)
    gain_two = wider(norm_gains[1:], 1, width)
    response = wider(spectral_filter, L, width)
    fields = [pack(me, fields_in, c, depth, lon) for c in range(chunks)]
    upstreams = [None] * mids
    waiting = [(f"fields_{c}", fields, c) for c in range(chunks)]
    waiting += [(f"upstream_{c}", upstreams, c) for c in range(mids)]

    def send_next(after):
        if not waiting or waiting[0][1][waiting[0][2]] is None:
            return after
        name, packs, c = waiting.pop(0)
        after, slots = tie(after, packs[c])
        packs[c] = exchange_lon(name, slots, 1)
        return after

    fields[0] = exchange_lon("fields_0", fields[0], 1)
    del waiting[0]
    fields[0], fields[1:], offset, gain_one, gain_two, response = tie(
        fields[0], fields[1:], offset, gain_one, gain_two, response
    )

    spectra = []
    for c in range(chunks):

        def to_spectra(cotangent, *slots):
            rows_now = first_forward(me, analysis, slots, offset, gain_one, depth, points, channels)
            rows_now = exchange_lat(f"spectra_{c}", rows_now)
            return rows_now, [pack(me, a, c, depth * pair, lon) for a in cotangent]

        if c > 0:
            fields[c], spectra[c - 1] = tie(fields[c], spectra[c - 1])
        fields[c] = send_next(fields[c])
        rows_now, packed = unit(to_spectra, [cotangent] if c < mids else [], *fields[c])
        upstreams[c : c + 1] = packed if c < mids else upstreams[c : c + 1]
        spectra.append(rows_now)

    def to_coefficients(weight_in, weight_out, *spectra):
        *values, coefs = filter_forward(
            first,
            (weighted, plain_back),
            spots,
            response,
            spectra,
            [1] * chunks,
            [pair] * mids,
            lat,
            each,
            groups,
        )
        values[0] = exchange_lat("synthesis_0", values[0])
        return values, coefs, prepare_weights(weight_in, weight_out, width, hidden_width)

    spectra[-1] = send_next(spectra[-1])
    values, coefs, weights = unit(to_coefficients, weight_in, weight_out, *spectra)

    splits = [1] * (mids - 1) + [pair]
    backs, grads, parts, outputs = [], [], [], []
    gain_parts = []
    for c in range(mids):

        def step(spectrum, slots, upstream, following, before):
            out = feed_forward(
                me,
                (synthesis, back_analysis),
                weights,
                offset,
                gain_two,
                spectrum,
                slots,
                upstream,
                lat,
                depth,
                points,
                channels,
                splits[c],
            )
            following = [exchange_lat(f"synthesis_{c + 1}", a) for a in following]
            before = [exchange_lat(f"back_synthesis_{c - 1}", a) for a in before]
            return out, following, before

        out, values[c + 1 : c + 2], backs[c - 1 : c] = unit(
            step,
            values[c],
            fields[c * pair : (c + 1) * pair],
            upstreams[c],
            values[c + 1 : c + 2],
            backs[c - 1 : c],
        )
        for p in range(splits[c]):
            leaving = out[p * lon : (p + 1) * lon]
            outputs.append(exchange_lon(f"output_{c}_{p}", leaving, -1))
        grad, *part, gain_part, back = out[splits[c] * lon :]
        grads.append(grad)
        parts.append(part)
        gain_parts.append(gain_part)
        backs.append(back)

    def to_weights(late, parts):
        return exchange_lat(f"back_synthesis_{mids - 1}", late), weight_sums(parts, kept)

    def to_gradients(backs, coefs, gain_parts):
        *values, filter_part = filter_backward(
            first,
            (plain, weighted_back),
            spots,
            response,
            coefs,
            backs,
            [pair] * mids,
            [1] * chunks,
            lat,
            each,
            groups,
        )
        gain_part = sum(jnp.sum(a, axis=0) for a in gain_parts)
        return values, spread(jnp.concatenate([filter_part, gain_part[None]], axis=0))

    early = mids - 1
    backs[-1], weight_part = unit(to_weights, backs[-1], parts)
    outputs[:early], order[0], weight_part = tie(outputs[:early], order[0], weight_part)
    values, small = unit(to_gradients, backs, coefs, gain_parts)
    outputs[early:-1], order[0] = tie(outputs[early:-1], order[0])

    gradients = []
    with jax.named_scope("weights_lat"):
        part = lax.psum_scatter(weight_part, "lat", scatter_dimension=0, tiled=True)

    for c in range(chunks):
        if c == min(1, chunks - 1):
            outputs[-1], order[0] = tie(outputs[-1], order[0])
        if c == min(2, chunks - 1):
            part, order[0] = tie(part, order[0])
            with jax.named_scope("weights_lon"):
                part = lax.psum(part.astype(LOW), "lon")
        if c >= 2:
            gradients[c - 2], order[0] = tie(gradients[c - 2], order[0])

        def to_input(spectrum, slots, grad, outputs):
            block_output, row = None, 0
            for arrived in outputs:
                tall = depth * pair if arrived[0].shape[0] > slots[0].shape[0] else depth
                block_output = unpack(
                    me, arrived, block_output, row // tall, tall, fields_in.shape, LOW
                )
                row += tall
            out = first_backward(
                me,
                back_synthesis,
                exchange_lat(f"back_spectra_{c}", spectrum),
                slots,
                grad,
                c % pair,
                pair,
                offset,
                gain_one,
                depth,
                points,
                channels,
            )
            return out, block_output

        out, block_output = unit(
            to_input, values[c], fields[c], grads[c // pair], outputs if c == chunks - 1 else []
        )
        gradients.append(exchange_lon(f"input_grad_{c}", out, -1))

    def to_small(small, gradients):
        input_grad = None
        for c, arrived in enumerate(gradients):
            input_grad = unpack(me, arrived, input_grad, c, depth, fields_in.shape, F32)
        part = exchange_lat("small", small).reshape(lat, -1, width)
        return jnp.sum(part, axis=0), input_grad

    part, gradients[-2:-1], order[0] = tie(part, gradients[-2:-1], order[0])
    small, input_grad = unit(to_small, small, gradients[:-1])
    with jax.named_scope("small"):
        bit = 1
        while bit < lon:
            small = small + lax.ppermute(small, "lon", [(i, i ^ bit) for i in range(lon)])
            bit *= 2
    with jax.named_scope("weights_lat"):
        summed = lax.all_gather(part, "lat", axis=0, tiled=True)
    decay_rate = 1.0 - STEP ** (-0.8)

    def to_updates(small, summed, weight_in, weight_out):
        inner = adafactor_call(
            summed, 0, weight_in, in_row_stats, in_column_stats, True, decay_rate
        )
        outer = adafactor_call(
            summed, 1, weight_out.T, out_column_stats, out_row_stats, False, decay_rate
        )
        return gathered(small), inner, outer

    small, inner, outer = unit(to_updates, small, summed, weight_in, weight_out)
    grad_weight_in, new_weight_in, new_in_rows, new_in_columns = inner
    grad_weight_out, new_weight_out, new_out_columns, new_out_rows = outer
    gradients[-1], small = tie(gradients[-1], small)
    input_grad = unpack(
        me, gradients[-1], input_grad, chunks - 1, depth, fields_in.shape, F32
    )

    grad_filter = small[:L, :channels]
    grad_one = jnp.sum(spectral_filter * grad_filter, axis=0) / norm_gains[0]
    grad_gains = jnp.stack([grad_one, small[L, :channels]])
    grad_weight_out, new_weight_out = grad_weight_out.T, new_weight_out.T
    new_filter, new_filter_rows, new_filter_columns = adafactor_matrix(
        spectral_filter, grad_filter, filter_row_stats, filter_column_stats, decay_rate
    )
    new_gains, new_moments = adafactor_vector(norm_gains, grad_gains, gain_moments, decay_rate)
    return (
        block_output,
        input_grad,
        grad_weight_in,
        grad_weight_out,
        grad_filter,
        grad_gains,
        new_weight_in,
        new_weight_out,
        new_filter,
        new_gains,
        new_in_rows,
        new_in_columns,
        new_out_rows,
        new_out_columns,
        new_filter_rows,
        new_filter_columns,
        new_moments,
    )


def solution(mesh):
    spread = P(None, "lat", "lon", None)
    return jax.shard_map(
        body,
        mesh=mesh,
        in_specs=(spread, spread) + (P(),) * 13,
        out_specs=(spread, spread) + (P(),) * 15,
        check_vma=False,
    )
```

```python
import math

import jax
import jax.numpy as jnp
import numpy as np
from jax import lax
from jax.experimental import pallas as pl
from jax.experimental.pallas import tpu as pltpu
from jax.sharding import PartitionSpec as P

NLAT = 128
NLON = 256
L = 128
M = 96
Q = 2 * M
STEP = 3
LANES = 128

NORM_EPS = 1e-06
FIRST_EPS = 1e-30
SECOND_EPS = 0.001
CLIP_LEVEL = 0.5
STEP_RATE = 0.5
F32 = jnp.float32
LOW = jnp.bfloat16
VMEM_LIMIT = 60 * 1024 * 1024


def legendre_table():
    angles = math.pi * (np.arange(NLAT) + 0.5) / NLAT
    cosine, sine = np.cos(angles), np.sin(angles)
    table = np.zeros((M, L, NLAT))
    for m in range(M):
        factors = np.arange(1, m + 1)
        scale = math.sqrt(0.5 * np.prod((2.0 * factors + 1.0) / (2.0 * factors)))
        table[m, m] = scale * sine**m
        for l in range(m + 1, L):
            a = math.sqrt((4.0 * l * l - 1.0) / (l * l - m * m))
            b = math.sqrt(((l - 1.0) ** 2 - m * m) / (4.0 * (l - 1.0) ** 2 - 1.0))
            earlier = table[m, l - 2] if l >= m + 2 else 0.0
            table[m, l] = a * (cosine * table[m, l - 1] - b * earlier)
    return table, math.pi / NLAT * sine


def dft_tables():
    phases = 2.0 * math.pi * (np.outer(np.arange(NLON), np.arange(M)) % NLON) / NLON
    cosine, sine = np.cos(phases), np.sin(phases)
    doubling = np.where(np.arange(M) == 0, 1.0, 2.0)
    forward = np.stack([cosine, -sine], axis=2).reshape(NLON, Q) / NLON
    inverse = np.stack([doubling * cosine, -doubling * sine], axis=2).reshape(NLON, Q).T
    return forward, inverse


EXTRA = 16


def point_masks(n, points):
    row_of = lax.broadcasted_iota(jnp.int32, (n, EXTRA), 0) // points
    sel = (row_of == lax.broadcasted_iota(jnp.int32, (n, EXTRA), 1)).astype(F32).astype(LOW)
    place = lax.broadcasted_iota(jnp.int32, (n, LANES), 0) % points
    lane = lax.broadcasted_iota(jnp.int32, (n, LANES), 1)
    return sel, place == lane, lane == 0


def load_points(ref, n, points):
    tiles = ref.shape[0] // n
    sel, diagonal, first = point_masks(n, points)
    extra = jnp.dot(sel, ref[tiles * n : tiles * n + EXTRA, :], preferred_element_type=F32)
    column = jnp.sum(jnp.where(diagonal, extra, 0.0), axis=1, keepdims=True)
    pieces = [ref[t * n : (t + 1) * n, :].astype(F32) for t in range(tiles)]
    return jnp.concatenate([*pieces, jnp.where(first, column, 0.0)], axis=1)


def store_points(ref, values, last, points):
    n = values.shape[0]
    tiles = ref.shape[0] // n
    _, diagonal, _ = point_masks(n, points)
    for t in range(tiles):
        ref[t * n : (t + 1) * n, :] = values[:, t * LANES : (t + 1) * LANES]
    spread = jnp.where(diagonal, last, 0.0).astype(LOW)
    row_of = lax.broadcasted_iota(jnp.int32, (EXTRA, n), 1) // points
    pick = (row_of == lax.broadcasted_iota(jnp.int32, (EXTRA, n), 0)).astype(F32).astype(LOW)
    ref[tiles * n : tiles * n + EXTRA, :] = jnp.dot(
        pick, spread, preferred_element_type=F32
    ).astype(LOW)


def params():
    return pltpu.CompilerParams(vmem_limit_bytes=VMEM_LIMIT)


def cost(flops, size, transcendentals=0):
    return pl.CostEstimate(flops=1024, bytes_accessed=400_000_000, transcendentals=0)


def fixed(array):
    zeros = (0,) * len(array.shape)
    return pl.BlockSpec(array.shape, lambda *_: zeros)


def once(array):
    zeros = (0,) * len(array.shape)
    return pl.BlockSpec(array.shape, lambda *_: zeros, pipeline_mode=pl.Buffered(1))


def slot_table(table, count):
    return pl.BlockSpec(
        (1, *table.shape[1:]), lambda s, me_ref: ((me_ref[0] + (count - s)) % count, 0, 0)
    )


def pack(me, source, chunk, depth, count):
    _, _, points, channels = source.shape
    n = depth * points
    tiles = channels // LANES

    def kernel(me_ref, source_ref, *outs):
        step = pl.program_id(0)
        values = source_ref[0].reshape(n, channels)
        last = values[:, tiles * LANES :].astype(F32)
        for s, out in enumerate(outs):

            @pl.when(step == s)
            def _():
                store_points(out, values, last, points)

    shape = jax.ShapeDtypeStruct((tiles * n + EXTRA, LANES), LOW)
    return pl.pallas_call(
        kernel,
        out_shape=[shape] * count,
        grid_spec=pltpu.PrefetchScalarGridSpec(
            num_scalar_prefetch=1,
            grid=(count,),
            in_specs=[
                pl.BlockSpec(
                    (1, depth, points, channels),
                    lambda s, me_ref: ((me_ref[0] + s) % count, chunk, 0, 0),
                )
            ],
            out_specs=[fixed(shape)] * count,
        ),
        compiler_params=params(),
        cost_estimate=cost(0, 4 * count * n * channels),
        name="pack",
    )(me, source)


def unpack(me, slots, target, chunk, depth, shape, dtype):
    members, rows, points, channels = shape
    n = depth * points
    count = len(slots)

    def kernel(me_ref, *refs):
        out = refs[-1]
        step = pl.program_id(0)
        for s in range(count):

            @pl.when(step == s)
            def _():
                values = load_points(refs[s], n, points)[:, :channels]
                out[0] = values.astype(dtype).reshape(depth, points, channels)

    specs = [fixed(s) for s in slots]
    arrays = list(slots)
    aliases = {}
    if target is not None:
        specs.append(pl.BlockSpec(memory_space=pl.ANY))
        arrays.append(target)
        aliases = {count + 1: 0}
    return pl.pallas_call(
        kernel,
        out_shape=jax.ShapeDtypeStruct(shape, dtype),
        grid_spec=pltpu.PrefetchScalarGridSpec(
            num_scalar_prefetch=1,
            grid=(count,),
            in_specs=specs,
            out_specs=pl.BlockSpec(
                (1, depth, points, channels),
                lambda s, me_ref: ((me_ref[0] + s) % count, chunk, 0, 0),
            ),
        ),
        input_output_aliases=aliases,
        compiler_params=params(),
        cost_estimate=cost(0, 6 * count * n * channels),
        name="unpack",
    )(me, *arrays)


def first_forward(me, table, slots, offset, gain, depth, points, channels):
    n = depth * points
    count = len(slots)

    def kernel(me_ref, table_ref, offset_ref, gain_ref, *refs):
        out, total = refs[-2:]
        for s, slot in enumerate(refs[:-2]):
            shifted = load_points(slot, n, points) + offset_ref[...]
            square = jnp.sum(shifted * shifted, axis=1, keepdims=True)
            scale = lax.rsqrt(square * (1.0 / channels) + NORM_EPS)
            normed = (shifted * scale * gain_ref[...]).astype(LOW)
            owner = (me_ref[0] + (count - s)) % count
            part = jnp.dot(table_ref[owner], normed, preferred_element_type=F32)
            if s == 0:
                total[...] = part
            else:
                total[...] += part
        out[...] = total[...].astype(LOW)

    width = gain.shape[1]
    size = table.shape[1]
    arrays = [table, offset, gain, *slots]
    shape = jax.ShapeDtypeStruct((size, width), LOW)
    return pl.pallas_call(
        kernel,
        out_shape=shape,
        grid_spec=pltpu.PrefetchScalarGridSpec(
            num_scalar_prefetch=1,
            grid=(1,),
            in_specs=[fixed(a) for a in arrays],
            out_specs=fixed(shape),
            scratch_shapes=[pltpu.VMEM((size, width), F32)],
        ),
        compiler_params=params(),
        cost_estimate=cost(2 * size * count * n * width, 6 * 1024 * 1024),
        name="first_forward",
    )(me, *arrays)


def degree_blocks(refs, counts, lat, step, groups):
    for ref, count in zip(refs, counts):
        size = ref.shape[0]
        if groups == 1 and count == 1:
            yield ref, slice(0, size)
            continue
        part = size // lat // count // groups
        for c in range(count):
            for i in range(lat):
                start = (i * count + c) * (part * groups) + step * part
                yield ref, pl.ds(pl.multiple_of(start, part), part)


def degree_tables(to_ref, back_ref, spots_ref, spots_back_ref, each):
    group = spots_ref.shape[0]
    to = [
        jnp.dot(to_ref[q // each], spots_ref[q], preferred_element_type=F32).astype(LOW)
        for q in range(group)
    ]
    back = [
        jnp.dot(spots_back_ref[q], back_ref[q // each], preferred_element_type=F32).astype(LOW)
        for q in range(group)
    ]
    return jnp.concatenate(to, axis=0), jnp.concatenate(back, axis=1)


def filter_call(kernel, name, first, tables, spots, response, extra, spectra, each, groups, outs):
    part = tables[0].shape[0]
    block = spots[0].shape[0] // each
    tabled = pl.BlockSpec((block, L, NLAT), lambda g, first: (first[0] + g, 0, 0))
    grouped = lambda a: pl.BlockSpec((1, *a.shape[1:]), lambda g, first: (g, 0, 0))
    spec = lambda a: grouped(a) if len(a.shape) == 3 else fixed(a)
    arrays = [*tables, *spots, response, *extra, *spectra]
    return pl.pallas_call(
        kernel,
        out_shape=outs,
        grid_spec=pltpu.PrefetchScalarGridSpec(
            num_scalar_prefetch=1,
            grid=(groups,),
            in_specs=[tabled, tabled, fixed(spots[0]), fixed(spots[1]), fixed(response)]
            + [spec(a) for a in (*extra, *spectra)],
            out_specs=[spec(o) for o in outs],
        ),
        compiler_params=params(),
        cost_estimate=cost(16 * part, 24 * 1024 * 1024),
        name=name,
    )(first, *arrays)


def filter_forward(
    first, tables, spots, response, spectra, counts, out_counts, lat, each, groups
):
    size = spots[0].shape[2]
    width = response.shape[1]
    count = len(spectra)

    def kernel(first_ref, to_ref, back_ref, spots_ref, spots_back_ref, response_ref, *refs):
        step = pl.program_id(0)
        ins, outs, coefs = refs[:count], refs[count:-1], refs[-1]
        to, back = degree_tables(to_ref, back_ref, spots_ref, spots_back_ref, each)
        values = jnp.concatenate(
            [ref[rows, :] for ref, rows in degree_blocks(ins, counts, lat, step, groups)], axis=0
        )
        coef = jnp.dot(to, values, preferred_element_type=F32)
        coefs[0] = coef
        scale = jnp.concatenate([response_ref[...]] * (size // L), axis=0)
        filtered = (scale * coef).astype(LOW)
        result = jnp.dot(back, filtered, preferred_element_type=F32).astype(LOW)
        begin = 0
        for ref, rows in degree_blocks(outs, out_counts, lat, step, groups):
            length = rows.stop if isinstance(rows, slice) else rows.size
            ref[rows, :] = result[begin : begin + length]
            begin += length

    height = sum(s.shape[0] for s in spectra) // sum(counts)
    outs = [jax.ShapeDtypeStruct((height * c, width), LOW) for c in out_counts]
    outs.append(jax.ShapeDtypeStruct((groups, size, width), F32))
    return filter_call(
        kernel, "filter_forward", first, tables, spots, response, (), spectra, each, groups, outs
    )


def filter_backward(
    first, tables, spots, response, coefs, spectra, counts, out_counts, lat, each, groups
):
    size = spots[0].shape[2]
    width = response.shape[1]
    count = len(spectra)

    def kernel(
        first_ref, to_ref, back_ref, spots_ref, spots_back_ref, response_ref, coefs_ref, *refs
    ):
        step = pl.program_id(0)
        ins, outs, grad_ref = refs[:count], refs[count:-1], refs[-1]
        to, back = degree_tables(to_ref, back_ref, spots_ref, spots_back_ref, each)
        values = jnp.concatenate(
            [ref[rows, :] for ref, rows in degree_blocks(ins, counts, lat, step, groups)], axis=0
        )
        upstream = jnp.dot(to, values, preferred_element_type=F32)
        product = coefs_ref[0] * upstream
        grad = product[:L]
        for q in range(1, size // L):
            grad = grad + product[q * L : (q + 1) * L]

        @pl.when(step == 0)
        def _():
            grad_ref[...] = jnp.zeros_like(grad_ref)

        grad_ref[...] += grad
        scale = jnp.concatenate([response_ref[...]] * (size // L), axis=0)
        filtered = (scale * upstream).astype(LOW)
        result = jnp.dot(back, filtered, preferred_element_type=F32).astype(LOW)
        begin = 0
        for ref, rows in degree_blocks(outs, out_counts, lat, step, groups):
            length = rows.stop if isinstance(rows, slice) else rows.size
            ref[rows, :] = result[begin : begin + length]
            begin += length

    height = sum(s.shape[0] for s in spectra) // sum(counts)
    outs = [jax.ShapeDtypeStruct((height * c, width), LOW) for c in out_counts]
    outs.append(jax.ShapeDtypeStruct((L, width), F32))
    return filter_call(
        kernel,
        "filter_backward",
        first,
        tables,
        spots,
        response,
        (coefs,),
        spectra,
        each,
        groups,
        outs,
    )


def prepare_weights(weight_in, weight_out, width, hidden_width):
    channels, units = weight_in.shape

    def kernel(in_ref, out_ref, w_in, w_out, w_in_t, w_out_t):
        w_in[...] = jnp.zeros_like(w_in)
        w_out_t[...] = jnp.zeros_like(w_out_t)
        w_in[:channels, :units] = in_ref[...].astype(LOW)
        w_out_t[:channels, :units] = out_ref[...].astype(LOW)
        w_in_t[...] = w_in[...].T
        w_out[...] = w_out_t[...].T

    outs = [
        jax.ShapeDtypeStruct(shape, LOW)
        for shape in [(width, hidden_width), (hidden_width, width)] * 2
    ]
    outs = [outs[0], outs[1], outs[1], outs[0]]
    return pl.pallas_call(
        kernel, out_shape=outs, compiler_params=params(), name="prepare_weights"
    )(weight_in, weight_out.T)


def feed_forward(
    me, tables, weights, offset, gain, spectra, slots, upstreams, lat, depth, points, channels, split
):
    n = depth * points
    pair, count = len(slots), len(slots[0])
    flat = [slot for chunk in slots for slot in chunk]
    width, hidden_width = weights[0].shape
    size = spectra.shape[0] // pair
    part = size // lat
    inverse_channels = 1.0 / channels

    def kernel(
        me_ref, out_table, back_table, w_in, w_out, w_in_t, w_out_t, offset_ref, gain_ref, y, *refs
    ):
        ins, ups = refs[: pair * count], refs[pair * count : (pair + 1) * count]
        refs = refs[(pair + 1) * count :]
        outs = refs[: split * count]
        refs = refs[split * count :]
        grad_ref, second_ref, active_ref, pre_ref, cot_ref, gain_part, back_ref = refs[:-4]
        x_now, up_now, y_now, total = refs[-4:]
        step = pl.program_id(0)

        @pl.when(step == 0)
        def _():
            gain_part[...] = jnp.zeros_like(gain_part)
            total[...] = jnp.zeros_like(total)
            for c in range(pair):
                for i in range(lat):
                    y_now[c, i * part : (i + 1) * part] = y[
                        (i * pair + c) * part : (i * pair + c + 1) * part
                    ]

        for s in range(count):

            @pl.when(step == s)
            def _():
                for c in range(pair):
                    x_now[c] = ins[c * count + s][...]
                up_now[...] = ups[s][...]

        rows = lambda parts: jnp.concatenate(parts, axis=0) if pair > 1 else parts[0]
        branch = rows(
            [
                jnp.dot(out_table[0], y_now[c], preferred_element_type=F32).astype(LOW)
                for c in range(pair)
            ]
        )
        shifted = rows([load_points(x_now.at[c], n, points) for c in range(pair)])
        hidden = shifted + offset_ref[...] + branch.astype(F32)
        square = jnp.sum(hidden * hidden, axis=1, keepdims=True)
        scale = lax.rsqrt(square * inverse_channels + NORM_EPS)
        second = (hidden * scale * gain_ref[...]).astype(LOW)
        second_ref[...] = second
        upstream = load_points(up_now, pair * n, points)
        upstream_low = upstream.astype(LOW)
        cot_ref[...] = upstream_low
        preact = jnp.dot(second, w_in[...], preferred_element_type=F32)
        back_active = jnp.dot(upstream_low, w_out_t[...], preferred_element_type=F32)
        share = 0.5 + 0.5 * lax.erf(preact * math.sqrt(0.5))
        density = jnp.exp(-0.5 * preact * preact) * (1.0 / math.sqrt(2.0 * math.pi))
        active = (preact * share).astype(LOW)
        active_ref[...] = active
        back_preact = (back_active * (share + preact * density)).astype(LOW)
        pre_ref[...] = back_preact
        output = hidden + jnp.dot(active, w_out[...], preferred_element_type=F32)
        back_second = jnp.dot(back_preact, w_in_t[...], preferred_element_type=F32)
        scaled = back_second * gain_ref[...]
        inner = jnp.sum(hidden * scaled, axis=1, keepdims=True) * inverse_channels
        grad = scale * scaled - hidden * (scale * scale * scale * inner) + upstream
        grad_ref[...] = grad
        grad_low = grad.astype(LOW)
        for c in range(pair):
            total[c] += jnp.dot(
                back_table[0], grad_low[c * n : (c + 1) * n], preferred_element_type=F32
            )
        gain_part[...] += jnp.sum(
            (back_second * (hidden * scale)).reshape(pair * n // 8, 8, width), axis=0
        )

        @pl.when(step == count - 1)
        def _():
            for c in range(pair):
                for i in range(lat):
                    back_ref[(i * pair + c) * part : (i * pair + c + 1) * part] = total[
                        c, i * part : (i + 1) * part
                    ].astype(LOW)

        m = pair * n // split
        leaving = [x_now.at[c] for c in range(pair)] if split > 1 else [up_now]
        for c in range(split):
            block = output[c * m : (c + 1) * m]
            store_points(leaving[c], block.astype(LOW), block[:, channels - 1 : channels], points)
        for s in range(count):

            @pl.when(step == s)
            def _():
                for c in range(split):
                    outs[c * count + s][...] = leaving[c][...]

    rows = lambda w: pl.BlockSpec((pair * n, w), lambda s, me_ref: (s, 0))
    slot = jax.ShapeDtypeStruct((flat if split > 1 else upstreams)[0].shape, LOW)
    height = count * pair * n
    outs = [slot] * (split * count) + [
        jax.ShapeDtypeStruct((height, width), F32),
        jax.ShapeDtypeStruct((height, width), LOW),
        jax.ShapeDtypeStruct((height, hidden_width), LOW),
        jax.ShapeDtypeStruct((height, hidden_width), LOW),
        jax.ShapeDtypeStruct((height, width), LOW),
        jax.ShapeDtypeStruct((8, width), F32),
        jax.ShapeDtypeStruct(spectra.shape, LOW),
    ]
    out_specs = [fixed(slot)] * (split * count) + [
        rows(width),
        rows(width),
        rows(hidden_width),
        rows(hidden_width),
        rows(width),
        fixed(outs[-2]),
        fixed(outs[-1]),
    ]
    arrays = [*tables, *weights, offset, gain, spectra, *flat, *upstreams]
    return pl.pallas_call(
        kernel,
        out_shape=outs,
        grid_spec=pltpu.PrefetchScalarGridSpec(
            num_scalar_prefetch=1,
            grid=(count,),
            in_specs=[slot_table(t, count) for t in tables] + [once(a) for a in arrays[2:]],
            out_specs=out_specs,
            scratch_shapes=[
                pltpu.VMEM((pair, *flat[0].shape), LOW),
                pltpu.VMEM(upstreams[0].shape, LOW),
                pltpu.VMEM((pair, size, width), LOW),
                pltpu.VMEM((pair, size, width), F32),
            ],
        ),
        compiler_params=params(),
        cost_estimate=cost(0, 0),
        name="feed_forward",
    )(me, *arrays)


def weight_sums(parts, kept, block=512):
    count = len(parts)
    height, width = parts[0][0].shape
    hidden_width = parts[0][1].shape[1]
    block = min(block, height)
    steps = height // block

    def kernel(*refs):
        ins, out = refs[:-1], refs[-1]
        step = pl.program_id(0)

        @pl.when(step == 0)
        def _():
            out[...] = jnp.zeros_like(out)

        def add(row, left, right):
            result = lax.dot_general(
                left[...], right[...], (((0,), (0,)), ((), ())), preferred_element_type=F32
            )
            out[row : row + kept, :] += result[:kept]

        for m in range(count):

            @pl.when((step >= m * steps) & (step < (m + 1) * steps))
            def _():
                second, active, pre, cot = ins[4 * m : 4 * m + 4]
                add(0, second, pre)
                add(kept, cot, active)

    def spec(array, m):
        return pl.BlockSpec(
            (block, array.shape[1]),
            lambda k: (jnp.clip(k - m * steps, 0, steps - 1), 0),
        )

    shape = jax.ShapeDtypeStruct((2 * kept, hidden_width), F32)
    return pl.pallas_call(
        kernel,
        out_shape=shape,
        grid=(count * steps,),
        in_specs=[spec(a, m) for m, part in enumerate(parts) for a in part],
        out_specs=fixed(shape),
        compiler_params=params(),
        cost_estimate=cost(0, 0),
        name="weight_sums",
    )(*[a for part in parts for a in part])


def first_backward(
    me, table, spectra, slots, grads, place, pair, offset, gain, depth, points, channels
):
    n = depth * points
    count = len(slots)
    width = gain.shape[1]
    inverse_channels = 1.0 / channels

    def kernel(me_ref, table_ref, y, grad_ref, offset_ref, gain_ref, *refs):
        ins, outs, now = refs[:count], refs[count:-1], refs[-1]
        step = pl.program_id(0)
        for s in range(count):

            @pl.when(step == s)
            def _():
                now[...] = ins[s][...]

        back = jnp.dot(table_ref[0], y[...], preferred_element_type=F32).astype(LOW).astype(F32)
        shifted = load_points(now, n, points) + offset_ref[...]
        square = jnp.sum(shifted * shifted, axis=1, keepdims=True)
        scale = lax.rsqrt(square * inverse_channels + NORM_EPS)
        scaled = back * gain_ref[...]
        inner = jnp.sum(shifted * scaled, axis=1, keepdims=True) * inverse_channels
        result = grad_ref[...] + scale * scaled - shifted * (scale * scale * scale * inner)
        store_points(now, result.astype(LOW), result[:, channels - 1 : channels], points)
        for s in range(count):

            @pl.when(step == s)
            def _():
                outs[s][...] = now[...]

    slot = jax.ShapeDtypeStruct(slots[0].shape, LOW)
    outs = [slot] * count
    return pl.pallas_call(
        kernel,
        out_shape=outs,
        grid_spec=pltpu.PrefetchScalarGridSpec(
            num_scalar_prefetch=1,
            grid=(count,),
            in_specs=[
                slot_table(table, count),
                fixed(spectra),
                pl.BlockSpec((n, width), lambda s, me_ref: (s * pair + place, 0)),
                fixed(offset),
                fixed(gain),
            ]
            + [fixed(s) for s in slots],
            out_specs=[fixed(o) for o in outs],
            scratch_shapes=[pltpu.VMEM(slot.shape, LOW)],
        ),
        compiler_params=params(),
        cost_estimate=cost(2 * count * n * width * spectra.shape[0], 12 * 1024 * 1024),
        name="first_backward",
    )(me, table, spectra, grads, offset, gain, *slots)


def adafactor_matrix(weight_now, gradient, rows_old, columns_old, decay_rate):
    squares = gradient * gradient + FIRST_EPS
    rows_new = decay_rate * rows_old + (1.0 - decay_rate) * jnp.mean(squares, axis=1)
    columns_new = decay_rate * columns_old + (1.0 - decay_rate) * jnp.mean(squares, axis=0)
    estimate = rows_new[:, None] * columns_new[None, :] / jnp.mean(rows_new)
    update = gradient * lax.rsqrt(estimate)
    update = update / jnp.maximum(1.0, jnp.sqrt(jnp.mean(update * update)) / CLIP_LEVEL)
    scale_now = STEP_RATE * jnp.maximum(SECOND_EPS, jnp.sqrt(jnp.mean(weight_now * weight_now)))
    return (weight_now - scale_now * update, rows_new, columns_new)


def adafactor_call(gradients, place, weight_now, rows_old, columns_old, by_rows, decay_rate):
    height, width = weight_now.shape

    def kernel(grad_ref, weight_ref, rows_ref, columns_ref, grad_out, new, rows_out, columns_out):
        gradient = grad_ref[:height, :width].astype(F32)
        grad_out[...] = gradient
        squares = gradient * gradient + FIRST_EPS
        rows_mean = jnp.sum(squares, axis=1, keepdims=True) * (1.0 / width)
        columns_mean = jnp.sum(squares, axis=0, keepdims=True) * (1.0 / height)
        rows_new = decay_rate * rows_ref[...] + (1.0 - decay_rate) * rows_mean
        columns_new = decay_rate * columns_ref[...] + (1.0 - decay_rate) * columns_mean
        across = lax.broadcasted_iota(jnp.int32, (height, height), 0)
        along = lax.broadcasted_iota(jnp.int32, (height, height), 1)
        turned = jnp.sum(jnp.where(across == along, rows_new, 0.0), axis=0, keepdims=True)
        rows_out[...] = turned[0]
        columns_out[...] = columns_new[0]
        mean = jnp.mean(rows_new) if by_rows else jnp.mean(columns_new)
        update = gradient * (lax.rsqrt(rows_new / mean) * lax.rsqrt(columns_new))
        weight = weight_ref[...]
        size = 1.0 / (height * width)
        clip = jnp.maximum(1.0, jnp.sqrt(jnp.sum(update * update) * size) / CLIP_LEVEL)
        rate = STEP_RATE * jnp.maximum(SECOND_EPS, jnp.sqrt(jnp.sum(weight * weight) * size))
        new[...] = weight - update * (rate / clip)

    whole = lambda a: pl.BlockSpec(a.shape, lambda i: (0,) * len(a.shape))
    tall, wide = gradients.shape
    matrix = jax.ShapeDtypeStruct((height, width), F32)
    outs = [matrix, matrix]
    outs += [jax.ShapeDtypeStruct((height,), F32), jax.ShapeDtypeStruct((width,), F32)]
    arrays = [weight_now, rows_old[:, None], columns_old[None]]
    return pl.pallas_call(
        kernel,
        out_shape=outs,
        grid=(1,),
        in_specs=[pl.BlockSpec((tall // 2, wide), lambda i: (place, 0))]
        + [whole(a) for a in arrays],
        out_specs=[whole(o) for o in outs],
        compiler_params=params(),
        cost_estimate=cost(0, 0),
        name="adafactor",
    )(gradients, *arrays)


def adafactor_vector(weight_now, gradient, moments_old, decay_rate):
    moments_new = decay_rate * moments_old + (1.0 - decay_rate) * (gradient * gradient + FIRST_EPS)
    update = gradient * lax.rsqrt(moments_new)
    update = update / jnp.maximum(
        1.0, jnp.sqrt(jnp.mean(update * update, axis=1, keepdims=True)) / CLIP_LEVEL
    )
    scale_now = STEP_RATE * jnp.maximum(
        SECOND_EPS, jnp.sqrt(jnp.mean(weight_now * weight_now, axis=1, keepdims=True))
    )
    return (weight_now - scale_now * update, moments_new)


def tie(*groups):
    return lax.optimization_barrier(groups)


def take(array, index):
    return lax.dynamic_index_in_dim(array, index, 0, keepdims=False)


def chunk_rows(rows):
    return rows // 4 if rows % 4 == 0 else rows


def group_size(share, depth):
    for size in range(1, share):
        if share % size == 0 and size * depth % 16 == 0:
            return size
    return share


def body(
    fields_in,
    cotangent,
    member_dates,
    date_table,
    norm_gains,
    spectral_filter,
    weight_in,
    weight_out,
    gain_moments,
    in_row_stats,
    in_column_stats,
    out_row_stats,
    out_column_stats,
    filter_row_stats,
    filter_column_stats,
):
    members, rows, points, channels = fields_in.shape
    units = weight_in.shape[1]
    width = -(-channels // LANES) * LANES
    hidden_width = -(-units // LANES) * LANES
    lat, lon = lax.axis_size("lat"), lax.axis_size("lon")
    lat_me, lon_me = lax.axis_index("lat"), lax.axis_index("lon")
    me = lon_me.astype(jnp.int32).reshape(1)
    share = Q // lat
    depth = chunk_rows(rows)
    chunks = rows // depth
    pair = 2 if chunks % 2 == 0 else 1
    mids = chunks // pair
    n = depth * points
    kept = -(-channels // (4 * lat)) * (4 * lat)

    def wider(array, *sizes):
        return jnp.pad(array, [(0, s - d) for s, d in zip(sizes, array.shape)])

    def exchange_lon(name, slots, sign):
        with jax.named_scope(name):
            return [
                slot
                if s == 0
                else lax.ppermute(slot, "lon", [(i, (i + sign * s) % lon) for i in range(lon)])
                for s, slot in enumerate(slots)
            ]

    def exchange_lat(name, *spectra):
        blocks = [a.reshape(lat, -1, width) for a in spectra]
        blocks = jnp.concatenate(blocks, axis=1) if len(blocks) > 1 else blocks[0]
        with jax.named_scope(name):
            blocks = lax.all_to_all(blocks, "lat", split_axis=0, concat_axis=0, tiled=True)
        return blocks.reshape(-1, width)

    inside = lat_me < lat

    order = [norm_gains[:1, :LANES]]

    def unit(function, *arrays):
        run = lambda token, *arrays: tie(token, function(*arrays))
        shapes = jax.eval_shape(run, order[0], *arrays)
        blank = lambda *_: jax.tree.map(lambda a: jnp.zeros(a.shape, a.dtype), shapes)
        order[0], out = lax.cond(inside, run, blank, order[0], *arrays)
        return out

    def spread(values):
        height = -(-values.shape[0] // (8 * lat)) * 8
        return wider(values, height * lat, values.shape[1])

    def gathered(part):
        return exchange_lat("gather", jnp.broadcast_to(part[None], (lat, *part.shape)))

    forward, inverse = dft_tables()

    def by_device(table):
        blocks = table.reshape(lon, points, Q).transpose(0, 2, 1)
        return np.einsum("zqk,ab->zqabk", blocks, np.eye(depth)).reshape(lon, Q * depth, n)

    analysis = jnp.asarray(by_device(forward), LOW)
    back_analysis = jnp.asarray(by_device(inverse.T), LOW)
    synthesis = jnp.asarray(by_device(inverse.T).transpose(0, 2, 1), LOW)
    back_synthesis = jnp.asarray(by_device(forward).transpose(0, 2, 1), LOW)

    legendre, quadrature = legendre_table()
    group = group_size(share, depth)
    groups = share // group
    places = np.arange(NLAT).reshape(lat, chunks, depth).transpose(1, 0, 2)
    spots = np.zeros((group, NLAT, chunks, lat, group, depth))
    for q in range(group):
        for c in range(chunks):
            for i in range(lat):
                spots[q, places[c, i], c, i, q, np.arange(depth)] = 1.0
    spots = spots.reshape(group, NLAT, group * NLAT)
    spots = (jnp.asarray(spots, LOW), jnp.asarray(spots.transpose(0, 2, 1), LOW))
    each = 2 if group % 2 == 0 else 1
    first = (lat_me * groups if each == 2 else 0 * lat_me).astype(jnp.int32).reshape(1)

    def own_degrees(table):
        table = jnp.asarray(table, LOW)
        if each == 2:
            return table
        own_q = (lat_me * share + jnp.arange(share, dtype=jnp.int32)) // 2
        return jnp.take(table, own_q, axis=0)

    plain = own_degrees(legendre)
    weighted = own_degrees(legendre * quadrature)
    plain_back = own_degrees(legendre.transpose(0, 2, 1))
    weighted_back = own_degrees((legendre * quadrature).transpose(0, 2, 1))

    date_selector = (
        member_dates[:, None] == jnp.arange(date_table.shape[0], dtype=jnp.int32)[None, :]
    ).astype(F32)
    offsets = jnp.dot(date_selector, date_table, precision=lax.Precision.HIGHEST)
    offset = wider(take(offsets, lon_me)[None], 1, width)
    gain_one = wider(norm_gains[:1], 1, width)
    gain_two = wider(norm_gains[1:], 1, width)
    response = wider(spectral_filter, L, width)
    fields = [pack(me, fields_in, c, depth, lon) for c in range(chunks)]
    upstreams = [None] * mids
    waiting = [(f"fields_{c}", fields, c) for c in range(chunks)]
    waiting += [(f"upstream_{c}", upstreams, c) for c in range(mids)]

    def send_next(after):
        if not waiting or waiting[0][1][waiting[0][2]] is None:
            return after
        name, packs, c = waiting.pop(0)
        after, slots = tie(after, packs[c])
        packs[c] = exchange_lon(name, slots, 1)
        return after

    fields[0] = exchange_lon("fields_0", fields[0], 1)
    del waiting[0]
    fields[0], fields[1:], offset, gain_one, gain_two, response = tie(
        fields[0], fields[1:], offset, gain_one, gain_two, response
    )

    spectra = []
    for c in range(chunks):

        def to_spectra(cotangent, *slots):
            rows_now = first_forward(me, analysis, slots, offset, gain_one, depth, points, channels)
            rows_now = exchange_lat(f"spectra_{c}", rows_now)
            return rows_now, [pack(me, a, c, depth * pair, lon) for a in cotangent]

        if c > 0:
            fields[c], spectra[c - 1] = tie(fields[c], spectra[c - 1])
        fields[c] = send_next(fields[c])
        rows_now, packed = unit(to_spectra, [cotangent] if c < mids else [], *fields[c])
        upstreams[c : c + 1] = packed if c < mids else upstreams[c : c + 1]
        spectra.append(rows_now)

    def to_coefficients(weight_in, weight_out, *spectra):
        *values, coefs = filter_forward(
            first,
            (weighted, plain_back),
            spots,
            response,
            spectra,
            [1] * chunks,
            [pair] * mids,
            lat,
            each,
            groups,
        )
        values[0] = exchange_lat("synthesis_0", values[0])
        return values, coefs, prepare_weights(weight_in, weight_out, width, hidden_width)

    spectra[-1] = send_next(spectra[-1])
    values, coefs, weights = unit(to_coefficients, weight_in, weight_out, *spectra)

    splits = [1] * (mids - 1) + [pair]
    backs, grads, parts, outputs = [], [], [], []
    gain_parts = []
    for c in range(mids):

        def step(spectrum, slots, upstream, following, before):
            out = feed_forward(
                me,
                (synthesis, back_analysis),
                weights,
                offset,
                gain_two,
                spectrum,
                slots,
                upstream,
                lat,
                depth,
                points,
                channels,
                splits[c],
            )
            following = [exchange_lat(f"synthesis_{c + 1}", a) for a in following]
            before = [exchange_lat(f"back_synthesis_{c - 1}", a) for a in before]
            return out, following, before

        out, values[c + 1 : c + 2], backs[c - 1 : c] = unit(
            step,
            values[c],
            fields[c * pair : (c + 1) * pair],
            upstreams[c],
            values[c + 1 : c + 2],
            backs[c - 1 : c],
        )
        for p in range(splits[c]):
            leaving = out[p * lon : (p + 1) * lon]
            outputs.append(exchange_lon(f"output_{c}_{p}", leaving, -1))
        grad, *part, gain_part, back = out[splits[c] * lon :]
        grads.append(grad)
        parts.append(part)
        gain_parts.append(gain_part)
        backs.append(back)

    def to_weights(late, parts):
        return exchange_lat(f"back_synthesis_{mids - 1}", late), weight_sums(parts, kept)

    def to_gradients(backs, coefs, gain_parts):
        *values, filter_part = filter_backward(
            first,
            (plain, weighted_back),
            spots,
            response,
            coefs,
            backs,
            [pair] * mids,
            [1] * chunks,
            lat,
            each,
            groups,
        )
        gain_part = sum(jnp.sum(a, axis=0) for a in gain_parts)
        return values, spread(jnp.concatenate([filter_part, gain_part[None]], axis=0))

    early = mids - 1
    backs[-1], weight_part = unit(to_weights, backs[-1], parts)
    outputs[:early], order[0], weight_part = tie(outputs[:early], order[0], weight_part)
    values, small = unit(to_gradients, backs, coefs, gain_parts)
    outputs[early:-1], order[0] = tie(outputs[early:-1], order[0])

    gradients = []
    with jax.named_scope("weights_lat"):
        part = lax.psum_scatter(weight_part, "lat", scatter_dimension=0, tiled=True)

    for c in range(chunks):
        if c == min(1, chunks - 1):
            outputs[-1], order[0] = tie(outputs[-1], order[0])
        if c == min(2, chunks - 1):
            part, order[0] = tie(part, order[0])
            with jax.named_scope("weights_lon"):
                part = lax.psum(part.astype(LOW), "lon")
        if c >= 2:
            gradients[c - 2], order[0] = tie(gradients[c - 2], order[0])

        def to_input(spectrum, slots, grad, outputs):
            block_output, row = None, 0
            for arrived in outputs:
                tall = depth * pair if arrived[0].shape[0] > slots[0].shape[0] else depth
                block_output = unpack(
                    me, arrived, block_output, row // tall, tall, fields_in.shape, LOW
                )
                row += tall
            out = first_backward(
                me,
                back_synthesis,
                exchange_lat(f"back_spectra_{c}", spectrum),
                slots,
                grad,
                c % pair,
                pair,
                offset,
                gain_one,
                depth,
                points,
                channels,
            )
            return out, block_output

        out, block_output = unit(
            to_input, values[c], fields[c], grads[c // pair], outputs if c == chunks - 1 else []
        )
        gradients.append(exchange_lon(f"input_grad_{c}", out, -1))

    def to_small(small, gradients):
        input_grad = None
        for c, arrived in enumerate(gradients):
            input_grad = unpack(me, arrived, input_grad, c, depth, fields_in.shape, F32)
        part = exchange_lat("small", small).reshape(lat, -1, width)
        return jnp.sum(part, axis=0), input_grad

    part, gradients[-2:-1], order[0] = tie(part, gradients[-2:-1], order[0])
    small, input_grad = unit(to_small, small, gradients[:-1])
    with jax.named_scope("small"):
        bit = 1
        while bit < lon:
            small = small + lax.ppermute(small, "lon", [(i, i ^ bit) for i in range(lon)])
            bit *= 2
    with jax.named_scope("weights_lat"):
        summed = lax.all_gather(part, "lat", axis=0, tiled=True)
    decay_rate = 1.0 - STEP ** (-0.8)

    def to_updates(small, summed, weight_in, weight_out):
        inner = adafactor_call(
            summed, 0, weight_in, in_row_stats, in_column_stats, True, decay_rate
        )
        outer = adafactor_call(
            summed, 1, weight_out.T, out_column_stats, out_row_stats, False, decay_rate
        )
        return gathered(small), inner, outer

    gradients[-1], small = tie(gradients[-1], small)
    input_grad = unpack(
        me, gradients[-1], input_grad, chunks - 1, depth, fields_in.shape, F32
    )
    input_grad, order[0] = tie(input_grad, order[0])
    small, inner, outer = unit(to_updates, small, summed, weight_in, weight_out)
    grad_weight_in, new_weight_in, new_in_rows, new_in_columns = inner
    grad_weight_out, new_weight_out, new_out_columns, new_out_rows = outer

    grad_filter = small[:L, :channels]
    grad_one = jnp.sum(spectral_filter * grad_filter, axis=0) / norm_gains[0]
    grad_gains = jnp.stack([grad_one, small[L, :channels]])
    grad_weight_out, new_weight_out = grad_weight_out.T, new_weight_out.T
    new_filter, new_filter_rows, new_filter_columns = adafactor_matrix(
        spectral_filter, grad_filter, filter_row_stats, filter_column_stats, decay_rate
    )
    new_gains, new_moments = adafactor_vector(norm_gains, grad_gains, gain_moments, decay_rate)
    return (
        block_output,
        input_grad,
        grad_weight_in,
        grad_weight_out,
        grad_filter,
        grad_gains,
        new_weight_in,
        new_weight_out,
        new_filter,
        new_gains,
        new_in_rows,
        new_in_columns,
        new_out_rows,
        new_out_columns,
        new_filter_rows,
        new_filter_columns,
        new_moments,
    )


def solution(mesh):
    spread = P(None, "lat", "lon", None)
    return jax.shard_map(
        body,
        mesh=mesh,
        in_specs=(spread, spread) + (P(),) * 13,
        out_specs=(spread, spread) + (P(),) * 15,
        check_vma=False,
    )
```
